512 devices in a mesh: dp: 32 (over z_lo, y), ctx: 16 (over z_hi, x, core).
Axes of the slice: x: 4, y: 4, z: 16 (z_hi: 2, z_lo: 8; z = z_hi * 8 + z_lo), core: 2. Of those that a mesh axis runs over, the one named last changes fastest.
Arguments:
- queries_q: bfloat16 [32, 2048, 1792], P('dp', 'ctx'), may hold values from -5 to 5
- keys: bfloat16 [32, 2048, 256], P('dp', 'ctx'), may hold values from -5 to 5
- values: bfloat16 [32, 2048, 256], P('dp', 'ctx'), may hold values from -6 to 6
- lengths: int32 [32, 4], P('dp'), may hold values from 1 to 1536, 2048 in all within a row
- query_emb: bfloat16 [4096, 1792], P('dp'), may hold values from -6 to 6
- positive: int32 [4096], P('dp'), may hold values from 0 to 127
Outputs:
- query_grad: float32 [4096, 1792], P('dp')
- grad_queries: bfloat16 [32, 2048, 1792], P('dp', 'ctx')
- grad_keys: bfloat16 [32, 2048, 256], P('dp', 'ctx')
- grad_values: bfloat16 [32, 2048, 256], P('dp', 'ctx')
The draws below stay inside these ranges and needn't reach their ends.
Inputs may be any that keep to these rules, and one draw needn't show every extreme that they name: The 4 lengths of each row sum to 2048, and the longest is 1536.
All inputs are finite; a program needn't handle non-finite values.
Results may differ from the reference program's by a relative error of at most 0.012.
The reference program's roundings to bfloat16 on the way count: a program that leaves them out, or rounds other values in their place, can miss the bound.
Values may be sent and summed in bfloat16 or wider, within the bound.
No kernel may reach another device: no remote copies, remote signals or barrier semaphores. Data moves between devices by JAX's collectives and lax.ppermute only.
A program may use at most 64 MiB of HBM per device.

```python
import math
import jax
import jax.numpy as jnp
import numpy as np
from jax import lax

HEAD_DIM = 128
HEADS = 14
KV_HEADS = 2
DOCS = 4
ROWS = 32
SEQ = 2048
EMB = 1792
KVW = 256
NQ = 4096
NDOC = 128
N_CTX = 16


def draw_queries_q(key, part):
    key = jax.random.fold_in(key, 5)
    per_group = HEADS // KV_HEADS
    draw_shape = (ROWS, SEQ, KV_HEADS, per_group, HEAD_DIM)
    seed_sample = jnp.clip(jax.random.normal(key, draw_shape, jnp.float32), -4.0, 4.0)
    return seed_sample.reshape(ROWS, SEQ, HEADS * HEAD_DIM).astype(jnp.bfloat16)


def draw_keys(key, part):
    key = jax.random.fold_in(key, 9)
    draw_shape = (ROWS, SEQ, KV_HEADS, HEAD_DIM)
    seed_sample = jnp.clip(jax.random.normal(key, draw_shape, jnp.float32), -4.0, 4.0)
    return seed_sample.reshape(ROWS, SEQ, KV_HEADS * HEAD_DIM).astype(jnp.bfloat16)


def place_ends(drawn, rng, low, largest):
    extent = drawn.shape
    place = [jax.random.randint(jax.random.fold_in(rng, axis), (), 0, extent[axis]) for axis in range(len(extent))]
    drawn = drawn.at[tuple(place)].set(low)
    longest = extent.index(max(extent))
    place[longest] = (place[longest] + 1) % extent[longest]
    return drawn.at[tuple(place)].set(largest)


def block_levels(own_key, extent, cuts, low, largest):
    def one(axis_at, blocks):
        draws = jax.random.uniform(jax.random.fold_in(jax.random.fold_in(own_key, 6), axis_at), (blocks,), jnp.float32, low / len(cuts), largest / len(cuts))
        return jnp.repeat(jnp.exp(draws), extent[axis_at] // blocks).reshape((-1,) + (1,) * (len(extent) - axis_at - 1))

    level = one(*cuts[0])
    for cut in cuts[1:]:
        level = level * one(*cut)
    return level


def length_profile(amount, total, bound, skew):
    weights = [(1 << 20) // math.isqrt(rank ** skew) + 1 for rank in range(2, amount + 1)]
    spare, given = total - bound - (amount - 1), [1] * (amount - 1)
    while spare > 0:
        candidates = [i for i in range(amount - 1) if given[i] < bound]
        whole, budget = sum([weights[i] for i in candidates]), spare
        for i in candidates:
            more = min(bound - given[i], max(1, budget * weights[i] // whole), spare)
            given[i] = given[i] + more
            spare = spare - more
    return np.array([bound] + given)


def ragged(key, amount, total, reach, slope):
    if amount == 2:
        one = jax.random.randint(key, (), max(1, total - reach), min(reach, total - 1) + 1)
        return jnp.stack([one, total - one])
    sizes = jnp.asarray(length_profile(amount, total, reach, slope), jnp.int32)
    pairs = (amount - 1) // 2
    giver, receiver = sizes[1:1 + 2 * pairs:2], sizes[2:2 + 2 * pairs:2]
    slack = jnp.minimum(giver - 1, reach - receiver)
    passed = jax.random.randint(jax.random.fold_in(key, 1), (pairs,), 0, 1 << 20) % (slack + 1)
    sizes = sizes.at[1:1 + 2 * pairs:2].set(giver - passed).at[2:2 + 2 * pairs:2].set(receiver + passed)
    return sizes[jax.random.permutation(jax.random.fold_in(key, 2), amount)]


def noise(own_key, dims, scale, limit, cuts=(), kind=jnp.bfloat16):
    entries = scale * jax.random.normal(own_key, dims, jnp.float32)
    if cuts:
        entries = entries * block_levels(own_key, dims, cuts, -0.22, 0.18)
    return jnp.clip(entries, -limit, limit).astype(kind)


def setup_inputs(seed: int = 0) -> dict:
    seeds = jax.random.split(jax.random.key(seed), 7)
    return {
        "queries_q": draw_queries_q(jax.random.fold_in(seeds[6], 71), 0),
        "keys": draw_keys(jax.random.fold_in(seeds[6], 71), 0),
        "values": noise(seeds[2], (ROWS, SEQ, KVW), 1.0, 6.0, ((0, 32), (1, 16))),
        "lengths": jax.vmap(lambda own: ragged(own, DOCS, SEQ, SEQ - SEQ // 4, 2))(jax.random.split(seeds[3], ROWS)).reshape((ROWS, DOCS)).astype(jnp.int32),
        "query_emb": noise(seeds[4], (NQ, EMB), 1.0, 6.0, ((0, 32),)),
        "positive": place_ends(jax.random.randint(seeds[5], (NQ,), 0, NDOC), jax.random.fold_in(seeds[5], 1), 0, NDOC - 1).astype(jnp.int32),
    }


INVERSE_TEMPER = 0.05
EPSILON = 1e-06
FULL_ACCURACY = lax.Precision.HIGHEST

def document_ids(lengths_row, positions):
    doc_ends = jnp.cumsum(lengths_row)
    return lax.optimization_barrier(jnp.sum((positions[:, None] >= doc_ends[None, :]).astype(jnp.int32), axis=1))

def rounded(values_in):
    return lax.optimization_barrier(values_in.astype(jnp.bfloat16)).astype(jnp.float32)

def rescale_back(inverse, unit_vec, upstream):
    inner_sum = lax.optimization_barrier(jnp.sum(unit_vec * upstream, axis=1, keepdims=True))
    return inverse * (upstream - unit_vec * inner_sum)

def reference(queries_q, keys, values, lengths, query_emb, positive):
    seq_len = queries_q.shape[1]
    tok_rows = seq_len // N_CTX
    per_group = HEADS // KV_HEADS
    factor = HEAD_DIM ** (-0.5)
    positions = jnp.arange(seq_len, dtype=jnp.int32)
    doc_index = jnp.arange(DOCS, dtype=jnp.int32)

    def scores_of(q_rows, k_row, row_start, doc_row):
        q_heads = q_rows.reshape(tok_rows, KV_HEADS, per_group, HEAD_DIM).astype(jnp.float32)
        k_heads = k_row.reshape(seq_len, KV_HEADS, HEAD_DIM).astype(jnp.float32)
        raw_scores = jnp.einsum('tgqd,sgd->gqts', q_heads, k_heads) * factor
        query_doc = lax.dynamic_slice_in_dim(doc_row, row_start, tok_rows, 0)
        query_pos = row_start + jnp.arange(tok_rows, dtype=jnp.int32)
        allowed = (query_doc[:, None] == doc_row[None, :]) & (positions[None, :] <= query_pos[:, None])
        return jnp.where(allowed, raw_scores, -jnp.inf)

    def forward_row(row_item):
        q_row, k_row, v_row, len_row = row_item
        doc_row = document_ids(len_row, positions)
        v_heads = v_row.reshape(seq_len, KV_HEADS, HEAD_DIM).astype(jnp.float32)

        def shard_pass(block_idx):
            row_start = block_idx * tok_rows
            q_rows = lax.dynamic_slice_in_dim(q_row, row_start, tok_rows, 0)
            scores = scores_of(q_rows, k_row, row_start, doc_row)
            row_top = lax.optimization_barrier(jnp.max(scores, axis=-1, keepdims=True))
            log_total = row_top + jnp.log(lax.optimization_barrier(jnp.sum(jnp.exp(scores - row_top), axis=-1, keepdims=True)))
            weights = rounded(jnp.exp(scores - log_total))
            out_rows = jnp.einsum('gqts,sgd->tgqd', weights, v_heads).reshape(tok_rows, EMB)
            return (out_rows, log_total)
        out_rows, log_rows = lax.map(shard_pass, jnp.arange(N_CTX, dtype=jnp.int32))
        attended = out_rows.reshape(seq_len, EMB)
        member = (doc_index[:, None] == doc_row[None, :]).astype(jnp.float32)
        doc_sum = jnp.dot(member, attended, precision=FULL_ACCURACY)
        return (attended, log_rows, doc_sum)
    attended, log_rows, doc_sums = lax.map(forward_row, (queries_q, keys, values, lengths))
    doc_len = lengths.reshape(-1).astype(jnp.float32)[:, None]
    doc_emb = doc_sums.reshape(-1, EMB) / doc_len
    doc_inv = lax.rsqrt(lax.optimization_barrier(jnp.sum(doc_emb * doc_emb, axis=1, keepdims=True)) + EPSILON)
    document_normalized = doc_emb * doc_inv
    query_f = query_emb.astype(jnp.float32)
    query_inv = lax.rsqrt(lax.optimization_barrier(jnp.sum(query_f * query_f, axis=1, keepdims=True)) + EPSILON)
    query_normalized = query_f * query_inv
    similarity_logits = jnp.dot(query_normalized, document_normalized.T, precision=FULL_ACCURACY) / INVERSE_TEMPER
    exp_logits = jnp.exp(similarity_logits)
    target = (jnp.arange(document_normalized.shape[0], dtype=jnp.int32)[None, :] == positive[:, None]).astype(jnp.float32)
    scaling_coefficient = exp_logits / lax.optimization_barrier(jnp.sum(exp_logits, axis=1, keepdims=True)) - target
    query_upstream_gradient = jnp.dot(scaling_coefficient, document_normalized, precision=FULL_ACCURACY) / INVERSE_TEMPER
    document_upstream_gradient = jnp.dot(scaling_coefficient.T, query_normalized, precision=FULL_ACCURACY) / INVERSE_TEMPER
    query_grad = rescale_back(query_inv, query_normalized, query_upstream_gradient)
    passage_derivative = (rescale_back(doc_inv, document_normalized, document_upstream_gradient) / doc_len).reshape(-1, DOCS, EMB)

    def backward_row(row_item):
        q_row, k_row, v_row, len_row, attended_row, log_row, grad_row = row_item
        doc_row = document_ids(len_row, positions)
        member = (doc_index[:, None] == doc_row[None, :]).astype(jnp.float32)
        out_grad = jnp.dot(member.T, grad_row, precision=FULL_ACCURACY)
        k_heads = k_row.reshape(seq_len, KV_HEADS, HEAD_DIM).astype(jnp.float32)
        v_heads = v_row.reshape(seq_len, KV_HEADS, HEAD_DIM).astype(jnp.float32)

        def shard_pass(carry, block_idx):
            key_acc, value_acc = carry
            row_start = block_idx * tok_rows
            q_rows = lax.dynamic_slice_in_dim(q_row, row_start, tok_rows, 0)
            q_heads = q_rows.reshape(tok_rows, KV_HEADS, per_group, HEAD_DIM).astype(jnp.float32)
            up_rows = lax.dynamic_slice_in_dim(out_grad, row_start, tok_rows, 0)
            att_rows = lax.dynamic_slice_in_dim(attended_row, row_start, tok_rows, 0)
            out_heads = rounded(up_rows).reshape(tok_rows, KV_HEADS, per_group, HEAD_DIM)
            row_delta = lax.optimization_barrier(jnp.sum((up_rows * att_rows).reshape(tok_rows, KV_HEADS, per_group, HEAD_DIM), axis=-1))
            row_delta = jnp.transpose(row_delta, (1, 2, 0))[..., None]
            scores = scores_of(q_rows, k_row, row_start, doc_row)
            probability = jnp.exp(scores - log_row[block_idx])
            weights = rounded(probability)
            flow_grad = jnp.einsum('tgqd,sgd->gqts', out_heads, v_heads)
            score_grad = rounded(probability * (flow_grad - row_delta))
            grad_rows = (jnp.einsum('gqts,sgd->tgqd', score_grad, k_heads) * factor).astype(jnp.bfloat16)
            key_part = rounded(jnp.einsum('gqts,tgqd->sgd', score_grad, q_heads) * factor)
            value_part = rounded(jnp.einsum('gqts,tgqd->sgd', weights, out_heads))
            return ((key_acc + key_part, value_acc + value_part), grad_rows.reshape(tok_rows, EMB))
        empty_acc = jnp.zeros((seq_len, KV_HEADS, HEAD_DIM), jnp.float32)
        (key_acc, value_acc), grad_rows = lax.scan(shard_pass, (empty_acc, empty_acc), jnp.arange(N_CTX, dtype=jnp.int32))
        return (grad_rows.reshape(seq_len, EMB), key_acc.reshape(seq_len, KVW).astype(jnp.bfloat16), value_acc.reshape(seq_len, KVW).astype(jnp.bfloat16))
    grad_queries, grad_keys, grad_values = lax.map(backward_row, (queries_q, keys, values, lengths, attended, log_rows, passage_derivative))
    return (query_grad, grad_queries, grad_keys, grad_values)
```

```python
import jax
import jax.numpy as jnp
from jax import lax
from jax.experimental import pallas as pl
from jax.experimental.pallas import tpu as pltpu
from jax.sharding import Mesh
from jax.sharding import PartitionSpec as P

HEAD_DIM = 128
HEADS = 14
KV_HEADS = 2
PER_GROUP = HEADS // KV_HEADS
DOCS = 4
TOK = 128
SEQ = 2048
EMB = HEADS * HEAD_DIM
KVW = KV_HEADS * HEAD_DIM
GROUP_W = PER_GROUP * TOK
CHUNK = 2 * TOK
HALF = SEQ // 2
HALF_CHUNKS = HALF // CHUNK
CHUNKS = 2 * HALF_CHUNKS
PIECE = EMB // 2
NDOC = 128

FACTOR = HEAD_DIM ** (-0.5)
INVERSE_TEMPER = 0.05
EPSILON = 1e-06
FULL_ACCURACY = lax.Precision.HIGHEST
MASKED = -1e30
NT = (((1,), (1,)), ((), ()))
TN = (((0,), (0,)), ((), ()))
NN = (((1,), (0,)), ((), ()))
NEAR = ("x", "core")
VMEM_BYTES = 40 * 1024 * 1024


def mm(a, b, dims, precision=None):
    return lax.dot_general(a, b, dims, precision=precision, preferred_element_type=jnp.float32)


class Row:
    def __init__(self, info):
        self.first, self.core, self.high = info[0], info[1], info[2]
        self.ends = [info[3], info[4], info[5]]
        self.qpos = self.first + lax.broadcasted_iota(jnp.int32, (1, TOK), 1)
        start = jnp.zeros((1, TOK), jnp.int32)
        doc = jnp.zeros((1, TOK), jnp.int32)
        first_start = jnp.int32(0)
        for end in self.ends:
            start = jnp.where(self.qpos >= end, end, start)
            doc = doc + (self.qpos >= end).astype(jnp.int32)
            first_start = jnp.where(self.first >= end, end, first_start)
        self.start = start
        rows = lax.broadcasted_iota(jnp.int32, (8, TOK), 0)
        self.member = (rows == doc).astype(jnp.float32)
        self.skip = HALF_CHUNKS * (1 - self.high)
        self.low_chunk = lax.div(first_start, CHUNK) + self.skip
        self.high_chunk = lax.div(self.first + (TOK - 1), CHUNK) + self.skip + 1

    def bias(self, chunk):
        place = lax.broadcasted_iota(jnp.int32, (CHUNK, TOK), 0)
        half = lax.div(place, TOK)
        turned = jnp.where(self.core == 1, 1 - half, half)
        pos = (chunk - self.skip) * CHUNK + turned * TOK + (place - half * TOK)
        allowed = (pos >= self.start) & (pos <= self.qpos)
        one = jnp.where(allowed, 0.0, MASKED).astype(jnp.float32)
        return jnp.concatenate([one] * PER_GROUP, axis=1)


def chunk_of(mine, other, chunk, column):
    at = slice(column * HEAD_DIM, (column + 1) * HEAD_DIM)
    return jnp.concatenate([mine[chunk, :, at], other[chunk, :, at]], axis=0)


def head_rows(ref, group):
    return jnp.concatenate(
        [
            ref[:, (group * PER_GROUP + h) * HEAD_DIM : (group * PER_GROUP + h + 1) * HEAD_DIM]
            for h in range(PER_GROUP)
        ],
        axis=0,
    )


def attend_kernel(info, q, mine, other, att, lse, doc_sum, held):
    row = Row(info)
    for group in range(KV_HEADS):
        q_rows = head_rows(q, group)
        columns = slice(group * GROUP_W, (group + 1) * GROUP_W)

        def score_step(chunk, top):
            scores = mm(chunk_of(mine, other, chunk, group), q_rows, NT) * FACTOR
            scores = scores + row.bias(chunk)
            held[chunk] = scores
            return jnp.maximum(top, jnp.max(scores, axis=0, keepdims=True))

        top = lax.fori_loop(
            row.low_chunk,
            row.high_chunk,
            score_step,
            jnp.full((1, GROUP_W), MASKED, jnp.float32),
        )

        def total_step(chunk, total):
            return total + jnp.sum(jnp.exp(held[chunk] - top), axis=0, keepdims=True)

        total = lax.fori_loop(
            row.low_chunk, row.high_chunk, total_step, jnp.zeros((1, GROUP_W), jnp.float32)
        )
        log_total = top + jnp.log(total)
        lse[:, columns] = jnp.broadcast_to(log_total, (8, GROUP_W))
        att[:, columns] = jnp.zeros((HEAD_DIM, GROUP_W), jnp.float32)

        def out_step(chunk, carry):
            weights = jnp.exp(held[chunk] - log_total).astype(jnp.bfloat16)
            v_rows = chunk_of(mine, other, chunk, KV_HEADS + group)
            att[:, columns] += mm(v_rows, weights, TN)
            return carry

        lax.fori_loop(row.low_chunk, row.high_chunk, out_step, 0)
        for h in range(PER_GROUP):
            at = slice(group * GROUP_W + h * TOK, group * GROUP_W + (h + 1) * TOK)
            doc_sum[:, at] = mm(row.member, att[:, at], NT, FULL_ACCURACY)


def back_kernel(info, q, mine, other, att, lse, doc_grad, dq, d_mine, d_other, dq_acc):
    row = Row(info)
    d_mine[...] = jnp.zeros(d_mine.shape, d_mine.dtype)
    d_other[...] = jnp.zeros(d_other.shape, d_other.dtype)
    member_low = row.member.astype(jnp.bfloat16)
    for group in range(KV_HEADS):
        columns = slice(group * GROUP_W, (group + 1) * GROUP_W)
        q_rows = head_rows(q, group)
        log_total = lse[0:1, columns]
        out_rows, deltas = [], []
        for h in range(PER_GROUP):
            at = slice(group * GROUP_W + h * TOK, group * GROUP_W + (h + 1) * TOK)
            grad = doc_grad[:, at]
            out_rows.append(mm(member_low, grad.astype(jnp.bfloat16), TN).astype(jnp.bfloat16))
            by_doc = mm(grad, att[:, at], NN, FULL_ACCURACY)
            deltas.append(jnp.sum(row.member * by_doc, axis=0, keepdims=True))
        out_low = jnp.concatenate(out_rows, axis=0)
        delta = jnp.concatenate(deltas, axis=1)
        dq_acc[...] = jnp.zeros(dq_acc.shape, jnp.float32)

        def step(chunk, carry):
            k_rows = chunk_of(mine, other, chunk, group)
            v_rows = chunk_of(mine, other, chunk, KV_HEADS + group)
            scores = mm(k_rows, q_rows, NT) * FACTOR + row.bias(chunk)
            probs = jnp.exp(scores - log_total)
            flow = mm(v_rows, out_low, NT)
            score_grad = (probs * (flow - delta)).astype(jnp.bfloat16)
            dq_acc[...] += mm(k_rows, score_grad, TN)
            k_part = (mm(score_grad, q_rows, NN) * FACTOR).astype(jnp.bfloat16)
            v_part = mm(probs.astype(jnp.bfloat16), out_low, NN).astype(jnp.bfloat16)
            k_at = slice(group * HEAD_DIM, (group + 1) * HEAD_DIM)
            v_at = slice(KVW + group * HEAD_DIM, KVW + (group + 1) * HEAD_DIM)
            d_mine[chunk, :, k_at] = k_part[:TOK]
            d_other[chunk, :, k_at] = k_part[TOK:]
            d_mine[chunk, :, v_at] = v_part[:TOK]
            d_other[chunk, :, v_at] = v_part[TOK:]
            return carry

        lax.fori_loop(row.low_chunk, row.high_chunk, step, 0)
        for h in range(PER_GROUP):
            at = slice((group * PER_GROUP + h) * HEAD_DIM, (group * PER_GROUP + h + 1) * HEAD_DIM)
            block = dq_acc[:, h * TOK : (h + 1) * TOK]
            dq[:, at] = (block.T * FACTOR).astype(jnp.bfloat16)


def vmem():
    return pl.BlockSpec(memory_space=pltpu.VMEM)


def attend(info, q, mine, other):
    return pl.pallas_call(
        attend_kernel,
        out_shape=(
            jax.ShapeDtypeStruct((HEAD_DIM, HEADS * TOK), jnp.float32),
            jax.ShapeDtypeStruct((8, HEADS * TOK), jnp.float32),
            jax.ShapeDtypeStruct((8, EMB), jnp.float32),
        ),
        in_specs=[pl.BlockSpec(memory_space=pltpu.SMEM)] + [vmem()] * 3,
        out_specs=(vmem(),) * 3,
        scratch_shapes=[pltpu.VMEM((CHUNKS, CHUNK, GROUP_W), jnp.float32)],
        compiler_params=pltpu.CompilerParams(vmem_limit_bytes=VMEM_BYTES),
        name="attend",
    )(info, q, mine, other)


def attend_back(info, q, mine, other, att, lse, doc_grad):
    return pl.pallas_call(
        back_kernel,
        out_shape=(
            jax.ShapeDtypeStruct((TOK, EMB), jnp.bfloat16),
            jax.ShapeDtypeStruct((CHUNKS, TOK, 2 * KVW), jnp.bfloat16),
            jax.ShapeDtypeStruct((CHUNKS, TOK, 2 * KVW), jnp.bfloat16),
        ),
        in_specs=[pl.BlockSpec(memory_space=pltpu.SMEM)] + [vmem()] * 6,
        out_specs=(vmem(),) * 3,
        scratch_shapes=[pltpu.VMEM((HEAD_DIM, GROUP_W), jnp.float32)],
        compiler_params=pltpu.CompilerParams(vmem_limit_bytes=VMEM_BYTES),
        name="attend_back",
    )(info, q, mine, other, att, lse, doc_grad)


def to_all(block, axes, count):
    return lax.all_to_all(jnp.broadcast_to(block[None], (count,) + block.shape), axes, 0, 0)


def swap_cores(block):
    return lax.ppermute(block, "core", [(0, 1), (1, 0)])


def rescale_back(inverse, unit_vec, upstream):
    inner_sum = jnp.sum(unit_vec * upstream, axis=1, keepdims=True)
    return inverse * (upstream - unit_vec * inner_sum)


def per_device(queries_q, keys, values, lengths, query_emb, positive):
    z_lo, y, z_hi, x, core = (lax.axis_index(a) for a in ("zlo", "y", "zhi", "x", "core"))
    q = queries_q[0]
    len_row = lengths[0]
    ends = jnp.cumsum(len_row)
    first_pos = ((z_hi * 4 + x) * 2 + core) * TOK
    info = jnp.stack([first_pos, core, z_hi, ends[0], ends[1], ends[2], ends[3], z_lo])
    info = info.astype(jnp.int32)

    kv = jnp.concatenate([keys[0], values[0]], axis=1)
    kv_low = lax.ppermute(kv, "zhi", [(0, 1)])
    own_part = to_all(kv, "x", 4)
    low_part = to_all(kv_low, "x", 4)
    mine = jnp.concatenate([low_part, own_part], axis=0)
    other = swap_cores(mine)

    att, lse, doc_sum = attend(info, q, mine, other)

    doc_len = len_row.astype(jnp.float32)[:, None]
    doc_part = (doc_sum[:DOCS] / doc_len).reshape(8, 7, 128)
    doc_part = jnp.sum(lax.all_to_all(doc_part, NEAR, 0, 0), axis=0)
    column = to_all(doc_part, ("zlo", "zhi"), 16).reshape(8, 2, 7, 128)
    column = column[:, 0] + column[:, 1]
    every = to_all(column, ("y", "x", "core"), 32).reshape(4, 4, 2, 8, PIECE)
    every = every.transpose(3, 0, 1, 2, 4).reshape(NDOC, EMB)

    every_inv = lax.rsqrt(jnp.sum(every * every, axis=1, keepdims=True) + EPSILON)
    every_unit = every * every_inv
    query_f = query_emb.astype(jnp.float32)
    query_inv = lax.rsqrt(jnp.sum(query_f * query_f, axis=1, keepdims=True) + EPSILON)
    query_unit = query_f * query_inv
    logits = jnp.dot(query_unit, every_unit.T, precision=FULL_ACCURACY) / INVERSE_TEMPER
    exp_logits = jnp.exp(logits)
    target = jnp.arange(NDOC, dtype=jnp.int32)[None, :] == positive[:, None]
    coefficient = exp_logits / jnp.sum(exp_logits, axis=1, keepdims=True) - target.astype(
        jnp.float32
    )

    near_coefficient = lax.dynamic_index_in_dim(
        coefficient.T.reshape(32, DOCS, 128), x, axis=1, keepdims=False
    )
    near_unit = lax.dynamic_slice_in_dim(query_unit, core * PIECE, PIECE, 1)
    terms = jnp.dot(near_coefficient, near_unit, precision=FULL_ACCURACY) / INVERSE_TEMPER
    terms = lax.all_to_all(terms.reshape(32, 7, 128), ("zlo", "y"), 0, 0)
    upstream = to_all(jnp.sum(terms, axis=0), NEAR, 8).reshape(DOCS, EMB)

    row_at = (z_lo * 4 + y) * DOCS
    doc_unit = lax.dynamic_slice_in_dim(every_unit, row_at, DOCS, 0)
    doc_inv = lax.dynamic_slice_in_dim(every_inv, row_at, DOCS, 0)
    doc_grad = rescale_back(doc_inv, doc_unit, upstream) / doc_len
    doc_grad = jnp.concatenate([doc_grad, jnp.zeros_like(doc_grad)], axis=0)

    dq, d_mine, d_other = attend_back(info, q, mine, other, att, lse, doc_grad)

    got = swap_cores(d_other)
    paired = (d_mine.astype(jnp.float32) + got.astype(jnp.float32)).astype(jnp.bfloat16)
    low_terms = lax.all_to_all(paired[:HALF_CHUNKS], "x", 0, 0)
    low_sum = jnp.sum(low_terms.astype(jnp.float32), axis=0).astype(jnp.bfloat16)
    from_high = lax.ppermute(low_sum, "zhi", [(1, 0)])
    own_terms = lax.all_to_all(paired[HALF_CHUNKS:], "x", 0, 0)
    own_sum = jnp.sum(own_terms.astype(jnp.float32), axis=0)
    total = (own_sum + from_high.astype(jnp.float32)).astype(jnp.bfloat16)

    query_up = jnp.dot(coefficient, every_unit, precision=FULL_ACCURACY) / INVERSE_TEMPER
    query_grad = rescale_back(query_inv, query_unit, query_up)
    return (query_grad, dq[None], total[None, :, :KVW], total[None, :, KVW:])


def solution(mesh):
    fine = Mesh(mesh.devices.reshape(8, 4, 2, 4, 2), ("zlo", "y", "zhi", "x", "core"))
    dp, ctx = ("zlo", "y"), ("zhi", "x", "core")
    tokens = P(dp, ctx, None)
    return jax.shard_map(
        per_device,
        mesh=fine,
        in_specs=(tokens, tokens, tokens, P(dp, None), P(dp, None), P(dp)),
        out_specs=(P(dp, None), tokens, tokens, tokens),
        check_vma=False,
    )
```

```python
import jax
import jax.numpy as jnp
from jax import lax
from jax.experimental import pallas as pl
from jax.experimental.pallas import tpu as pltpu
from jax.sharding import Mesh
from jax.sharding import PartitionSpec as P

HEAD_DIM = 128
HEADS = 14
KV_HEADS = 2
PER_GROUP = HEADS // KV_HEADS
DOCS = 4
TOK = 128
SEQ = 2048
EMB = HEADS * HEAD_DIM
KVW = KV_HEADS * HEAD_DIM
GROUP_W = PER_GROUP * TOK
CHUNK = 2 * TOK
HALF = SEQ // 2
CHUNKS = HALF // CHUNK
PIECE = EMB // 2
NDOC = 128

FACTOR = HEAD_DIM ** (-0.5)
INVERSE_TEMPER = 0.05
EPSILON = 1e-06
FULL_ACCURACY = lax.Precision.HIGHEST
MASKED = -1e30
TINY = 1e-30
NT = (((1,), (1,)), ((), ()))
TN = (((0,), (0,)), ((), ()))
NN = (((1,), (0,)), ((), ()))
NEAR = ("x", "core")
VMEM_BYTES = 40 * 1024 * 1024


def mm(a, b, dims, precision=None):
    return lax.dot_general(a, b, dims, precision=precision, preferred_element_type=jnp.float32)


def place():
    return tuple(lax.axis_index(axis) for axis in ("zlo", "y", "zhi", "x", "core"))


class Row:
    def __init__(self, lengths):
        _, _, self.high, x, self.core = place()
        self.first = ((self.high * 4 + x) * 2 + self.core) * TOK
        self.lengths = [lengths[0, d] for d in range(DOCS)]
        qpos = self.first + lax.broadcasted_iota(jnp.int32, (1, TOK), 1)
        start = jnp.zeros((1, TOK), jnp.int32)
        doc = jnp.zeros((1, TOK), jnp.int32)
        first_start = jnp.int32(0)
        end = jnp.int32(0)
        for d in range(DOCS - 1):
            end = end + self.lengths[d]
            start = jnp.where(qpos >= end, end, start)
            doc = doc + (qpos >= end).astype(jnp.int32)
            first_start = jnp.where(self.first >= end, end, first_start)
        self.qpos, self.start = qpos, start
        self.member = (lax.broadcasted_iota(jnp.int32, (8, TOK), 0) == doc).astype(jnp.float32)
        own_base = self.high * HALF
        self.own = (
            own_base,
            lax.div(jnp.maximum(first_start - own_base, 0), CHUNK),
            lax.div(self.first + (TOK - 1) - own_base, CHUNK) + 1,
        )
        self.low = (jnp.int32(0), lax.div(first_start, CHUNK), CHUNKS * self.high)

    def length_column(self):
        rows = lax.broadcasted_iota(jnp.int32, (8, 1), 0)
        column = jnp.ones((8, 1), jnp.float32)
        for d in range(DOCS):
            column = jnp.where(rows == d, self.lengths[d].astype(jnp.float32), column)
        return column

    def bias(self, base, chunk, split):
        at = lax.broadcasted_iota(jnp.int32, (CHUNK, TOK), 0)
        if split:
            half = lax.div(at, TOK)
            turned = jnp.where(self.core == 1, 1 - half, half)
            at = turned * TOK + (at - half * TOK)
        pos = base + chunk * CHUNK + at
        allowed = (pos >= self.start) & (pos <= self.qpos)
        one = jnp.where(allowed, 0.0, MASKED).astype(jnp.float32)
        return jnp.concatenate([one] * PER_GROUP, axis=1)


def chunk_of(kv, chunk, column):
    at = slice(column * HEAD_DIM, (column + 1) * HEAD_DIM)
    if len(kv) == 1:
        return kv[0][chunk, :, at]
    return jnp.concatenate([half[chunk, :, at] for half in kv], axis=0)


def put_chunk(refs, chunk, column, rows):
    at = slice(column * HEAD_DIM, (column + 1) * HEAD_DIM)
    if len(refs) == 1:
        refs[0][chunk, :, at] = rows
    else:
        refs[0][chunk, :, at] = rows[:TOK]
        refs[1][chunk, :, at] = rows[TOK:]


def head_rows(ref, group):
    return jnp.concatenate(
        [
            ref[:, (group * PER_GROUP + h) * HEAD_DIM : (group * PER_GROUP + h + 1) * HEAD_DIM]
            for h in range(PER_GROUP)
        ],
        axis=0,
    )


def head_columns(group, h):
    at = (group * PER_GROUP + h) * HEAD_DIM
    return slice(at, at + HEAD_DIM)


def part_attention(row, part, group, q, kv, held, out):
    base, low, high = part
    q_rows = head_rows(q, group)

    def score_step(chunk, top):
        scores = mm(chunk_of(kv, chunk, group), q_rows, NT) * FACTOR
        scores = scores + row.bias(base, chunk, len(kv) > 1)
        held[chunk] = scores
        return jnp.maximum(top, jnp.max(scores, axis=0, keepdims=True))

    top = lax.fori_loop(low, high, score_step, jnp.full((1, GROUP_W), MASKED, jnp.float32))

    def total_step(chunk, total):
        exps = jnp.exp(held[chunk] - top)
        held[chunk] = exps
        return total + jnp.sum(exps, axis=0, keepdims=True)

    total = lax.fori_loop(low, high, total_step, jnp.zeros((1, GROUP_W), jnp.float32))
    total = jnp.maximum(total, TINY)
    inverse = 1.0 / total
    out[...] = jnp.zeros((HEAD_DIM, GROUP_W), jnp.float32)

    def out_step(chunk, carry):
        weights = (held[chunk] * inverse).astype(jnp.bfloat16)
        out[...] += mm(chunk_of(kv, chunk, KV_HEADS + group), weights, TN)
        return carry

    lax.fori_loop(low, high, out_step, 0)
    return top + jnp.log(total)


def attend_own_kernel(lengths, q, kv, att, lse, held, out):
    row = Row(lengths)
    for group in range(KV_HEADS):
        columns = slice(group * GROUP_W, (group + 1) * GROUP_W)
        log_total = part_attention(row, row.own, group, q, (kv,), held, out)
        att[:, columns] = out[...]
        lse[:, columns] = jnp.broadcast_to(log_total, (8, GROUP_W))


def attend_low_kernel(
    lengths, q, mine, other, own_att, own_lse, att, lse, pieces, held, out, doc_sum
):
    row = Row(lengths)
    for group in range(KV_HEADS):
        columns = slice(group * GROUP_W, (group + 1) * GROUP_W)
        low_total = part_attention(row, row.low, group, q, (mine, other), held, out)
        own_total = own_lse[0:1, columns]
        top = jnp.maximum(low_total, own_total)
        log_total = top + jnp.log(jnp.exp(low_total - top) + jnp.exp(own_total - top))
        att[:, columns] = own_att[:, columns] * jnp.exp(own_total - log_total) + out[
            ...
        ] * jnp.exp(low_total - log_total)
        lse[:, columns] = jnp.broadcast_to(log_total, (8, GROUP_W))
        for h in range(PER_GROUP):
            at = head_columns(group, h)
            doc_sum[:, at] = mm(row.member, att[:, at], NT, FULL_ACCURACY)
    mean = doc_sum[...] / row.length_column()
    for d in range(DOCS):
        for c in range(2):
            pieces[2 * d + c] = mean[d : d + 1, c * PIECE : (c + 1) * PIECE]


def contrast_kernel(q, positive, docs_mine, docs_other, coefficient, terms, own_docs):
    z_lo, y, _, x, core = place()
    d_mine, d_other = docs_mine[...], docs_other[...]
    doc_inv = lax.rsqrt(
        jnp.sum(d_mine * d_mine, axis=1, keepdims=True)
        + jnp.sum(d_other * d_other, axis=1, keepdims=True)
        + EPSILON
    )
    q_all = q[...].astype(jnp.float32)
    query_inv = lax.rsqrt(jnp.sum(q_all * q_all, axis=1, keepdims=True) + EPSILON)
    q_unit = q_all * query_inv
    q_mine = jnp.where(core == 1, q_unit[:, PIECE:], q_unit[:, :PIECE])
    q_other = jnp.where(core == 1, q_unit[:, :PIECE], q_unit[:, PIECE:])
    logits = mm(d_mine * doc_inv, q_mine, NT, FULL_ACCURACY)
    logits = (logits + mm(d_other * doc_inv, q_other, NT, FULL_ACCURACY)) / INVERSE_TEMPER
    exps = jnp.exp(logits)
    at = lax.broadcasted_iota(jnp.int32, (NDOC, 128), 0)
    doc = ((at % 8) * 4 + at // 32) * DOCS + (at // 8) % 4
    target = (doc == positive[...]).astype(jnp.float32)
    coefficient[...] = exps / jnp.sum(exps, axis=0, keepdims=True) - target
    near = jnp.concatenate(
        [coefficient[pl.ds(pl.multiple_of(b * 32 + x * 8, 8), 8), :] for b in range(4)], axis=0
    )
    near_terms = mm(near, q_mine, NN, FULL_ACCURACY) / INVERSE_TEMPER
    for r in range(32):
        terms[r] = near_terms[r : r + 1]
    own_docs[...] = jnp.zeros((8, EMB), jnp.float32)
    for d in range(DOCS):
        r = y * 32 + d * 8 + z_lo
        a, b = docs_mine[pl.ds(r, 1), :], docs_other[pl.ds(r, 1), :]
        own_docs[d : d + 1, :PIECE] = jnp.where(core == 1, b, a)
        own_docs[d : d + 1, PIECE:] = jnp.where(core == 1, a, b)


def query_kernel(q, docs_mine, docs_other, coefficient, query_grad):
    _, _, _, _, core = place()
    d_mine, d_other = docs_mine[...], docs_other[...]
    doc_inv = lax.rsqrt(
        jnp.sum(d_mine * d_mine, axis=1, keepdims=True)
        + jnp.sum(d_other * d_other, axis=1, keepdims=True)
        + EPSILON
    )
    scaled = coefficient[...] * doc_inv
    u_mine = mm(scaled, d_mine, TN, FULL_ACCURACY) / INVERSE_TEMPER
    u_other = mm(scaled, d_other, TN, FULL_ACCURACY) / INVERSE_TEMPER
    u_left = jnp.where(core == 1, u_other, u_mine)
    u_right = jnp.where(core == 1, u_mine, u_other)
    q_all = q[...].astype(jnp.float32)
    query_inv = lax.rsqrt(jnp.sum(q_all * q_all, axis=1, keepdims=True) + EPSILON)
    q_unit = q_all * query_inv
    q_left, q_right = q_unit[:, :PIECE], q_unit[:, PIECE:]
    inner = jnp.sum(q_left * u_left, axis=1, keepdims=True) + jnp.sum(
        q_right * u_right, axis=1, keepdims=True
    )
    query_grad[:, :PIECE] = query_inv * (u_left - q_left * inner)
    query_grad[:, PIECE:] = query_inv * (u_right - q_right * inner)


def back_part(row, part, group, q, kv, log_total, out_rows, delta, dq, d_kv):
    base, low, high = part
    q_rows = head_rows(q, group)

    def step(chunk, carry):
        k_rows = chunk_of(kv, chunk, group)
        v_rows = chunk_of(kv, chunk, KV_HEADS + group)
        scores = mm(k_rows, q_rows, NT) * FACTOR + row.bias(base, chunk, len(kv) > 1)
        probs = jnp.exp(scores - log_total)
        flow = mm(v_rows, out_rows, NT)
        score_grad = (probs * (flow - delta)).astype(jnp.bfloat16)
        dq[...] += mm(k_rows, score_grad, TN)
        k_part = (mm(score_grad, q_rows, NN) * FACTOR).astype(jnp.bfloat16)
        v_part = mm(probs.astype(jnp.bfloat16), out_rows, NN).astype(jnp.bfloat16)
        put_chunk(d_kv, chunk, group, k_part)
        put_chunk(d_kv, chunk, KV_HEADS + group, v_part)
        return carry

    lax.fori_loop(low, high, step, 0)


def back_low_kernel(
    lengths,
    q,
    mine,
    other,
    att,
    lse,
    own_docs,
    upstream,
    out_low,
    delta,
    dq_low,
    d_mine,
    d_other,
    dq,
):
    row = Row(lengths)
    d_mine[...] = jnp.zeros(d_mine.shape, d_mine.dtype)
    d_other[...] = jnp.zeros(d_other.shape, d_other.dtype)
    w = jnp.concatenate(
        [
            jnp.concatenate([upstream[2 * d + c] for d in range(DOCS)] * 2, axis=0)
            for c in range(2)
        ],
        axis=1,
    )
    docs = own_docs[...]
    doc_inv = lax.rsqrt(jnp.sum(docs * docs, axis=1, keepdims=True) + EPSILON)
    unit = docs * doc_inv
    inner = jnp.sum(unit * w, axis=1, keepdims=True)
    doc_grad = doc_inv * (w - unit * inner) / row.length_column()
    low_grad = doc_grad.astype(jnp.bfloat16)
    member_low = row.member.astype(jnp.bfloat16)
    out_low[...] = mm(member_low, low_grad, TN).astype(jnp.bfloat16)
    for group in range(KV_HEADS):
        columns = slice(group * GROUP_W, (group + 1) * GROUP_W)
        for h in range(PER_GROUP):
            at = head_columns(group, h)
            by_doc = mm(doc_grad[:, at], att[:, at], NN, FULL_ACCURACY)
            one = jnp.sum(row.member * by_doc, axis=0, keepdims=True)
            delta[:, at] = jnp.broadcast_to(one, (8, TOK))
        dq[...] = jnp.zeros(dq.shape, jnp.float32)
        back_part(
            row,
            row.low,
            group,
            q,
            (mine, other),
            lse[0:1, columns],
            head_rows(out_low, group),
            delta[0:1, columns],
            dq,
            (d_mine, d_other),
        )
        dq_low[:, columns] = dq[...]


def back_own_kernel(lengths, q, kv, lse, out_low, delta, dq_low, grad_q, d_kv, dq):
    row = Row(lengths)
    d_kv[...] = jnp.zeros(d_kv.shape, d_kv.dtype)
    for group in range(KV_HEADS):
        columns = slice(group * GROUP_W, (group + 1) * GROUP_W)
        dq[...] = dq_low[:, columns]
        back_part(
            row,
            row.own,
            group,
            q,
            (kv,),
            lse[0:1, columns],
            head_rows(out_low, group),
            delta[0:1, columns],
            dq,
            (d_kv,),
        )
        for h in range(PER_GROUP):
            block = dq[:, h * TOK : (h + 1) * TOK]
            grad_q[:, head_columns(group, h)] = (block.T * FACTOR).astype(jnp.bfloat16)


F32, BF16 = jnp.float32, jnp.bfloat16


def shape(dims, dtype):
    return jax.ShapeDtypeStruct(dims, dtype)


def run(kernel, name, outs, scratch, lengths, *arrays, flops=0):
    vmem = pl.BlockSpec(memory_space=pltpu.VMEM)
    smem = pl.BlockSpec(memory_space=pltpu.SMEM)
    first = () if lengths is None else (lengths,)
    return pl.pallas_call(
        kernel,
        out_shape=outs,
        in_specs=[smem] * len(first) + [vmem] * len(arrays),
        out_specs=tuple(vmem for _ in outs),
        scratch_shapes=scratch,
        compiler_params=pltpu.CompilerParams(vmem_limit_bytes=VMEM_BYTES),
        cost_estimate=pl.CostEstimate(flops=flops, bytes_accessed=0, transcendentals=0),
        name=name,
    )(*first, *arrays)


TERMS = shape((CHUNKS, TOK, 2 * KVW), BF16)
HELD = pltpu.VMEM((CHUNKS, CHUNK, GROUP_W), F32)
WIDE = pltpu.VMEM((HEAD_DIM, GROUP_W), F32)


def attend_own(lengths, *arrays):
    outs = (shape((HEAD_DIM, EMB), F32), shape((8, EMB), F32))
    return run(attend_own_kernel, "attend_own", outs, [HELD, WIDE], lengths, *arrays)


def attend_low(lengths, *arrays):
    outs = (shape((HEAD_DIM, EMB), F32), shape((8, EMB), F32), shape((8, 1, PIECE), F32))
    scratch = [HELD, WIDE, pltpu.VMEM((8, EMB), F32)]
    return run(attend_low_kernel, "attend_low", outs, scratch, lengths, *arrays)


def contrast(*arrays):
    outs = (shape((NDOC, 128), F32), shape((32, 1, PIECE), F32), shape((8, EMB), F32))
    return run(contrast_kernel, "contrast", outs, [], None, *arrays)


def query_back(*arrays):
    return run(query_kernel, "query_back", (shape((128, EMB), F32),), [], None, *arrays)[0]


def back_low(lengths, *arrays):
    outs = (
        shape((TOK, EMB), BF16),
        shape((8, EMB), F32),
        shape((HEAD_DIM, EMB), F32),
        TERMS,
        TERMS,
    )
    return run(back_low_kernel, "back_low", outs, [WIDE], lengths, *arrays)


def back_own(lengths, *arrays):
    outs = (shape((TOK, EMB), BF16), shape((CHUNKS, CHUNK, 2 * KVW), BF16))
    return run(back_own_kernel, "back_own", outs, [WIDE], lengths, *arrays)


def to_all(block, axes, count):
    return lax.all_to_all(jnp.broadcast_to(block[None], (count,) + block.shape), axes, 0, 0)


def swap_cores(block):
    return lax.ppermute(block, "core", [(0, 1), (1, 0)])


def per_device(queries_q, keys, values, lengths, query_emb, positive):
    q = queries_q[0]
    kv = jnp.concatenate([keys[0], values[0]], axis=1)
    kv_low = lax.ppermute(kv, "zhi", [(0, 1)])
    own_kv = to_all(kv, NEAR, 8).reshape(CHUNKS, CHUNK, 2 * KVW)
    own_att, own_lse = attend_own(lengths, q, own_kv)
    kv_low, own_att = lax.optimization_barrier((kv_low, own_att))
    low_mine = to_all(kv_low, "x", 4)
    low_other = swap_cores(low_mine)
    att, lse, pieces = attend_low(lengths, q, low_mine, low_other, own_att, own_lse)

    part = jnp.sum(lax.all_to_all(pieces, NEAR, 0, 0), axis=0)
    column = to_all(part, ("zlo", "zhi"), 16).reshape(8, 2, PIECE)
    column = column[:, 0] + column[:, 1]
    docs_mine = to_all(column, ("y", "x"), 16).reshape(NDOC, PIECE)
    docs_other = swap_cores(docs_mine)

    coefficient, terms, own_docs = contrast(
        query_emb, positive.reshape(1, 128), docs_mine, docs_other
    )
    terms = jnp.sum(lax.all_to_all(terms, ("y", "zlo"), 0, 0), axis=0)
    upstream = to_all(terms, NEAR, 8)

    out_low, delta, dq_low, d_mine, d_other = back_low(
        lengths, q, low_mine, low_other, att, lse, own_docs, upstream
    )
    got = swap_cores(d_other)
    grad_q, own_d = back_own(lengths, q, own_kv, lse, out_low, delta, dq_low)
    own_d, got = lax.optimization_barrier((own_d, got))
    paired = (d_mine.astype(F32) + got.astype(F32)).astype(BF16)
    low_terms = lax.all_to_all(paired, "x", 0, 0)
    low_sum = jnp.sum(low_terms.astype(F32), axis=0).astype(BF16)
    low_sum, own_d = lax.optimization_barrier((low_sum, own_d))
    from_high = lax.ppermute(low_sum, "zhi", [(1, 0)])
    own_terms = lax.all_to_all(own_d.reshape(8, TOK, 2 * KVW), NEAR, 0, 0)
    own_sum = jnp.sum(own_terms.astype(F32), axis=0)
    coefficient, low_sum = lax.optimization_barrier((coefficient, low_sum))
    query_grad = query_back(query_emb, docs_mine, docs_other, coefficient)
    query_grad, from_high = lax.optimization_barrier((query_grad, from_high))
    total = (own_sum + from_high.astype(F32)).astype(BF16)
    return (query_grad, grad_q[None], total[None, :, :KVW], total[None, :, KVW:])


def solution(mesh):
    fine = Mesh(mesh.devices.reshape(8, 4, 2, 4, 2), ("zlo", "y", "zhi", "x", "core"))
    dp, ctx = ("zlo", "y"), ("zhi", "x", "core")
    tokens = P(dp, ctx, None)
    return jax.shard_map(
        per_device,
        mesh=fine,
        in_specs=(tokens, tokens, tokens, P(dp, None), P(dp, None), P(dp)),
        out_specs=(P(dp, None), tokens, tokens, tokens),
        check_vma=False,
    )
```

```python
import jax
import jax.numpy as jnp
from jax import lax
from jax.experimental import pallas as pl
from jax.experimental.pallas import tpu as pltpu
from jax.sharding import Mesh
from jax.sharding import PartitionSpec as P

HEAD_DIM = 128
HEADS = 14
KV_HEADS = 2
PER_GROUP = HEADS // KV_HEADS
DOCS = 4
TOK = 128
SEQ = 2048
EMB = HEADS * HEAD_DIM
KVW = KV_HEADS * HEAD_DIM
GROUP_W = PER_GROUP * TOK
CHUNK = 2 * TOK
HALF = SEQ // 2
CHUNKS = HALF // CHUNK
PIECE = EMB // 2
NDOC = 128

FACTOR = HEAD_DIM ** (-0.5)
INVERSE_TEMPER = 0.05
EPSILON = 1e-06
FULL_ACCURACY = lax.Precision.HIGHEST
MASKED = -1e30
TINY = 1e-30
NT = (((1,), (1,)), ((), ()))
TN = (((0,), (0,)), ((), ()))
NN = (((1,), (0,)), ((), ()))
NEAR = ("x", "core")
VMEM_BYTES = 24 * 1024 * 1024


def mm(a, b, dims, precision=None):
    return lax.dot_general(a, b, dims, precision=precision, preferred_element_type=jnp.float32)


def place():
    return tuple(lax.axis_index(axis) for axis in ("zlo", "y", "zhi", "x", "core"))


class Row:
    def __init__(self, lengths):
        _, _, self.high, x, self.core = place()
        self.first = ((self.high * 4 + x) * 2 + self.core) * TOK
        self.lengths = [lengths[0, d] for d in range(DOCS)]
        qpos = self.first + lax.broadcasted_iota(jnp.int32, (1, TOK), 1)
        start = jnp.zeros((1, TOK), jnp.int32)
        doc = jnp.zeros((1, TOK), jnp.int32)
        first_start = jnp.int32(0)
        end = jnp.int32(0)
        for d in range(DOCS - 1):
            end = end + self.lengths[d]
            start = jnp.where(qpos >= end, end, start)
            doc = doc + (qpos >= end).astype(jnp.int32)
            first_start = jnp.where(self.first >= end, end, first_start)
        self.qpos, self.start = qpos, start
        self.member = (lax.broadcasted_iota(jnp.int32, (8, TOK), 0) == doc).astype(jnp.float32)
        own_base = self.high * HALF
        self.own = (
            own_base,
            lax.div(jnp.maximum(first_start - own_base, 0), CHUNK),
            lax.div(self.first + (TOK - 1) - own_base, CHUNK) + 1,
        )
        self.low = (jnp.int32(0), lax.div(first_start, CHUNK), CHUNKS * self.high)

    def length_column(self):
        rows = lax.broadcasted_iota(jnp.int32, (8, 1), 0)
        column = jnp.ones((8, 1), jnp.float32)
        for d in range(DOCS):
            column = jnp.where(rows == d, self.lengths[d].astype(jnp.float32), column)
        return column

    def bias(self, base, chunk, split):
        at = lax.broadcasted_iota(jnp.int32, (CHUNK, TOK), 0)
        if split:
            half = lax.div(at, TOK)
            turned = jnp.where(self.core == 1, 1 - half, half)
            at = turned * TOK + (at - half * TOK)
        pos = base + chunk * CHUNK + at
        allowed = (pos >= self.start) & (pos <= self.qpos)
        one = jnp.where(allowed, 0.0, MASKED).astype(jnp.float32)
        return jnp.concatenate([one] * PER_GROUP, axis=1)


def chunk_of(kv, chunk, column):
    at = slice(column * HEAD_DIM, (column + 1) * HEAD_DIM)
    if len(kv) == 1:
        return kv[0][chunk, :, at]
    return jnp.concatenate([half[chunk, :, at] for half in kv], axis=0)


def put_chunk(refs, chunk, column, rows):
    at = slice(column * HEAD_DIM, (column + 1) * HEAD_DIM)
    if len(refs) == 1:
        refs[0][chunk, :, at] = rows
    else:
        refs[0][chunk, :, at] = rows[:TOK]
        refs[1][chunk, :, at] = rows[TOK:]


def head_rows(ref, group):
    return jnp.concatenate(
        [
            ref[:, (group * PER_GROUP + h) * HEAD_DIM : (group * PER_GROUP + h + 1) * HEAD_DIM]
            for h in range(PER_GROUP)
        ],
        axis=0,
    )


def head_columns(group, h):
    at = (group * PER_GROUP + h) * HEAD_DIM
    return slice(at, at + HEAD_DIM)


def part_attention(row, part, group, q, kv, held, out):
    base, low, high = part
    q_rows = head_rows(q, group)

    def score_step(chunk, top):
        scores = mm(chunk_of(kv, chunk, group), q_rows, NT) * FACTOR
        scores = scores + row.bias(base, chunk, len(kv) > 1)
        held[chunk] = scores
        return jnp.maximum(top, jnp.max(scores, axis=0, keepdims=True))

    top = lax.fori_loop(low, high, score_step, jnp.full((1, GROUP_W), MASKED, jnp.float32))

    def total_step(chunk, total):
        exps = jnp.exp(held[chunk] - top)
        held[chunk] = exps
        return total + jnp.sum(exps, axis=0, keepdims=True)

    total = lax.fori_loop(low, high, total_step, jnp.zeros((1, GROUP_W), jnp.float32))
    total = jnp.maximum(total, TINY)
    inverse = 1.0 / total
    out[...] = jnp.zeros((HEAD_DIM, GROUP_W), jnp.float32)

    def out_step(chunk, carry):
        weights = (held[chunk] * inverse).astype(jnp.bfloat16)
        out[...] += mm(chunk_of(kv, chunk, KV_HEADS + group), weights, TN)
        return carry

    lax.fori_loop(low, high, out_step, 0)
    return top + jnp.log(total)


def attend_own_kernel(lengths, q, mine, other, att, lse, held, out):
    row = Row(lengths)
    for group in range(KV_HEADS):
        columns = slice(group * GROUP_W, (group + 1) * GROUP_W)
        log_total = part_attention(row, row.own, group, q, (mine, other), held, out)
        att[:, columns] = out[...]
        lse[:, columns] = jnp.broadcast_to(log_total, (8, GROUP_W))


def attend_low_kernel(
    lengths, q, mine, other, own_att, own_lse, att, lse, pieces, held, out, doc_sum
):
    row = Row(lengths)
    for group in range(KV_HEADS):
        columns = slice(group * GROUP_W, (group + 1) * GROUP_W)
        low_total = part_attention(row, row.low, group, q, (mine, other), held, out)
        own_total = own_lse[0:1, columns]
        top = jnp.maximum(low_total, own_total)
        log_total = top + jnp.log(jnp.exp(low_total - top) + jnp.exp(own_total - top))
        att[:, columns] = own_att[:, columns] * jnp.exp(own_total - log_total) + out[
            ...
        ] * jnp.exp(low_total - log_total)
        lse[:, columns] = jnp.broadcast_to(log_total, (8, GROUP_W))
        for h in range(PER_GROUP):
            at = head_columns(group, h)
            doc_sum[:, at] = mm(row.member, att[:, at], NT, FULL_ACCURACY)
    mean = doc_sum[...] / row.length_column()
    for d in range(DOCS):
        for c in range(2):
            pieces[2 * d + c] = mean[d : d + 1, c * PIECE : (c + 1) * PIECE]


def contrast_kernel(q, positive, docs_mine, docs_other, coefficient, terms, own_docs):
    z_lo, y, _, x, core = place()
    d_mine, d_other = docs_mine[...], docs_other[...]
    doc_inv = lax.rsqrt(
        jnp.sum(d_mine * d_mine, axis=1, keepdims=True)
        + jnp.sum(d_other * d_other, axis=1, keepdims=True)
        + EPSILON
    )
    q_all = q[...].astype(jnp.float32)
    query_inv = lax.rsqrt(jnp.sum(q_all * q_all, axis=1, keepdims=True) + EPSILON)
    q_unit = q_all * query_inv
    q_mine = jnp.where(core == 1, q_unit[:, PIECE:], q_unit[:, :PIECE])
    q_other = jnp.where(core == 1, q_unit[:, :PIECE], q_unit[:, PIECE:])
    logits = mm(d_mine * doc_inv, q_mine, NT, FULL_ACCURACY)
    logits = (logits + mm(d_other * doc_inv, q_other, NT, FULL_ACCURACY)) / INVERSE_TEMPER
    exps = jnp.exp(logits)
    at = lax.broadcasted_iota(jnp.int32, (NDOC, 128), 0)
    doc = ((at % 8) * 4 + at // 32) * DOCS + (at // 8) % 4
    target = (doc == positive[...]).astype(jnp.float32)
    coefficient[...] = exps / jnp.sum(exps, axis=0, keepdims=True) - target
    near = jnp.concatenate(
        [coefficient[pl.ds(pl.multiple_of(b * 32 + x * 8, 8), 8), :] for b in range(4)], axis=0
    )
    near_terms = mm(near, q_mine, NN, FULL_ACCURACY) / INVERSE_TEMPER
    for r in range(32):
        terms[r] = near_terms[r : r + 1]
    own_docs[...] = jnp.zeros((8, EMB), jnp.float32)
    for d in range(DOCS):
        r = y * 32 + d * 8 + z_lo
        a, b = docs_mine[pl.ds(r, 1), :], docs_other[pl.ds(r, 1), :]
        own_docs[d : d + 1, :PIECE] = jnp.where(core == 1, b, a)
        own_docs[d : d + 1, PIECE:] = jnp.where(core == 1, a, b)


def query_kernel(q, docs_mine, docs_other, coefficient, query_grad):
    _, _, _, _, core = place()
    d_mine, d_other = docs_mine[...], docs_other[...]
    doc_inv = lax.rsqrt(
        jnp.sum(d_mine * d_mine, axis=1, keepdims=True)
        + jnp.sum(d_other * d_other, axis=1, keepdims=True)
        + EPSILON
    )
    scaled = coefficient[...] * doc_inv
    u_mine = mm(scaled, d_mine, TN, FULL_ACCURACY) / INVERSE_TEMPER
    u_other = mm(scaled, d_other, TN, FULL_ACCURACY) / INVERSE_TEMPER
    u_left = jnp.where(core == 1, u_other, u_mine)
    u_right = jnp.where(core == 1, u_mine, u_other)
    q_all = q[...].astype(jnp.float32)
    query_inv = lax.rsqrt(jnp.sum(q_all * q_all, axis=1, keepdims=True) + EPSILON)
    q_unit = q_all * query_inv
    q_left, q_right = q_unit[:, :PIECE], q_unit[:, PIECE:]
    inner = jnp.sum(q_left * u_left, axis=1, keepdims=True) + jnp.sum(
        q_right * u_right, axis=1, keepdims=True
    )
    query_grad[:, :PIECE] = query_inv * (u_left - q_left * inner)
    query_grad[:, PIECE:] = query_inv * (u_right - q_right * inner)


def back_part(row, part, group, q, kv, log_total, out_rows, delta, dq, d_kv):
    base, low, high = part
    q_rows = head_rows(q, group)

    def step(chunk, carry):
        k_rows = chunk_of(kv, chunk, group)
        v_rows = chunk_of(kv, chunk, KV_HEADS + group)
        scores = mm(k_rows, q_rows, NT) * FACTOR + row.bias(base, chunk, len(kv) > 1)
        probs = jnp.exp(scores - log_total)
        flow = mm(v_rows, out_rows, NT)
        score_grad = (probs * (flow - delta)).astype(jnp.bfloat16)
        dq[...] += mm(k_rows, score_grad, TN)
        k_part = (mm(score_grad, q_rows, NN) * FACTOR).astype(jnp.bfloat16)
        v_part = mm(probs.astype(jnp.bfloat16), out_rows, NN).astype(jnp.bfloat16)
        put_chunk(d_kv, chunk, group, k_part)
        put_chunk(d_kv, chunk, KV_HEADS + group, v_part)
        return carry

    lax.fori_loop(low, high, step, 0)


def back_low_kernel(
    lengths,
    q,
    mine,
    other,
    att,
    lse,
    own_docs,
    upstream,
    out_low,
    delta,
    dq_low,
    d_mine,
    d_other,
    dq,
):
    row = Row(lengths)
    d_mine[...] = jnp.zeros(d_mine.shape, d_mine.dtype)
    d_other[...] = jnp.zeros(d_other.shape, d_other.dtype)
    w = jnp.concatenate(
        [
            jnp.concatenate([upstream[2 * d + c] for d in range(DOCS)] * 2, axis=0)
            for c in range(2)
        ],
        axis=1,
    )
    docs = own_docs[...]
    doc_inv = lax.rsqrt(jnp.sum(docs * docs, axis=1, keepdims=True) + EPSILON)
    unit = docs * doc_inv
    inner = jnp.sum(unit * w, axis=1, keepdims=True)
    doc_grad = doc_inv * (w - unit * inner) / row.length_column()
    low_grad = doc_grad.astype(jnp.bfloat16)
    member_low = row.member.astype(jnp.bfloat16)
    out_low[...] = mm(member_low, low_grad, TN).astype(jnp.bfloat16)
    for group in range(KV_HEADS):
        columns = slice(group * GROUP_W, (group + 1) * GROUP_W)
        for h in range(PER_GROUP):
            at = head_columns(group, h)
            by_doc = mm(doc_grad[:, at], att[:, at], NN, FULL_ACCURACY)
            one = jnp.sum(row.member * by_doc, axis=0, keepdims=True)
            delta[:, at] = jnp.broadcast_to(one, (8, TOK))
        dq[...] = jnp.zeros(dq.shape, jnp.float32)
        back_part(
            row,
            row.low,
            group,
            q,
            (mine, other),
            lse[0:1, columns],
            head_rows(out_low, group),
            delta[0:1, columns],
            dq,
            (d_mine, d_other),
        )
        dq_low[:, columns] = dq[...]


def back_own_kernel(
    lengths, q, mine, other, lse, out_low, delta, dq_low, grad_q, d_mine, d_other, dq
):
    row = Row(lengths)
    d_mine[...] = jnp.zeros(d_mine.shape, d_mine.dtype)
    d_other[...] = jnp.zeros(d_other.shape, d_other.dtype)
    for group in range(KV_HEADS):
        columns = slice(group * GROUP_W, (group + 1) * GROUP_W)
        dq[...] = dq_low[:, columns]
        back_part(
            row,
            row.own,
            group,
            q,
            (mine, other),
            lse[0:1, columns],
            head_rows(out_low, group),
            delta[0:1, columns],
            dq,
            (d_mine, d_other),
        )
        for h in range(PER_GROUP):
            block = dq[:, h * TOK : (h + 1) * TOK]
            grad_q[:, head_columns(group, h)] = (block.T * FACTOR).astype(jnp.bfloat16)


F32, BF16 = jnp.float32, jnp.bfloat16


def shape(dims, dtype):
    return jax.ShapeDtypeStruct(dims, dtype)


def run(kernel, name, outs, scratch, lengths, *arrays, flops=0):
    vmem = pl.BlockSpec(memory_space=pltpu.VMEM)
    smem = pl.BlockSpec(memory_space=pltpu.SMEM)
    first = () if lengths is None else (lengths,)
    return pl.pallas_call(
        kernel,
        out_shape=outs,
        in_specs=[smem] * len(first) + [vmem] * len(arrays),
        out_specs=tuple(vmem for _ in outs),
        scratch_shapes=scratch,
        compiler_params=pltpu.CompilerParams(vmem_limit_bytes=VMEM_BYTES),
        cost_estimate=pl.CostEstimate(flops=flops, bytes_accessed=0, transcendentals=0),
        name=name,
    )(*first, *arrays)


TERMS = shape((CHUNKS, TOK, 2 * KVW), BF16)
HELD = pltpu.VMEM((CHUNKS, CHUNK, GROUP_W), F32)
WIDE = pltpu.VMEM((HEAD_DIM, GROUP_W), F32)


def attend_own(lengths, *arrays):
    outs = (shape((HEAD_DIM, EMB), F32), shape((8, EMB), F32))
    return run(attend_own_kernel, "attend_own", outs, [HELD, WIDE], lengths, *arrays)


def attend_low(lengths, *arrays):
    outs = (shape((HEAD_DIM, EMB), F32), shape((8, EMB), F32), shape((8, 1, PIECE), F32))
    scratch = [HELD, WIDE, pltpu.VMEM((8, EMB), F32)]
    return run(attend_low_kernel, "attend_low", outs, scratch, lengths, *arrays)


def contrast(*arrays):
    outs = (shape((NDOC, 128), F32), shape((32, 1, PIECE), F32), shape((8, EMB), F32))
    return run(contrast_kernel, "contrast", outs, [], None, *arrays)


def query_back(*arrays):
    return run(query_kernel, "query_back", (shape((128, EMB), F32),), [], None, *arrays)[0]


def back_low(lengths, *arrays):
    outs = (
        shape((TOK, EMB), BF16),
        shape((8, EMB), F32),
        shape((HEAD_DIM, EMB), F32),
        TERMS,
        TERMS,
    )
    return run(back_low_kernel, "back_low", outs, [WIDE], lengths, *arrays)


def back_own(lengths, *arrays):
    outs = (shape((TOK, EMB), BF16), TERMS, TERMS)
    return run(back_own_kernel, "back_own", outs, [WIDE], lengths, *arrays)


def to_all(block, axes, count):
    return lax.all_to_all(jnp.broadcast_to(block[None], (count,) + block.shape), axes, 0, 0)


def swap_cores(block):
    return lax.ppermute(block, "core", [(0, 1), (1, 0)])


def added(blocks):
    total = blocks[0].astype(F32)
    for i in range(1, blocks.shape[0]):
        total = total + blocks[i].astype(F32)
    return total


def pair_terms(d_mine, d_other):
    got = swap_cores(d_other)
    return (d_mine.astype(F32) + got.astype(F32)).astype(BF16)


def per_device(queries_q, keys, values, lengths, query_emb, positive):
    q = queries_q[0]
    kv = jnp.concatenate([keys[0], values[0]], axis=1)
    kv_low = lax.ppermute(kv, "zhi", [(0, 1)])
    own_mine = to_all(kv, "x", 4)
    kv_low, own_mine = lax.optimization_barrier((kv_low, own_mine))
    own_other = swap_cores(own_mine)
    own_att, own_lse = attend_own(lengths, q, own_mine, own_other)
    low_mine = to_all(kv_low, "x", 4)
    low_other = swap_cores(low_mine)
    att, lse, pieces = attend_low(lengths, q, low_mine, low_other, own_att, own_lse)

    part = added(lax.all_to_all(pieces, NEAR, 0, 0))
    column = to_all(part, ("zlo", "zhi"), 16)
    column = (column[0::2] + column[1::2]).reshape(8, PIECE)
    docs_mine = to_all(column, ("y", "x"), 16).reshape(NDOC, PIECE)
    docs_other = swap_cores(docs_mine)

    coefficient, terms, own_docs = contrast(
        query_emb, positive.reshape(1, 128), docs_mine, docs_other
    )
    terms = added(lax.all_to_all(terms, ("y", "zlo"), 0, 0))
    upstream = to_all(terms, NEAR, 8)

    out_low, delta, dq_low, d_mine, d_other = back_low(
        lengths, q, low_mine, low_other, att, lse, own_docs, upstream
    )
    grad_q, own_d_mine, own_d_other = back_own(
        lengths, q, own_mine, own_other, lse, out_low, delta, dq_low
    )
    low_terms = lax.all_to_all(pair_terms(d_mine, d_other), "x", 0, 0)
    low_sum = added(low_terms).astype(BF16)
    own_paired = pair_terms(own_d_mine, own_d_other)
    low_sum, own_paired = lax.optimization_barrier((low_sum, own_paired))
    from_high = lax.ppermute(low_sum, "zhi", [(1, 0)])
    own_terms = lax.all_to_all(own_paired, "x", 0, 0)
    own_sum = added(own_terms)
    coefficient, low_sum = lax.optimization_barrier((coefficient, low_sum))
    query_grad = query_back(query_emb, docs_mine, docs_other, coefficient)
    query_grad, from_high = lax.optimization_barrier((query_grad, from_high))
    total = (own_sum + from_high.astype(F32)).astype(BF16)
    return (query_grad, grad_q[None], total[None, :, :KVW], total[None, :, KVW:])


def solution(mesh):
    fine = Mesh(mesh.devices.reshape(8, 4, 2, 4, 2), ("zlo", "y", "zhi", "x", "core"))
    dp, ctx = ("zlo", "y"), ("zhi", "x", "core")
    tokens = P(dp, ctx, None)
    return jax.shard_map(
        per_device,
        mesh=fine,
        in_specs=(tokens, tokens, tokens, P(dp, None), P(dp, None), P(dp)),
        out_specs=(P(dp, None), tokens, tokens, tokens),
        check_vma=False,
    )
```

```python
import jax
import jax.numpy as jnp
from jax import lax
from jax.experimental import pallas as pl
from jax.experimental.pallas import tpu as pltpu
from jax.sharding import Mesh
from jax.sharding import PartitionSpec as P

HEAD_DIM = 128
HEADS = 14
KV_HEADS = 2
PER_GROUP = HEADS // KV_HEADS
DOCS = 4
TOK = 128
SEQ = 2048
EMB = HEADS * HEAD_DIM
KVW = KV_HEADS * HEAD_DIM
GROUP_W = PER_GROUP * TOK
CHUNK = 2 * TOK
HALF = SEQ // 2
CHUNKS = HALF // CHUNK
PIECE = EMB // 2
NDOC = 128

FACTOR = HEAD_DIM ** (-0.5)
INVERSE_TEMPER = 0.05
EPSILON = 1e-06
FULL_ACCURACY = lax.Precision.HIGHEST
MASKED = -1e30
TINY = 1e-30
NT = (((1,), (1,)), ((), ()))
TN = (((0,), (0,)), ((), ()))
NN = (((1,), (0,)), ((), ()))
NEAR = ("x", "core")
VMEM_BYTES = 24 * 1024 * 1024


def mm(a, b, dims, precision=None):
    return lax.dot_general(a, b, dims, precision=precision, preferred_element_type=jnp.float32)


def place():
    return tuple(lax.axis_index(axis) for axis in ("zlo", "y", "zhi", "x", "core"))


class Row:
    def __init__(self, lengths):
        _, _, self.high, x, self.core = place()
        self.first = ((self.high * 4 + x) * 2 + self.core) * TOK
        self.lengths = [lengths[0, d] for d in range(DOCS)]
        qpos = self.first + lax.broadcasted_iota(jnp.int32, (1, TOK), 1)
        start = jnp.zeros((1, TOK), jnp.int32)
        doc = jnp.zeros((1, TOK), jnp.int32)
        first_start = jnp.int32(0)
        end = jnp.int32(0)
        for d in range(DOCS - 1):
            end = end + self.lengths[d]
            start = jnp.where(qpos >= end, end, start)
            doc = doc + (qpos >= end).astype(jnp.int32)
            first_start = jnp.where(self.first >= end, end, first_start)
        self.qpos, self.start = qpos, start
        self.member = (lax.broadcasted_iota(jnp.int32, (8, TOK), 0) == doc).astype(jnp.float32)
        own_base = self.high * HALF
        self.own = (
            own_base,
            lax.div(jnp.maximum(first_start - own_base, 0), CHUNK),
            lax.div(self.first + (TOK - 1) - own_base, CHUNK) + 1,
        )
        self.low = (jnp.int32(0), lax.div(first_start, CHUNK), CHUNKS * self.high)

    def length_column(self):
        rows = lax.broadcasted_iota(jnp.int32, (8, 1), 0)
        column = jnp.ones((8, 1), jnp.float32)
        for d in range(DOCS):
            column = jnp.where(rows == d, self.lengths[d].astype(jnp.float32), column)
        return column

    def bias(self, base, chunk):
        at = lax.broadcasted_iota(jnp.int32, (CHUNK, TOK), 0)
        half = lax.div(at, TOK)
        turned = jnp.where(self.core == 1, 1 - half, half)
        pos = base + chunk * CHUNK + turned * TOK + (at - half * TOK)
        allowed = (pos >= self.start) & (pos <= self.qpos)
        return jnp.where(allowed, 0.0, MASKED).astype(jnp.float32)


def chunk_of(kv, chunk, column):
    at = slice(column * HEAD_DIM, (column + 1) * HEAD_DIM)
    return jnp.concatenate([half[chunk, :, at] for half in kv], axis=0)


def put_chunk(refs, chunk, column, rows):
    at = slice(column * HEAD_DIM, (column + 1) * HEAD_DIM)
    refs[0][chunk, :, at] = rows[:TOK]
    refs[1][chunk, :, at] = rows[TOK:]


def fill_bias(row, part, bias):
    base, low, high = part

    def step(chunk, carry):
        bias[chunk] = row.bias(base, chunk)
        return carry

    lax.fori_loop(low, high, step, 0)


def halves(values):
    top = values.astype(jnp.bfloat16)
    return top, (values - top.astype(jnp.float32)).astype(jnp.bfloat16)


def head_rows(ref, group):
    return jnp.concatenate(
        [
            ref[:, (group * PER_GROUP + h) * HEAD_DIM : (group * PER_GROUP + h + 1) * HEAD_DIM]
            for h in range(PER_GROUP)
        ],
        axis=0,
    )


def head(h):
    return slice(h * HEAD_DIM, (h + 1) * HEAD_DIM)


def part_attention(part, q, kv, bias, stats, weights, out):
    _, low, high = part
    stats[0] = jnp.full((HEADS, TOK), MASKED, jnp.float32)
    stats[1] = jnp.zeros((HEADS, TOK), jnp.float32)
    out[...] = jnp.zeros(out.shape, jnp.float32)

    def step(chunk, carry):
        blocked = bias[chunk]
        for group in range(KV_HEADS):
            k_rows = chunk_of(kv, chunk, group)
            scales = []
            for h in range(group * PER_GROUP, (group + 1) * PER_GROUP):
                scores = mm(k_rows, q[:, head(h)], NT) + blocked
                old = stats[0, h : h + 1]
                top = jnp.maximum(old, jnp.max(scores, axis=0, keepdims=True))
                exps = jnp.exp((scores - top) * FACTOR)
                weights[:, head(h)] = exps.astype(jnp.bfloat16)
                scale = jnp.exp((old - top) * FACTOR)
                stats[0, h : h + 1] = top
                stats[1, h : h + 1] = stats[1, h : h + 1] * scale + jnp.sum(
                    exps, axis=0, keepdims=True
                )
                scales.append(scale)
            columns = slice(group * GROUP_W, (group + 1) * GROUP_W)
            sums = mm(chunk_of(kv, chunk, KV_HEADS + group), weights[:, columns], TN)
            for i in range(PER_GROUP):
                at = head(group * PER_GROUP + i)
                out[:, at] = out[:, at] * scales[i] + sums[:, head(i)]
        return carry

    lax.fori_loop(low, high, step, 0)


def part_result(h, stats):
    total = jnp.maximum(stats[1, h : h + 1], TINY)
    return stats[0, h : h + 1] * FACTOR + jnp.log(total), 1.0 / total


def attend_own_kernel(lengths, q, mine, other, att, lse, bias, stats, weights, out):
    row = Row(lengths)
    fill_bias(row, row.own, bias)
    part_attention(row.own, q, (mine, other), bias, stats, weights, out)
    for h in range(HEADS):
        log_total, inverse = part_result(h, stats)
        att[:, head(h)] = out[:, head(h)] * inverse
        lse[:, head(h)] = jnp.broadcast_to(log_total, (8, TOK))


def attend_low_kernel(
    lengths, q, mine, other, own_att, own_lse, att, lse, pieces, bias, stats, weights, out, doc_sum
):
    row = Row(lengths)
    fill_bias(row, row.low, bias)
    member = jnp.concatenate([row.member, jnp.zeros((TOK - 8, TOK), jnp.float32)], axis=0)
    member = member.astype(jnp.bfloat16)
    part_attention(row.low, q, (mine, other), bias, stats, weights, out)
    for h in range(HEADS):
        at = head(h)
        low_total, inverse = part_result(h, stats)
        own_total = own_lse[0:1, at]
        top = jnp.maximum(low_total, own_total)
        log_total = top + jnp.log(jnp.exp(low_total - top) + jnp.exp(own_total - top))
        own_scale = jnp.exp(own_total - log_total)
        low_scale = jnp.exp(low_total - log_total) * inverse
        lse[:, at] = jnp.broadcast_to(log_total, (8, TOK))
        merged = own_att[:, at] * own_scale + out[:, at] * low_scale
        att[:, at] = merged
        big, small = halves(merged)
        doc_sum[:, at] = (mm(big, member, NT) + mm(small, member, NT)).T[:8]
    mean = doc_sum[...] / row.length_column()
    for d in range(DOCS):
        for c in range(2):
            pieces[2 * d + c] = mean[d : d + 1, c * PIECE : (c + 1) * PIECE]


def contrast_kernel(q, positive, docs_mine, docs_other, coefficient, terms, own_docs):
    z_lo, y, _, x, core = place()
    d_mine, d_other = docs_mine[...], docs_other[...]
    doc_inv = lax.rsqrt(
        jnp.sum(d_mine * d_mine, axis=1, keepdims=True)
        + jnp.sum(d_other * d_other, axis=1, keepdims=True)
        + EPSILON
    )
    q_all = q[...].astype(jnp.float32)
    query_inv = lax.rsqrt(jnp.sum(q_all * q_all, axis=1, keepdims=True) + EPSILON)
    q_unit = q_all * query_inv
    q_mine = jnp.where(core == 1, q_unit[:, PIECE:], q_unit[:, :PIECE])
    q_other = jnp.where(core == 1, q_unit[:, :PIECE], q_unit[:, PIECE:])
    logits = mm(d_mine * doc_inv, q_mine, NT, FULL_ACCURACY)
    logits = (logits + mm(d_other * doc_inv, q_other, NT, FULL_ACCURACY)) / INVERSE_TEMPER
    exps = jnp.exp(logits)
    at = lax.broadcasted_iota(jnp.int32, (NDOC, 128), 0)
    doc = ((at % 8) * 4 + at // 32) * DOCS + (at // 8) % 4
    target = (doc == positive[...]).astype(jnp.float32)
    coefficient[...] = exps / jnp.sum(exps, axis=0, keepdims=True) - target
    near = jnp.concatenate(
        [coefficient[pl.ds(pl.multiple_of(b * 32 + x * 8, 8), 8), :] for b in range(4)], axis=0
    )
    near_terms = mm(near, q_mine, NN, FULL_ACCURACY) / INVERSE_TEMPER
    for r in range(32):
        terms[r] = near_terms[r : r + 1]
    own_docs[...] = jnp.zeros((8, EMB), jnp.float32)
    for d in range(DOCS):
        r = y * 32 + d * 8 + z_lo
        a, b = docs_mine[pl.ds(r, 1), :], docs_other[pl.ds(r, 1), :]
        own_docs[d : d + 1, :PIECE] = jnp.where(core == 1, b, a)
        own_docs[d : d + 1, PIECE:] = jnp.where(core == 1, a, b)


def query_kernel(q, docs_mine, docs_other, coefficient, query_grad):
    _, _, _, _, core = place()
    d_mine, d_other = docs_mine[...], docs_other[...]
    doc_inv = lax.rsqrt(
        jnp.sum(d_mine * d_mine, axis=1, keepdims=True)
        + jnp.sum(d_other * d_other, axis=1, keepdims=True)
        + EPSILON
    )
    scaled = coefficient[...] * doc_inv
    u_mine = mm(scaled, d_mine, TN, FULL_ACCURACY) / INVERSE_TEMPER
    u_other = mm(scaled, d_other, TN, FULL_ACCURACY) / INVERSE_TEMPER
    u_left = jnp.where(core == 1, u_other, u_mine)
    u_right = jnp.where(core == 1, u_mine, u_other)
    q_all = q[...].astype(jnp.float32)
    query_inv = lax.rsqrt(jnp.sum(q_all * q_all, axis=1, keepdims=True) + EPSILON)
    q_unit = q_all * query_inv
    q_left, q_right = q_unit[:, :PIECE], q_unit[:, PIECE:]
    inner = jnp.sum(q_left * u_left, axis=1, keepdims=True) + jnp.sum(
        q_right * u_right, axis=1, keepdims=True
    )
    query_grad[:, :PIECE] = query_inv * (u_left - q_left * inner)
    query_grad[:, PIECE:] = query_inv * (u_right - q_right * inner)


def back_part(part, q, kv, bias, lse, out_low, delta, dq, d_kv, grads, weights):
    _, low, high = part

    def step(chunk, carry):
        blocked = bias[chunk]
        for group in range(KV_HEADS):
            k_rows = chunk_of(kv, chunk, group)
            v_rows = chunk_of(kv, chunk, KV_HEADS + group)
            for h in range(group * PER_GROUP, (group + 1) * PER_GROUP):
                at = head(h)
                scores = mm(k_rows, q[:, at], NT) * FACTOR + blocked
                probs = jnp.exp(scores - lse[0:1, at])
                flow = mm(v_rows, out_low[:, at], NT)
                grads[:, at] = (probs * (flow - delta[0:1, at])).astype(jnp.bfloat16)
                weights[:, at] = probs.astype(jnp.bfloat16)
            columns = slice(group * GROUP_W, (group + 1) * GROUP_W)
            score_grad = grads[:, columns]
            dq[:, columns] += mm(k_rows, score_grad, TN)
            k_part = mm(score_grad, head_rows(q, group), NN) * FACTOR
            v_part = mm(weights[:, columns], head_rows(out_low, group), NN)
            put_chunk(d_kv, chunk, group, k_part.astype(jnp.bfloat16))
            put_chunk(d_kv, chunk, KV_HEADS + group, v_part.astype(jnp.bfloat16))
        return carry

    lax.fori_loop(low, high, step, 0)


def back_low_kernel(
    lengths,
    q,
    mine,
    other,
    att,
    lse,
    own_docs,
    upstream,
    out_low,
    delta,
    dq_low,
    d_mine,
    d_other,
    bias,
    grads,
    weights,
):
    row = Row(lengths)
    d_mine[...] = jnp.zeros(d_mine.shape, d_mine.dtype)
    d_other[...] = jnp.zeros(d_other.shape, d_other.dtype)
    fill_bias(row, row.low, bias)
    w = jnp.concatenate(
        [
            jnp.concatenate([upstream[2 * d + c] for d in range(DOCS)] * 2, axis=0)
            for c in range(2)
        ],
        axis=1,
    )
    docs = own_docs[...]
    doc_inv = lax.rsqrt(jnp.sum(docs * docs, axis=1, keepdims=True) + EPSILON)
    unit = docs * doc_inv
    inner = jnp.sum(unit * w, axis=1, keepdims=True)
    doc_grad = doc_inv * (w - unit * inner) / row.length_column()
    big, small = halves(doc_grad)
    member = row.member.astype(jnp.bfloat16)
    out_low[...] = mm(member, big, TN).astype(jnp.bfloat16)
    both = jnp.concatenate([big, small], axis=0)
    twice = jnp.concatenate([member, member], axis=0)
    for h in range(HEADS):
        at = head(h)
        one = jnp.sum(mm(both[:, at], twice, TN) * att[:, at], axis=0, keepdims=True)
        delta[:, at] = jnp.broadcast_to(one, (8, TOK))
    dq_low[...] = jnp.zeros(dq_low.shape, jnp.float32)
    kv, d_kv = (mine, other), (d_mine, d_other)
    back_part(row.low, q, kv, bias, lse, out_low, delta, dq_low, d_kv, grads, weights)


def back_own_kernel(
    lengths,
    q,
    mine,
    other,
    lse,
    out_low,
    delta,
    dq_low,
    grad_q,
    d_mine,
    d_other,
    bias,
    dq,
    grads,
    weights,
):
    row = Row(lengths)
    d_mine[...] = jnp.zeros(d_mine.shape, d_mine.dtype)
    d_other[...] = jnp.zeros(d_other.shape, d_other.dtype)
    fill_bias(row, row.own, bias)
    dq[...] = dq_low[...]
    kv, d_kv = (mine, other), (d_mine, d_other)
    back_part(row.own, q, kv, bias, lse, out_low, delta, dq, d_kv, grads, weights)
    for h in range(HEADS):
        grad_q[:, head(h)] = (dq[:, head(h)].T * FACTOR).astype(jnp.bfloat16)


F32, BF16 = jnp.float32, jnp.bfloat16


def shape(dims, dtype):
    return jax.ShapeDtypeStruct(dims, dtype)


def run(kernel, name, outs, scratch, lengths, *arrays, flops=0):
    vmem = pl.BlockSpec(memory_space=pltpu.VMEM)
    smem = pl.BlockSpec(memory_space=pltpu.SMEM)
    first = () if lengths is None else (lengths,)
    return pl.pallas_call(
        kernel,
        out_shape=outs,
        in_specs=[smem] * len(first) + [vmem] * len(arrays),
        out_specs=tuple(vmem for _ in outs),
        scratch_shapes=scratch,
        compiler_params=pltpu.CompilerParams(vmem_limit_bytes=VMEM_BYTES),
        cost_estimate=pl.CostEstimate(flops=flops, bytes_accessed=0, transcendentals=0),
        name=name,
    )(*first, *arrays)


TERMS = shape((CHUNKS, TOK, 2 * KVW), BF16)
WIDE = pltpu.VMEM((HEAD_DIM, EMB), F32)
BIAS = pltpu.VMEM((CHUNKS, CHUNK, TOK), F32)
STATS = pltpu.VMEM((2, HEADS, TOK), F32)
ROUNDED = pltpu.VMEM((CHUNK, EMB), BF16)


def attend_own(lengths, *arrays):
    outs = (shape((HEAD_DIM, EMB), F32), shape((8, EMB), F32))
    return run(attend_own_kernel, "attend_own", outs, [BIAS, STATS, ROUNDED, WIDE], lengths, *arrays)


def attend_low(lengths, *arrays):
    outs = (shape((HEAD_DIM, EMB), F32), shape((8, EMB), F32), shape((8, 1, PIECE), F32))
    scratch = [BIAS, STATS, ROUNDED, WIDE, pltpu.VMEM((8, EMB), F32)]
    return run(attend_low_kernel, "attend_low", outs, scratch, lengths, *arrays)


def contrast(*arrays):
    outs = (shape((NDOC, 128), F32), shape((32, 1, PIECE), F32), shape((8, EMB), F32))
    return run(contrast_kernel, "contrast", outs, [], None, *arrays)


def query_back(*arrays):
    return run(query_kernel, "query_back", (shape((128, EMB), F32),), [], None, *arrays)[0]


def back_low(lengths, *arrays):
    outs = (
        shape((TOK, EMB), BF16),
        shape((8, EMB), F32),
        shape((HEAD_DIM, EMB), F32),
        TERMS,
        TERMS,
    )
    return run(back_low_kernel, "back_low", outs, [BIAS, ROUNDED, ROUNDED], lengths, *arrays)


def back_own(lengths, *arrays):
    outs = (shape((TOK, EMB), BF16), TERMS, TERMS)
    return run(back_own_kernel, "back_own", outs, [BIAS, WIDE, ROUNDED, ROUNDED], lengths, *arrays)


def to_all(block, axes, count):
    return lax.all_to_all(jnp.broadcast_to(block[None], (count,) + block.shape), axes, 0, 0)


def swap_cores(block):
    return lax.ppermute(block, "core", [(0, 1), (1, 0)])


def added(blocks):
    total = blocks[0].astype(F32)
    for i in range(1, blocks.shape[0]):
        total = total + blocks[i].astype(F32)
    return total


def pair_terms(d_mine, d_other):
    got = swap_cores(d_other)
    return (d_mine.astype(F32) + got.astype(F32)).astype(BF16)


def per_device(queries_q, keys, values, lengths, query_emb, positive):
    q = queries_q[0]
    kv = jnp.concatenate([keys[0], values[0]], axis=1)
    kv_low = lax.ppermute(kv, "zhi", [(0, 1)])
    own_mine = to_all(kv, "x", 4)
    kv_low, own_mine = lax.optimization_barrier((kv_low, own_mine))
    own_other = swap_cores(own_mine)
    own_att, own_lse = attend_own(lengths, q, own_mine, own_other)
    low_mine = to_all(kv_low, "x", 4)
    low_other = swap_cores(low_mine)
    att, lse, pieces = attend_low(lengths, q, low_mine, low_other, own_att, own_lse)

    part = added(lax.all_to_all(pieces, NEAR, 0, 0))
    column = to_all(part, ("zlo", "zhi"), 16)
    column = (column[0::2] + column[1::2]).reshape(8, PIECE)
    docs_mine = to_all(column, ("y", "x"), 16).reshape(NDOC, PIECE)
    docs_other = swap_cores(docs_mine)

    coefficient, terms, own_docs = contrast(
        query_emb, positive.reshape(1, 128), docs_mine, docs_other
    )
    terms = added(lax.all_to_all(terms, ("y", "zlo"), 0, 0))
    upstream = to_all(terms, NEAR, 8)

    out_low, delta, dq_low, d_mine, d_other = back_low(
        lengths, q, low_mine, low_other, att, lse, own_docs, upstream
    )
    paired = pair_terms(d_mine, d_other)
    paired, dq_low = lax.optimization_barrier((paired, dq_low))
    grad_q, own_d_mine, own_d_other = back_own(
        lengths, q, own_mine, own_other, lse, out_low, delta, dq_low
    )
    low_terms = lax.all_to_all(paired, "x", 0, 0)
    low_sum = added(low_terms).astype(BF16)
    own_paired = pair_terms(own_d_mine, own_d_other)
    low_sum, own_paired = lax.optimization_barrier((low_sum, own_paired))
    from_high = lax.ppermute(low_sum, "zhi", [(1, 0)])
    own_terms = lax.all_to_all(own_paired, "x", 0, 0)
    own_sum = added(own_terms)
    coefficient, low_sum = lax.optimization_barrier((coefficient, low_sum))
    query_grad = query_back(query_emb, docs_mine, docs_other, coefficient)
    query_grad, from_high = lax.optimization_barrier((query_grad, from_high))
    total = (own_sum + from_high.astype(F32)).astype(BF16)
    return (query_grad, grad_q[None], total[None, :, :KVW], total[None, :, KVW:])


def solution(mesh):
    fine = Mesh(mesh.devices.reshape(8, 4, 2, 4, 2), ("zlo", "y", "zhi", "x", "core"))
    dp, ctx = ("zlo", "y"), ("zhi", "x", "core")
    tokens = P(dp, ctx, None)
    return jax.shard_map(
        per_device,
        mesh=fine,
        in_specs=(tokens, tokens, tokens, P(dp, None), P(dp, None), P(dp)),
        out_specs=(P(dp, None), tokens, tokens, tokens),
        check_vma=False,
    )
```

```python
import jax
import jax.numpy as jnp
from jax import lax
from jax.experimental import pallas as pl
from jax.experimental.pallas import tpu as pltpu
from jax.sharding import Mesh
from jax.sharding import PartitionSpec as P

HEAD_DIM = 128
HEADS = 14
KV_HEADS = 2
PER_GROUP = HEADS // KV_HEADS
DOCS = 4
TOK = 128
SEQ = 2048
EMB = HEADS * HEAD_DIM
KVW = KV_HEADS * HEAD_DIM
GROUP_W = PER_GROUP * TOK
CHUNK = 2 * TOK
HALF = SEQ // 2
CHUNKS = HALF // CHUNK
PIECE = EMB // 2
NDOC = 128
SHARE = 32
SHARED = 8 * SHARE
SHARE_W = 2048

FACTOR = HEAD_DIM ** (-0.5)
INVERSE_TEMPER = 0.05
EPSILON = 1e-06
FULL_ACCURACY = lax.Precision.HIGHEST
MASKED = -1e30
TINY = 1e-30
NT = (((1,), (1,)), ((), ()))
TN = (((0,), (0,)), ((), ()))
NN = (((1,), (0,)), ((), ()))
NEAR = ("x", "core")
VMEM_BYTES = 24 * 1024 * 1024


def mm(a, b, dims, precision=None):
    return lax.dot_general(a, b, dims, precision=precision, preferred_element_type=jnp.float32)


def place():
    return tuple(lax.axis_index(axis) for axis in ("zlo", "y", "zhi", "x", "core"))


class Row:
    def __init__(self, lengths):
        _, _, self.high, x, self.core = place()
        self.first = ((self.high * 4 + x) * 2 + self.core) * TOK
        self.lengths = [lengths[0, d] for d in range(DOCS)]
        qpos = self.first + lax.broadcasted_iota(jnp.int32, (1, TOK), 1)
        start = jnp.zeros((1, TOK), jnp.int32)
        doc = jnp.zeros((1, TOK), jnp.int32)
        first_start = jnp.int32(0)
        end = jnp.int32(0)
        for d in range(DOCS - 1):
            end = end + self.lengths[d]
            start = jnp.where(qpos >= end, end, start)
            doc = doc + (qpos >= end).astype(jnp.int32)
            first_start = jnp.where(self.first >= end, end, first_start)
        self.qpos, self.start = qpos, start
        self.member = (lax.broadcasted_iota(jnp.int32, (8, TOK), 0) == doc).astype(jnp.float32)
        own_base = self.high * HALF
        self.own = (
            own_base,
            lax.div(jnp.maximum(first_start - own_base, 0), CHUNK),
            lax.div(self.first + (TOK - 1) - own_base, CHUNK) + 1,
        )
        self.low = (jnp.int32(0), lax.div(first_start, CHUNK), CHUNKS * self.high)

    def length_column(self):
        rows = lax.broadcasted_iota(jnp.int32, (8, 1), 0)
        column = jnp.ones((8, 1), jnp.float32)
        for d in range(DOCS):
            column = jnp.where(rows == d, self.lengths[d].astype(jnp.float32), column)
        return column

    def bias(self, base, chunk):
        at = lax.broadcasted_iota(jnp.int32, (CHUNK, TOK), 0)
        half = lax.div(at, TOK)
        turned = jnp.where(self.core == 1, 1 - half, half)
        pos = base + chunk * CHUNK + turned * TOK + (at - half * TOK)
        allowed = (pos >= self.start) & (pos <= self.qpos)
        return jnp.where(allowed, 0.0, MASKED).astype(jnp.float32)


def chunk_of(kv, chunk, column):
    at = slice(column * HEAD_DIM, (column + 1) * HEAD_DIM)
    return jnp.concatenate([half[chunk, :, at] for half in kv], axis=0)


def put_chunk(refs, chunk, column, rows):
    at = slice(column * HEAD_DIM, (column + 1) * HEAD_DIM)
    refs[0][chunk, :, at] = rows[:TOK]
    refs[1][chunk, :, at] = rows[TOK:]


def fill_bias(row, part, bias):
    base, low, high = part

    def step(chunk, carry):
        bias[chunk] = row.bias(base, chunk)
        return carry

    lax.fori_loop(low, high, step, 0)


def halves(values):
    top = values.astype(jnp.bfloat16)
    return top, (values - top.astype(jnp.float32)).astype(jnp.bfloat16)


def head_rows(ref, group):
    return jnp.concatenate(
        [
            ref[:, (group * PER_GROUP + h) * HEAD_DIM : (group * PER_GROUP + h + 1) * HEAD_DIM]
            for h in range(PER_GROUP)
        ],
        axis=0,
    )


def head(h):
    return slice(h * HEAD_DIM, (h + 1) * HEAD_DIM)


def part_attention(part, q, kv, bias, stats, weights, out):
    _, low, high = part
    stats[0] = jnp.full((HEADS, TOK), MASKED, jnp.float32)
    stats[1] = jnp.zeros((HEADS, TOK), jnp.float32)
    out[...] = jnp.zeros(out.shape, jnp.float32)

    def step(chunk, carry):
        blocked = bias[chunk]
        for group in range(KV_HEADS):
            k_rows = chunk_of(kv, chunk, group)
            scales = []
            for h in range(group * PER_GROUP, (group + 1) * PER_GROUP):
                scores = mm(k_rows, q[:, head(h)], NT) + blocked
                old = stats[0, h : h + 1]
                top = jnp.maximum(old, jnp.max(scores, axis=0, keepdims=True))
                exps = jnp.exp((scores - top) * FACTOR)
                weights[:, head(h)] = exps.astype(jnp.bfloat16)
                scale = jnp.exp((old - top) * FACTOR)
                stats[0, h : h + 1] = top
                stats[1, h : h + 1] = stats[1, h : h + 1] * scale + jnp.sum(
                    exps, axis=0, keepdims=True
                )
                scales.append(scale)
            columns = slice(group * GROUP_W, (group + 1) * GROUP_W)
            sums = mm(chunk_of(kv, chunk, KV_HEADS + group), weights[:, columns], TN)
            for i in range(PER_GROUP):
                at = head(group * PER_GROUP + i)
                out[:, at] = out[:, at] * scales[i] + sums[:, head(i)]
        return carry

    lax.fori_loop(low, high, step, 0)


def part_result(h, stats):
    total = jnp.maximum(stats[1, h : h + 1], TINY)
    return stats[0, h : h + 1] * FACTOR + jnp.log(total), 1.0 / total


def attend_own_kernel(lengths, q, mine, other, att, lse, bias, stats, weights, out):
    row = Row(lengths)
    fill_bias(row, row.own, bias)
    part_attention(row.own, q, (mine, other), bias, stats, weights, out)
    for h in range(HEADS):
        log_total, inverse = part_result(h, stats)
        att[:, head(h)] = out[:, head(h)] * inverse
        lse[:, head(h)] = jnp.broadcast_to(log_total, (8, TOK))


def attend_low_kernel(
    lengths, q, mine, other, own_att, own_lse, att, lse, pieces, bias, stats, weights, out, doc_sum
):
    row = Row(lengths)
    fill_bias(row, row.low, bias)
    member = jnp.concatenate([row.member, jnp.zeros((TOK - 8, TOK), jnp.float32)], axis=0)
    member = member.astype(jnp.bfloat16)
    part_attention(row.low, q, (mine, other), bias, stats, weights, out)
    for h in range(HEADS):
        at = head(h)
        low_total, inverse = part_result(h, stats)
        own_total = own_lse[0:1, at]
        top = jnp.maximum(low_total, own_total)
        log_total = top + jnp.log(jnp.exp(low_total - top) + jnp.exp(own_total - top))
        own_scale = jnp.exp(own_total - log_total)
        low_scale = jnp.exp(low_total - log_total) * inverse
        lse[:, at] = jnp.broadcast_to(log_total, (8, TOK))
        merged = own_att[:, at] * own_scale + out[:, at] * low_scale
        att[:, at] = merged
        big, small = halves(merged)
        doc_sum[:, at] = (mm(big, member, NT) + mm(small, member, NT)).T[:8]
    mean = doc_sum[...] / row.length_column()
    for d in range(DOCS):
        for c in range(2):
            pieces[2 * d + c] = mean[d : d + 1, c * PIECE : (c + 1) * PIECE]


def own_rows(core, left_or_mine, right_or_other):
    return jnp.where(core == 1, right_or_other, left_or_mine)


def share_kernel(q, positive, out):
    _, _, _, x, _ = place()
    first = x * SHARE
    rows = q[pl.ds(pl.multiple_of(first, SHARE), SHARE), :]
    out[:, :EMB] = rows
    values = rows.astype(jnp.float32)
    inverse = lax.rsqrt(jnp.sum(values * values, axis=1, keepdims=True) + EPSILON)
    lane = lax.broadcasted_iota(jnp.int32, (SHARE, 128), 1)
    row = lax.broadcasted_iota(jnp.int32, (SHARE, 128), 0)
    doc = jnp.sum(
        jnp.where(lane == first + row, positive[...].astype(jnp.float32), 0.0),
        axis=1,
        keepdims=True,
    )
    extra = jnp.where(lane == 0, doc, 0.0)
    rest = inverse
    for i in range(1, 4):
        piece = rest.astype(jnp.bfloat16).astype(jnp.float32)
        extra = jnp.where(lane == i, piece, extra)
        rest = rest - piece
    out[:, EMB : EMB + 128] = extra.astype(jnp.bfloat16)
    out[:, EMB + 128 :] = jnp.zeros((SHARE, SHARE_W - EMB - 128), jnp.bfloat16)


def contrast_kernel(shared, docs_mine, docs_other, terms, own_docs, coefficient):
    z_lo, y, _, _, core = place()
    d_mine, d_other = docs_mine[...], docs_other[...]
    doc_inv = lax.rsqrt(
        jnp.sum(d_mine * d_mine, axis=1, keepdims=True)
        + jnp.sum(d_other * d_other, axis=1, keepdims=True)
        + EPSILON
    )
    extra = shared[:, EMB : EMB + 128].astype(jnp.float32).T
    target_doc = extra[0:1]
    query_inv = extra[1:2] + extra[2:3] + extra[3:4]
    left = own_rows(core, d_mine, d_other) * doc_inv
    right = own_rows(core, d_other, d_mine) * doc_inv
    logits = jnp.zeros((NDOC, SHARED), jnp.float32)
    for part, at in ((left, slice(0, PIECE)), (right, slice(PIECE, EMB))):
        for piece in halves(part):
            logits = logits + mm(piece, shared[:, at], NT)
    exps = jnp.exp(logits * query_inv / INVERSE_TEMPER)
    at = lax.broadcasted_iota(jnp.int32, (NDOC, SHARED), 0)
    doc = ((at % 8) * 4 + at // 32) * DOCS + (at // 8) % 4
    target = (doc.astype(jnp.float32) == target_doc).astype(jnp.float32)
    share = exps / jnp.sum(exps, axis=0, keepdims=True) - target
    coefficient[...] = share * query_inv / INVERSE_TEMPER
    own_docs[...] = jnp.zeros((8, EMB), jnp.float32)
    near = []
    for d in range(DOCS):
        r = y * 32 + d * 8 + z_lo
        a, b = docs_mine[pl.ds(r, 1), :], docs_other[pl.ds(r, 1), :]
        own_docs[d : d + 1, :PIECE] = own_rows(core, a, b)
        own_docs[d : d + 1, PIECE:] = own_rows(core, b, a)
        for other_y in range(4):
            near.append(coefficient[pl.ds(other_y * 32 + d * 8 + z_lo, 1), :])
    big, small = halves(jnp.concatenate(near, axis=0))
    sums = mm(jnp.concatenate([big, small], axis=0), shared[:, :EMB], NN)
    for d in range(DOCS):
        for other_y in range(4):
            r = d * 4 + other_y
            one = sums[r : r + 1] + sums[16 + r : 17 + r]
            for c in range(2):
                row = 2 * d + c
                terms[other_y, row : row + 1, :] = one[:, c * PIECE : (c + 1) * PIECE]


def query_kernel(q, positive, docs_mine, docs_other, query_grad):
    _, _, _, _, core = place()
    d_mine, d_other = docs_mine[...], docs_other[...]
    doc_inv = lax.rsqrt(
        jnp.sum(d_mine * d_mine, axis=1, keepdims=True)
        + jnp.sum(d_other * d_other, axis=1, keepdims=True)
        + EPSILON
    )
    left = own_rows(core, d_mine, d_other) * doc_inv
    right = own_rows(core, d_other, d_mine) * doc_inv
    q_all = q[...].astype(jnp.float32)
    query_inv = lax.rsqrt(jnp.sum(q_all * q_all, axis=1, keepdims=True) + EPSILON)
    q_unit = q_all * query_inv
    q_left, q_right = q_unit[:, :PIECE], q_unit[:, PIECE:]
    logits = mm(left, q_left, NT, FULL_ACCURACY) + mm(right, q_right, NT, FULL_ACCURACY)
    exps = jnp.exp(logits / INVERSE_TEMPER)
    at = lax.broadcasted_iota(jnp.int32, (NDOC, 128), 0)
    doc = ((at % 8) * 4 + at // 32) * DOCS + (at // 8) % 4
    target = (doc == positive[...]).astype(jnp.float32)
    coefficient = exps / jnp.sum(exps, axis=0, keepdims=True) - target
    u_left = mm(coefficient, left, TN, FULL_ACCURACY) / INVERSE_TEMPER
    u_right = mm(coefficient, right, TN, FULL_ACCURACY) / INVERSE_TEMPER
    inner = jnp.sum(q_left * u_left, axis=1, keepdims=True) + jnp.sum(
        q_right * u_right, axis=1, keepdims=True
    )
    query_grad[:, :PIECE] = query_inv * (u_left - q_left * inner)
    query_grad[:, PIECE:] = query_inv * (u_right - q_right * inner)


def back_part(part, q, kv, bias, lse, out_low, delta, dq, d_kv, grads, weights):
    _, low, high = part

    def step(chunk, carry):
        blocked = bias[chunk]
        for group in range(KV_HEADS):
            k_rows = chunk_of(kv, chunk, group)
            v_rows = chunk_of(kv, chunk, KV_HEADS + group)
            for h in range(group * PER_GROUP, (group + 1) * PER_GROUP):
                at = head(h)
                scores = mm(k_rows, q[:, at], NT) * FACTOR + blocked
                probs = jnp.exp(scores - lse[0:1, at])
                flow = mm(v_rows, out_low[:, at], NT)
                grads[:, at] = (probs * (flow - delta[0:1, at])).astype(jnp.bfloat16)
                weights[:, at] = probs.astype(jnp.bfloat16)
            columns = slice(group * GROUP_W, (group + 1) * GROUP_W)
            score_grad = grads[:, columns]
            dq[:, columns] += mm(k_rows, score_grad, TN)
            k_part = mm(score_grad, head_rows(q, group), NN) * FACTOR
            v_part = mm(weights[:, columns], head_rows(out_low, group), NN)
            put_chunk(d_kv, chunk, group, k_part.astype(jnp.bfloat16))
            put_chunk(d_kv, chunk, KV_HEADS + group, v_part.astype(jnp.bfloat16))
        return carry

    lax.fori_loop(low, high, step, 0)


def back_low_kernel(
    lengths,
    q,
    mine,
    other,
    att,
    lse,
    own_docs,
    upstream,
    out_low,
    delta,
    dq_low,
    d_mine,
    d_other,
    bias,
    grads,
    weights,
):
    row = Row(lengths)
    d_mine[...] = jnp.zeros(d_mine.shape, d_mine.dtype)
    d_other[...] = jnp.zeros(d_other.shape, d_other.dtype)
    fill_bias(row, row.low, bias)
    w = jnp.concatenate(
        [
            jnp.concatenate([upstream[2 * d + c : 2 * d + c + 1] for d in range(DOCS)] * 2, axis=0)
            for c in range(2)
        ],
        axis=1,
    )
    docs = own_docs[...]
    doc_inv = lax.rsqrt(jnp.sum(docs * docs, axis=1, keepdims=True) + EPSILON)
    unit = docs * doc_inv
    inner = jnp.sum(unit * w, axis=1, keepdims=True)
    doc_grad = doc_inv * (w - unit * inner) / row.length_column()
    big, small = halves(doc_grad)
    member = row.member.astype(jnp.bfloat16)
    out_low[...] = mm(member, big, TN).astype(jnp.bfloat16)
    both = jnp.concatenate([big, small], axis=0)
    twice = jnp.concatenate([member, member], axis=0)
    for h in range(HEADS):
        at = head(h)
        one = jnp.sum(mm(both[:, at], twice, TN) * att[:, at], axis=0, keepdims=True)
        delta[:, at] = jnp.broadcast_to(one, (8, TOK))
    dq_low[...] = jnp.zeros(dq_low.shape, jnp.float32)
    kv, d_kv = (mine, other), (d_mine, d_other)
    back_part(row.low, q, kv, bias, lse, out_low, delta, dq_low, d_kv, grads, weights)


def back_own_kernel(
    lengths,
    q,
    mine,
    other,
    lse,
    out_low,
    delta,
    dq_low,
    grad_q,
    d_mine,
    d_other,
    bias,
    dq,
    grads,
    weights,
):
    row = Row(lengths)
    d_mine[...] = jnp.zeros(d_mine.shape, d_mine.dtype)
    d_other[...] = jnp.zeros(d_other.shape, d_other.dtype)
    fill_bias(row, row.own, bias)
    dq[...] = dq_low[...]
    kv, d_kv = (mine, other), (d_mine, d_other)
    back_part(row.own, q, kv, bias, lse, out_low, delta, dq, d_kv, grads, weights)
    for h in range(HEADS):
        grad_q[:, head(h)] = (dq[:, head(h)].T * FACTOR).astype(jnp.bfloat16)


F32, BF16 = jnp.float32, jnp.bfloat16


def shape(dims, dtype):
    return jax.ShapeDtypeStruct(dims, dtype)


def run(kernel, name, outs, scratch, lengths, *arrays, flops=0):
    vmem = pl.BlockSpec(memory_space=pltpu.VMEM)
    smem = pl.BlockSpec(memory_space=pltpu.SMEM)
    first = () if lengths is None else (lengths,)
    return pl.pallas_call(
        kernel,
        out_shape=outs,
        in_specs=[smem] * len(first) + [vmem] * len(arrays),
        out_specs=tuple(vmem for _ in outs),
        scratch_shapes=scratch,
        compiler_params=pltpu.CompilerParams(vmem_limit_bytes=VMEM_BYTES),
        cost_estimate=pl.CostEstimate(flops=flops, bytes_accessed=0, transcendentals=0),
        name=name,
    )(*first, *arrays)


TERMS = shape((CHUNKS, TOK, 2 * KVW), BF16)
WIDE = pltpu.VMEM((HEAD_DIM, EMB), F32)
BIAS = pltpu.VMEM((CHUNKS, CHUNK, TOK), F32)
STATS = pltpu.VMEM((2, HEADS, TOK), F32)
ROUNDED = pltpu.VMEM((CHUNK, EMB), BF16)


def attend_own(lengths, *arrays):
    outs = (shape((HEAD_DIM, EMB), F32), shape((8, EMB), F32))
    return run(attend_own_kernel, "attend_own", outs, [BIAS, STATS, ROUNDED, WIDE], lengths, *arrays)


def attend_low(lengths, *arrays):
    outs = (shape((HEAD_DIM, EMB), F32), shape((8, EMB), F32), shape((8, 1, PIECE), F32))
    scratch = [BIAS, STATS, ROUNDED, WIDE, pltpu.VMEM((8, EMB), F32)]
    return run(attend_low_kernel, "attend_low", outs, scratch, lengths, *arrays)


def share(*arrays):
    outs = (shape((SHARE, SHARE_W), BF16),)
    return run(share_kernel, "share", outs, [], None, *arrays)[0]


def contrast(*arrays):
    outs = (shape((4, 8, PIECE), F32), shape((8, EMB), F32))
    scratch = [pltpu.VMEM((NDOC, SHARED), F32)]
    return run(contrast_kernel, "contrast", outs, scratch, None, *arrays)


def query_back(*arrays):
    return run(query_kernel, "query_back", (shape((128, EMB), F32),), [], None, *arrays)[0]


def back_low(lengths, *arrays):
    outs = (
        shape((TOK, EMB), BF16),
        shape((8, EMB), F32),
        shape((HEAD_DIM, EMB), F32),
        TERMS,
        TERMS,
    )
    return run(back_low_kernel, "back_low", outs, [BIAS, ROUNDED, ROUNDED], lengths, *arrays)


def back_own(lengths, *arrays):
    outs = (shape((TOK, EMB), BF16), TERMS, TERMS)
    return run(back_own_kernel, "back_own", outs, [BIAS, WIDE, ROUNDED, ROUNDED], lengths, *arrays)


def to_all(block, axes, count):
    return lax.all_to_all(jnp.broadcast_to(block[None], (count,) + block.shape), axes, 0, 0)


def swap_cores(block):
    return lax.ppermute(block, "core", [(0, 1), (1, 0)])


def added(blocks):
    total = blocks[0].astype(F32)
    for i in range(1, blocks.shape[0]):
        total = total + blocks[i].astype(F32)
    return total


def pair_terms(d_mine, d_other):
    got = swap_cores(d_other)
    return (d_mine.astype(F32) + got.astype(F32)).astype(BF16)


def per_device(queries_q, keys, values, lengths, query_emb, positive):
    q = queries_q[0]
    kv = jnp.concatenate([keys[0], values[0]], axis=1)
    kv_low = lax.ppermute(kv, "zhi", [(0, 1)])
    own_mine = to_all(kv, "x", 4)
    positive = positive.reshape(1, 128)
    shared = lax.all_gather(share(query_emb, positive), "zlo", axis=0, tiled=True)
    kv_low, own_mine = lax.optimization_barrier((kv_low, own_mine))
    own_other = swap_cores(own_mine)
    own_att, own_lse = attend_own(lengths, q, own_mine, own_other)
    low_mine = to_all(kv_low, "x", 4)
    low_other = swap_cores(low_mine)
    att, lse, pieces = attend_low(lengths, q, low_mine, low_other, own_att, own_lse)

    part = added(lax.all_to_all(pieces, NEAR, 0, 0))
    column = to_all(part, ("zlo", "zhi"), 16)
    column = (column[0::2] + column[1::2]).reshape(8, PIECE)
    docs_mine = to_all(column, ("y", "x"), 16).reshape(NDOC, PIECE)
    docs_other = swap_cores(docs_mine)

    terms, own_docs = contrast(shared, docs_mine, docs_other)
    terms = jnp.broadcast_to(terms[:, None], (4, 4, 8, PIECE)).reshape(16, 8, PIECE)
    upstream = added(lax.all_to_all(terms, ("y", "x"), 0, 0))

    out_low, delta, dq_low, d_mine, d_other = back_low(
        lengths, q, low_mine, low_other, att, lse, own_docs, upstream
    )
    paired = pair_terms(d_mine, d_other)
    paired, dq_low = lax.optimization_barrier((paired, dq_low))
    grad_q, own_d_mine, own_d_other = back_own(
        lengths, q, own_mine, own_other, lse, out_low, delta, dq_low
    )
    low_terms = lax.all_to_all(paired, "x", 0, 0)
    low_sum = added(low_terms).astype(BF16)
    own_paired = pair_terms(own_d_mine, own_d_other)
    low_sum, own_paired = lax.optimization_barrier((low_sum, own_paired))
    from_high = lax.ppermute(low_sum, "zhi", [(1, 0)])
    own_terms = lax.all_to_all(own_paired, "x", 0, 0)
    own_sum = added(own_terms)
    docs_mine, low_sum = lax.optimization_barrier((docs_mine, low_sum))
    query_grad = query_back(query_emb, positive, docs_mine, docs_other)
    query_grad, from_high = lax.optimization_barrier((query_grad, from_high))
    total = (own_sum + from_high.astype(F32)).astype(BF16)
    return (query_grad, grad_q[None], total[None, :, :KVW], total[None, :, KVW:])


def solution(mesh):
    fine = Mesh(mesh.devices.reshape(8, 4, 2, 4, 2), ("zlo", "y", "zhi", "x", "core"))
    dp, ctx = ("zlo", "y"), ("zhi", "x", "core")
    tokens = P(dp, ctx, None)
    return jax.shard_map(
        per_device,
        mesh=fine,
        in_specs=(tokens, tokens, tokens, P(dp, None), P(dp, None), P(dp)),
        out_specs=(P(dp, None), tokens, tokens, tokens),
        check_vma=False,
    )
```

```python
import jax
import jax.numpy as jnp
from jax import lax
from jax.experimental import pallas as pl
from jax.experimental.pallas import tpu as pltpu
from jax.sharding import Mesh
from jax.sharding import PartitionSpec as P

HEAD_DIM = 128
HEADS = 14
KV_HEADS = 2
PER_GROUP = HEADS // KV_HEADS
DOCS = 4
TOK = 128
SEQ = 2048
EMB = HEADS * HEAD_DIM
KVW = KV_HEADS * HEAD_DIM
GROUP_W = PER_GROUP * TOK
CHUNK = 2 * TOK
HALF = SEQ // 2
CHUNKS = HALF // CHUNK
PIECE = EMB // 2
NDOC = 128

FACTOR = HEAD_DIM ** (-0.5)
INVERSE_TEMPER = 0.05
EPSILON = 1e-06
FULL_ACCURACY = lax.Precision.HIGHEST
MASKED = -1e30
TINY = 1e-30
FILLS_A_WAIT = 10**12
NT = (((1,), (1,)), ((), ()))
TN = (((0,), (0,)), ((), ()))
NN = (((1,), (0,)), ((), ()))
NEAR = ("x", "core")
VMEM_BYTES = 24 * 1024 * 1024


def mm(a, b, dims, precision=None):
    return lax.dot_general(a, b, dims, precision=precision, preferred_element_type=jnp.float32)


def place():
    return tuple(lax.axis_index(axis) for axis in ("zlo", "y", "zhi", "x", "core"))


class Row:
    def __init__(self, lengths):
        _, _, self.high, x, self.core = place()
        self.first = ((self.high * 4 + x) * 2 + self.core) * TOK
        self.lengths = [lengths[0, d] for d in range(DOCS)]
        qpos = self.first + lax.broadcasted_iota(jnp.int32, (1, TOK), 1)
        start = jnp.zeros((1, TOK), jnp.int32)
        doc = jnp.zeros((1, TOK), jnp.int32)
        first_start = jnp.int32(0)
        end = jnp.int32(0)
        for d in range(DOCS - 1):
            end = end + self.lengths[d]
            start = jnp.where(qpos >= end, end, start)
            doc = doc + (qpos >= end).astype(jnp.int32)
            first_start = jnp.where(self.first >= end, end, first_start)
        self.qpos, self.start = qpos, start
        self.member = (lax.broadcasted_iota(jnp.int32, (8, TOK), 0) == doc).astype(jnp.float32)
        own_base = self.high * HALF
        self.own = (
            own_base,
            lax.div(jnp.maximum(first_start - own_base, 0), CHUNK),
            lax.div(self.first + (TOK - 1) - own_base, CHUNK) + 1,
        )
        self.low = (jnp.int32(0), lax.div(first_start, CHUNK), CHUNKS * self.high)

    def length_column(self):
        rows = lax.broadcasted_iota(jnp.int32, (8, 1), 0)
        column = jnp.ones((8, 1), jnp.float32)
        for d in range(DOCS):
            column = jnp.where(rows == d, self.lengths[d].astype(jnp.float32), column)
        return column

    def bias(self, base, chunk):
        at = lax.broadcasted_iota(jnp.int32, (CHUNK, TOK), 0)
        half = lax.div(at, TOK)
        turned = jnp.where(self.core == 1, 1 - half, half)
        pos = base + chunk * CHUNK + turned * TOK + (at - half * TOK)
        allowed = (pos >= self.start) & (pos <= self.qpos)
        return jnp.where(allowed, 0.0, MASKED).astype(jnp.float32)


def chunk_of(kv, chunk, column):
    at = slice(column * HEAD_DIM, (column + 1) * HEAD_DIM)
    return jnp.concatenate([half[chunk, :, at] for half in kv], axis=0)


def put_chunk(refs, chunk, column, rows):
    at = slice(column * HEAD_DIM, (column + 1) * HEAD_DIM)
    refs[0][chunk, :, at] = rows[:TOK]
    refs[1][chunk, :, at] = rows[TOK:]


def fill_bias(row, part, bias):
    base, low, high = part

    def step(chunk, carry):
        bias[chunk] = row.bias(base, chunk)
        return carry

    lax.fori_loop(low, high, step, 0)


def halves(values):
    top = values.astype(jnp.bfloat16)
    return top, (values - top.astype(jnp.float32)).astype(jnp.bfloat16)


def head_rows(ref, group):
    return jnp.concatenate(
        [
            ref[:, (group * PER_GROUP + h) * HEAD_DIM : (group * PER_GROUP + h + 1) * HEAD_DIM]
            for h in range(PER_GROUP)
        ],
        axis=0,
    )


def head(h):
    return slice(h * HEAD_DIM, (h + 1) * HEAD_DIM)


def part_attention(part, q, kv, bias, stats, weights, out):
    _, low, high = part
    stats[0] = jnp.full((HEADS, TOK), MASKED, jnp.float32)
    stats[1] = jnp.zeros((HEADS, TOK), jnp.float32)
    out[...] = jnp.zeros(out.shape, jnp.float32)

    def step(chunk, carry):
        blocked = bias[chunk]
        for group in range(KV_HEADS):
            k_rows = chunk_of(kv, chunk, group)
            scales = []
            for h in range(group * PER_GROUP, (group + 1) * PER_GROUP):
                scores = mm(k_rows, q[:, head(h)], NT) + blocked
                old = stats[0, h : h + 1]
                top = jnp.maximum(old, jnp.max(scores, axis=0, keepdims=True))
                exps = jnp.exp((scores - top) * FACTOR)
                weights[:, head(h)] = exps.astype(jnp.bfloat16)
                scale = jnp.exp((old - top) * FACTOR)
                stats[0, h : h + 1] = top
                stats[1, h : h + 1] = stats[1, h : h + 1] * scale + jnp.sum(
                    exps, axis=0, keepdims=True
                )
                scales.append(scale)
            columns = slice(group * GROUP_W, (group + 1) * GROUP_W)
            sums = mm(chunk_of(kv, chunk, KV_HEADS + group), weights[:, columns], TN)
            for i in range(PER_GROUP):
                at = head(group * PER_GROUP + i)
                out[:, at] = out[:, at] * scales[i] + sums[:, head(i)]
        return carry

    lax.fori_loop(low, high, step, 0)


def part_result(h, stats):
    total = jnp.maximum(stats[1, h : h + 1], TINY)
    return stats[0, h : h + 1] * FACTOR + jnp.log(total), 1.0 / total


def attend_own_kernel(lengths, q, mine, other, att, lse, bias, stats, weights, out):
    row = Row(lengths)
    fill_bias(row, row.own, bias)
    part_attention(row.own, q, (mine, other), bias, stats, weights, out)
    for h in range(HEADS):
        log_total, inverse = part_result(h, stats)
        att[:, head(h)] = out[:, head(h)] * inverse
        lse[:, head(h)] = jnp.broadcast_to(log_total, (8, TOK))


def attend_low_kernel(
    lengths, q, mine, other, own_att, own_lse, att, lse, pieces, bias, stats, weights, out, doc_sum
):
    row = Row(lengths)
    fill_bias(row, row.low, bias)
    member = jnp.concatenate([row.member, jnp.zeros((TOK - 8, TOK), jnp.float32)], axis=0)
    member = member.astype(jnp.bfloat16)
    part_attention(row.low, q, (mine, other), bias, stats, weights, out)
    for h in range(HEADS):
        at = head(h)
        low_total, inverse = part_result(h, stats)
        own_total = own_lse[0:1, at]
        top = jnp.maximum(low_total, own_total)
        log_total = top + jnp.log(jnp.exp(low_total - top) + jnp.exp(own_total - top))
        own_scale = jnp.exp(own_total - log_total)
        low_scale = jnp.exp(low_total - log_total) * inverse
        lse[:, at] = jnp.broadcast_to(log_total, (8, TOK))
        merged = own_att[:, at] * own_scale + out[:, at] * low_scale
        att[:, at] = merged
        big, small = halves(merged)
        doc_sum[:, at] = (mm(big, member, NT) + mm(small, member, NT)).T[:8]
    mean = doc_sum[...] / row.length_column()
    for d in range(DOCS):
        for c in range(2):
            pieces[2 * d + c] = mean[d : d + 1, c * PIECE : (c + 1) * PIECE]


def inverse_kernel(q, inverse):
    values = q[...].astype(jnp.float32)
    query_inv = lax.rsqrt(jnp.sum(values * values, axis=1, keepdims=True) + EPSILON)
    inverse[...] = jnp.broadcast_to(query_inv, (128, 128))


def unit_kernel(q, inverse, unit):
    unit[...] = q[...].astype(jnp.float32) * inverse[:, :1]


def contrast_kernel(unit, positive, docs_mine, docs_other, coefficient, terms, own_docs):
    z_lo, y, _, x, core = place()
    d_mine, d_other = docs_mine[...], docs_other[...]
    doc_inv = lax.rsqrt(
        jnp.sum(d_mine * d_mine, axis=1, keepdims=True)
        + jnp.sum(d_other * d_other, axis=1, keepdims=True)
        + EPSILON
    )
    q_left, q_right = unit[:, :PIECE], unit[:, PIECE:]
    q_mine = jnp.where(core == 1, q_right, q_left)
    q_other = jnp.where(core == 1, q_left, q_right)
    logits = mm(d_mine * doc_inv, q_mine, NT, FULL_ACCURACY)
    logits = (logits + mm(d_other * doc_inv, q_other, NT, FULL_ACCURACY)) / INVERSE_TEMPER
    exps = jnp.exp(logits)
    at = lax.broadcasted_iota(jnp.int32, (NDOC, 128), 0)
    doc = ((at % 8) * 4 + at // 32) * DOCS + (at // 8) % 4
    target = (doc == positive[...]).astype(jnp.float32)
    coefficient[...] = exps / jnp.sum(exps, axis=0, keepdims=True) - target
    near = jnp.concatenate(
        [coefficient[pl.ds(pl.multiple_of(b * 32 + x * 8, 8), 8), :] for b in range(4)], axis=0
    )
    near_terms = mm(near, q_mine, NN, FULL_ACCURACY) / INVERSE_TEMPER
    for r in range(32):
        terms[r] = near_terms[r : r + 1]
    own_docs[...] = jnp.zeros((8, EMB), jnp.float32)
    for d in range(DOCS):
        r = y * 32 + d * 8 + z_lo
        a, b = docs_mine[pl.ds(r, 1), :], docs_other[pl.ds(r, 1), :]
        own_docs[d : d + 1, :PIECE] = jnp.where(core == 1, b, a)
        own_docs[d : d + 1, PIECE:] = jnp.where(core == 1, a, b)


def query_kernel(unit, inverse, docs_mine, docs_other, coefficient, query_grad):
    _, _, _, _, core = place()
    d_mine, d_other = docs_mine[...], docs_other[...]
    doc_inv = lax.rsqrt(
        jnp.sum(d_mine * d_mine, axis=1, keepdims=True)
        + jnp.sum(d_other * d_other, axis=1, keepdims=True)
        + EPSILON
    )
    scaled = coefficient[...] * doc_inv
    u_mine = mm(scaled, d_mine, TN, FULL_ACCURACY) / INVERSE_TEMPER
    u_other = mm(scaled, d_other, TN, FULL_ACCURACY) / INVERSE_TEMPER
    u_left = jnp.where(core == 1, u_other, u_mine)
    u_right = jnp.where(core == 1, u_mine, u_other)
    query_inv = inverse[:, :1]
    q_left, q_right = unit[:, :PIECE], unit[:, PIECE:]
    inner = jnp.sum(q_left * u_left, axis=1, keepdims=True) + jnp.sum(
        q_right * u_right, axis=1, keepdims=True
    )
    query_grad[:, :PIECE] = query_inv * (u_left - q_left * inner)
    query_grad[:, PIECE:] = query_inv * (u_right - q_right * inner)


def back_part(part, q, kv, bias, lse, out_low, delta, dq, d_kv, grads, weights):
    _, low, high = part

    def step(chunk, carry):
        blocked = bias[chunk]
        for group in range(KV_HEADS):
            k_rows = chunk_of(kv, chunk, group)
            v_rows = chunk_of(kv, chunk, KV_HEADS + group)
            for h in range(group * PER_GROUP, (group + 1) * PER_GROUP):
                at = head(h)
                scores = mm(k_rows, q[:, at], NT) * FACTOR + blocked
                probs = jnp.exp(scores - lse[0:1, at])
                flow = mm(v_rows, out_low[:, at], NT)
                grads[:, at] = (probs * (flow - delta[0:1, at])).astype(jnp.bfloat16)
                weights[:, at] = probs.astype(jnp.bfloat16)
            columns = slice(group * GROUP_W, (group + 1) * GROUP_W)
            score_grad = grads[:, columns]
            dq[:, columns] += mm(k_rows, score_grad, TN)
            k_part = mm(score_grad, head_rows(q, group), NN) * FACTOR
            v_part = mm(weights[:, columns], head_rows(out_low, group), NN)
            put_chunk(d_kv, chunk, group, k_part.astype(jnp.bfloat16))
            put_chunk(d_kv, chunk, KV_HEADS + group, v_part.astype(jnp.bfloat16))
        return carry

    lax.fori_loop(low, high, step, 0)


def back_low_kernel(
    lengths,
    q,
    mine,
    other,
    att,
    lse,
    own_docs,
    upstream,
    out_low,
    delta,
    dq_low,
    d_mine,
    d_other,
    bias,
    grads,
    weights,
):
    row = Row(lengths)
    d_mine[...] = jnp.zeros(d_mine.shape, d_mine.dtype)
    d_other[...] = jnp.zeros(d_other.shape, d_other.dtype)
    fill_bias(row, row.low, bias)
    w = jnp.concatenate(
        [
            jnp.concatenate([upstream[2 * d + c] for d in range(DOCS)] * 2, axis=0)
            for c in range(2)
        ],
        axis=1,
    )
    docs = own_docs[...]
    doc_inv = lax.rsqrt(jnp.sum(docs * docs, axis=1, keepdims=True) + EPSILON)
    unit = docs * doc_inv
    inner = jnp.sum(unit * w, axis=1, keepdims=True)
    doc_grad = doc_inv * (w - unit * inner) / row.length_column()
    big, small = halves(doc_grad)
    member = row.member.astype(jnp.bfloat16)
    out_low[...] = mm(member, big, TN).astype(jnp.bfloat16)
    both = jnp.concatenate([big, small], axis=0)
    twice = jnp.concatenate([member, member], axis=0)
    for h in range(HEADS):
        at = head(h)
        one = jnp.sum(mm(both[:, at], twice, TN) * att[:, at], axis=0, keepdims=True)
        delta[:, at] = jnp.broadcast_to(one, (8, TOK))
    dq_low[...] = jnp.zeros(dq_low.shape, jnp.float32)
    kv, d_kv = (mine, other), (d_mine, d_other)
    back_part(row.low, q, kv, bias, lse, out_low, delta, dq_low, d_kv, grads, weights)


def back_own_kernel(
    lengths,
    q,
    mine,
    other,
    lse,
    out_low,
    delta,
    dq_low,
    grad_q,
    d_mine,
    d_other,
    bias,
    dq,
    grads,
    weights,
):
    row = Row(lengths)
    d_mine[...] = jnp.zeros(d_mine.shape, d_mine.dtype)
    d_other[...] = jnp.zeros(d_other.shape, d_other.dtype)
    fill_bias(row, row.own, bias)
    dq[...] = dq_low[...]
    kv, d_kv = (mine, other), (d_mine, d_other)
    back_part(row.own, q, kv, bias, lse, out_low, delta, dq, d_kv, grads, weights)
    for h in range(HEADS):
        grad_q[:, head(h)] = (dq[:, head(h)].T * FACTOR).astype(jnp.bfloat16)


F32, BF16 = jnp.float32, jnp.bfloat16


def shape(dims, dtype):
    return jax.ShapeDtypeStruct(dims, dtype)


def run(kernel, name, outs, scratch, lengths, *arrays, flops=0):
    vmem = pl.BlockSpec(memory_space=pltpu.VMEM)
    smem = pl.BlockSpec(memory_space=pltpu.SMEM)
    first = () if lengths is None else (lengths,)
    return pl.pallas_call(
        kernel,
        out_shape=outs,
        in_specs=[smem] * len(first) + [vmem] * len(arrays),
        out_specs=tuple(vmem for _ in outs),
        scratch_shapes=scratch,
        compiler_params=pltpu.CompilerParams(vmem_limit_bytes=VMEM_BYTES),
        cost_estimate=pl.CostEstimate(flops=flops, bytes_accessed=0, transcendentals=0),
        name=name,
    )(*first, *arrays)


TERMS = shape((CHUNKS, TOK, 2 * KVW), BF16)
WIDE = pltpu.VMEM((HEAD_DIM, EMB), F32)
BIAS = pltpu.VMEM((CHUNKS, CHUNK, TOK), F32)
STATS = pltpu.VMEM((2, HEADS, TOK), F32)
ROUNDED = pltpu.VMEM((CHUNK, EMB), BF16)


def attend_own(lengths, *arrays):
    outs = (shape((HEAD_DIM, EMB), F32), shape((8, EMB), F32))
    scratch = [BIAS, STATS, ROUNDED, WIDE]
    return run(
        attend_own_kernel, "attend_own", outs, scratch, lengths, *arrays, flops=FILLS_A_WAIT
    )


def attend_low(lengths, *arrays):
    outs = (shape((HEAD_DIM, EMB), F32), shape((8, EMB), F32), shape((8, 1, PIECE), F32))
    scratch = [BIAS, STATS, ROUNDED, WIDE, pltpu.VMEM((8, EMB), F32)]
    return run(attend_low_kernel, "attend_low", outs, scratch, lengths, *arrays)


def query_inverses(q):
    outs = (shape((128, 128), F32),)
    return run(inverse_kernel, "query_inverses", outs, [], None, q, flops=FILLS_A_WAIT)[0]


def query_units(*arrays):
    outs = (shape((128, EMB), F32),)
    return run(unit_kernel, "query_units", outs, [], None, *arrays, flops=FILLS_A_WAIT)[0]


def contrast(*arrays):
    outs = (shape((NDOC, 128), F32), shape((32, 1, PIECE), F32), shape((8, EMB), F32))
    return run(contrast_kernel, "contrast", outs, [], None, *arrays)


def query_back(*arrays):
    outs = (shape((128, EMB), F32),)
    return run(query_kernel, "query_back", outs, [], None, *arrays, flops=FILLS_A_WAIT)[0]


def back_low(lengths, *arrays):
    outs = (
        shape((TOK, EMB), BF16),
        shape((8, EMB), F32),
        shape((HEAD_DIM, EMB), F32),
        TERMS,
        TERMS,
    )
    return run(back_low_kernel, "back_low", outs, [BIAS, ROUNDED, ROUNDED], lengths, *arrays)


def back_own(lengths, *arrays):
    outs = (shape((TOK, EMB), BF16), TERMS, TERMS)
    return run(back_own_kernel, "back_own", outs, [BIAS, WIDE, ROUNDED, ROUNDED], lengths, *arrays)


def to_all(block, axes, count):
    return lax.all_to_all(jnp.broadcast_to(block[None], (count,) + block.shape), axes, 0, 0)


def swap_cores(block):
    return lax.ppermute(block, "core", [(0, 1), (1, 0)])


def added(blocks):
    total = blocks[0].astype(F32)
    for i in range(1, blocks.shape[0]):
        total = total + blocks[i].astype(F32)
    return total


def pair_terms(d_mine, d_other):
    got = swap_cores(d_other)
    return (d_mine.astype(F32) + got.astype(F32)).astype(BF16)


def per_device(queries_q, keys, values, lengths, query_emb, positive):
    q = queries_q[0]
    kv = jnp.concatenate([keys[0], values[0]], axis=1)
    kv_low = lax.ppermute(kv, "zhi", [(0, 1)])
    own_mine = to_all(kv, "x", 4)
    inverse = query_inverses(query_emb)
    own_mine, inverse = lax.optimization_barrier((own_mine, inverse))
    unit = query_units(query_emb, inverse)
    own_other = swap_cores(own_mine)
    own_att, own_lse = attend_own(lengths, q, own_mine, own_other)
    kv_low, own_att, unit = lax.optimization_barrier((kv_low, own_att, unit))
    low_mine = to_all(kv_low, "x", 4)
    low_other = swap_cores(low_mine)
    att, lse, pieces = attend_low(lengths, q, low_mine, low_other, own_att, own_lse)

    part = added(lax.all_to_all(pieces, NEAR, 0, 0))
    column = to_all(part, ("zlo", "zhi"), 16)
    column = (column[0::2] + column[1::2]).reshape(8, PIECE)
    docs_mine = to_all(column, ("y", "x"), 16).reshape(NDOC, PIECE)
    docs_other = swap_cores(docs_mine)

    coefficient, terms, own_docs = contrast(
        unit, positive.reshape(1, 128), docs_mine, docs_other
    )
    terms = added(lax.all_to_all(terms, ("y", "zlo"), 0, 0))
    upstream = to_all(terms, NEAR, 8)

    out_low, delta, dq_low, d_mine, d_other = back_low(
        lengths, q, low_mine, low_other, att, lse, own_docs, upstream
    )
    paired = pair_terms(d_mine, d_other)
    paired, dq_low = lax.optimization_barrier((paired, dq_low))
    grad_q, own_d_mine, own_d_other = back_own(
        lengths, q, own_mine, own_other, lse, out_low, delta, dq_low
    )
    low_terms = lax.all_to_all(paired, "x", 0, 0)
    low_sum = added(low_terms).astype(BF16)
    own_paired = pair_terms(own_d_mine, own_d_other)
    from_high = lax.ppermute(low_sum, "zhi", [(1, 0)])
    low_sum, own_paired = lax.optimization_barrier((low_sum, own_paired))
    own_terms = lax.all_to_all(own_paired, "x", 0, 0)
    own_sum = added(own_terms)
    coefficient, low_sum = lax.optimization_barrier((coefficient, low_sum))
    query_grad = query_back(unit, inverse, docs_mine, docs_other, coefficient)
    query_grad, from_high = lax.optimization_barrier((query_grad, from_high))
    total = (own_sum + from_high.astype(F32)).astype(BF16)
    return (query_grad, grad_q[None], total[None, :, :KVW], total[None, :, KVW:])


def solution(mesh):
    fine = Mesh(mesh.devices.reshape(8, 4, 2, 4, 2), ("zlo", "y", "zhi", "x", "core"))
    dp, ctx = ("zlo", "y"), ("zhi", "x", "core")
    tokens = P(dp, ctx, None)
    return jax.shard_map(
        per_device,
        mesh=fine,
        in_specs=(tokens, tokens, tokens, P(dp, None), P(dp, None), P(dp)),
        out_specs=(P(dp, None), tokens, tokens, tokens),
        check_vma=False,
    )
```

```python
import jax
import jax.numpy as jnp
from jax import lax
from jax.experimental import pallas as pl
from jax.experimental.pallas import tpu as pltpu
from jax.sharding import Mesh
from jax.sharding import PartitionSpec as P

HEAD_DIM = 128
HEADS = 14
KV_HEADS = 2
PER_GROUP = HEADS // KV_HEADS
DOCS = 4
TOK = 128
SEQ = 2048
EMB = HEADS * HEAD_DIM
KVW = KV_HEADS * HEAD_DIM
GROUP_W = PER_GROUP * TOK
CHUNK = 2 * TOK
HALF = SEQ // 2
CHUNKS = HALF // CHUNK
PIECE = EMB // 2
NDOC = 128

FACTOR = HEAD_DIM ** (-0.5)
INVERSE_TEMPER = 0.05
EPSILON = 1e-06
FULL_ACCURACY = lax.Precision.HIGHEST
MASKED = -1e30
TINY = 1e-30
FILLS_A_WAIT = 10**12
NT = (((1,), (1,)), ((), ()))
TN = (((0,), (0,)), ((), ()))
NN = (((1,), (0,)), ((), ()))
NEAR = ("x", "core")
VMEM_BYTES = 24 * 1024 * 1024


def mm(a, b, dims, precision=None):
    return lax.dot_general(a, b, dims, precision=precision, preferred_element_type=jnp.float32)


def place():
    return tuple(lax.axis_index(axis) for axis in ("zlo", "y", "zhi", "x", "core"))


class Row:
    def __init__(self, lengths):
        _, _, self.high, x, self.core = place()
        self.first = ((self.high * 4 + x) * 2 + self.core) * TOK
        self.lengths = [lengths[0, d] for d in range(DOCS)]
        qpos = self.first + lax.broadcasted_iota(jnp.int32, (1, TOK), 1)
        start = jnp.zeros((1, TOK), jnp.int32)
        doc = jnp.zeros((1, TOK), jnp.int32)
        first_start = jnp.int32(0)
        end = jnp.int32(0)
        for d in range(DOCS - 1):
            end = end + self.lengths[d]
            start = jnp.where(qpos >= end, end, start)
            doc = doc + (qpos >= end).astype(jnp.int32)
            first_start = jnp.where(self.first >= end, end, first_start)
        self.qpos, self.start = qpos, start
        self.member = (lax.broadcasted_iota(jnp.int32, (8, TOK), 0) == doc).astype(jnp.float32)
        own_base = self.high * HALF
        self.own = (
            own_base,
            lax.div(jnp.maximum(first_start - own_base, 0), CHUNK),
            lax.div(self.first + (TOK - 1) - own_base, CHUNK) + 1,
        )
        self.low = (jnp.int32(0), lax.div(first_start, CHUNK), CHUNKS * self.high)

    def length_column(self):
        rows = lax.broadcasted_iota(jnp.int32, (8, 1), 0)
        column = jnp.ones((8, 1), jnp.float32)
        for d in range(DOCS):
            column = jnp.where(rows == d, self.lengths[d].astype(jnp.float32), column)
        return column

    def bias(self, base, chunk):
        at = lax.broadcasted_iota(jnp.int32, (CHUNK, TOK), 0)
        half = lax.div(at, TOK)
        turned = jnp.where(self.core == 1, 1 - half, half)
        pos = base + chunk * CHUNK + turned * TOK + (at - half * TOK)
        allowed = (pos >= self.start) & (pos <= self.qpos)
        return jnp.where(allowed, 0.0, MASKED).astype(jnp.float32)


def chunk_of(kv, chunk, column):
    at = slice(column * HEAD_DIM, (column + 1) * HEAD_DIM)
    return jnp.concatenate([half[chunk, :, at] for half in kv], axis=0)


def put_chunk(refs, chunk, column, rows):
    at = slice(column * HEAD_DIM, (column + 1) * HEAD_DIM)
    refs[0][chunk, :, at] = rows[:TOK]
    refs[1][chunk, :, at] = rows[TOK:]


def fill_bias(row, part, bias):
    base, low, high = part

    def step(chunk, carry):
        bias[chunk] = row.bias(base, chunk)
        return carry

    lax.fori_loop(low, high, step, 0)


def halves(values):
    top = values.astype(jnp.bfloat16)
    return top, (values - top.astype(jnp.float32)).astype(jnp.bfloat16)


def head_rows(ref, group):
    return jnp.concatenate(
        [
            ref[:, (group * PER_GROUP + h) * HEAD_DIM : (group * PER_GROUP + h + 1) * HEAD_DIM]
            for h in range(PER_GROUP)
        ],
        axis=0,
    )


def head(h):
    return slice(h * HEAD_DIM, (h + 1) * HEAD_DIM)


def join_kernel(keys, values, kv):
    kv[:, :KVW] = keys[...]
    kv[:, KVW:] = values[...]


def spread_kernel(kv, spread):
    for i in range(4):
        spread[i] = kv[...]


def part_attention(part, q, kv, bias, stats, weights, out):
    _, low, high = part
    stats[0] = jnp.full((HEADS, TOK), MASKED, jnp.float32)
    stats[1] = jnp.zeros((HEADS, TOK), jnp.float32)
    out[...] = jnp.zeros(out.shape, jnp.float32)

    def step(chunk, carry):
        blocked = bias[chunk]
        for group in range(KV_HEADS):
            k_rows = chunk_of(kv, chunk, group)
            scales = []
            for h in range(group * PER_GROUP, (group + 1) * PER_GROUP):
                scores = mm(k_rows, q[:, head(h)], NT) + blocked
                old = stats[0, h : h + 1]
                top = jnp.maximum(old, jnp.max(scores, axis=0, keepdims=True))
                exps = jnp.exp((scores - top) * FACTOR)
                weights[:, head(h)] = exps.astype(jnp.bfloat16)
                scale = jnp.exp((old - top) * FACTOR)
                stats[0, h : h + 1] = top
                stats[1, h : h + 1] = stats[1, h : h + 1] * scale + jnp.sum(
                    exps, axis=0, keepdims=True
                )
                scales.append(scale)
            columns = slice(group * GROUP_W, (group + 1) * GROUP_W)
            sums = mm(chunk_of(kv, chunk, KV_HEADS + group), weights[:, columns], TN)
            for i in range(PER_GROUP):
                at = head(group * PER_GROUP + i)
                out[:, at] = out[:, at] * scales[i] + sums[:, head(i)]
        return carry

    lax.fori_loop(low, high, step, 0)


def part_result(h, stats):
    total = jnp.maximum(stats[1, h : h + 1], TINY)
    return stats[0, h : h + 1] * FACTOR + jnp.log(total), 1.0 / total


def bias_kernel(lengths, bias):
    row = Row(lengths)
    fill_bias(row, row.own, bias)


def attend_own_kernel(lengths, q, mine, other, bias, att, lse, stats, weights, out):
    row = Row(lengths)
    part_attention(row.own, q, (mine, other), bias, stats, weights, out)
    for h in range(HEADS):
        log_total, inverse = part_result(h, stats)
        att[:, head(h)] = out[:, head(h)] * inverse
        lse[:, head(h)] = jnp.broadcast_to(log_total, (8, TOK))


def attend_low_kernel(
    lengths, q, mine, other, own_att, own_lse, att, lse, pieces, bias, stats, weights, out, doc_sum
):
    row = Row(lengths)
    fill_bias(row, row.low, bias)
    member = jnp.concatenate([row.member, jnp.zeros((TOK - 8, TOK), jnp.float32)], axis=0)
    member = member.astype(jnp.bfloat16)
    part_attention(row.low, q, (mine, other), bias, stats, weights, out)
    for h in range(HEADS):
        at = head(h)
        low_total, inverse = part_result(h, stats)
        own_total = own_lse[0:1, at]
        top = jnp.maximum(low_total, own_total)
        log_total = top + jnp.log(jnp.exp(low_total - top) + jnp.exp(own_total - top))
        own_scale = jnp.exp(own_total - log_total)
        low_scale = jnp.exp(low_total - log_total) * inverse
        lse[:, at] = jnp.broadcast_to(log_total, (8, TOK))
        merged = own_att[:, at] * own_scale + out[:, at] * low_scale
        att[:, at] = merged
        big, small = halves(merged)
        doc_sum[:, at] = (mm(big, member, NT) + mm(small, member, NT)).T[:8]
    mean = doc_sum[...] / row.length_column()
    for d in range(DOCS):
        for c in range(2):
            pieces[2 * d + c] = mean[d : d + 1, c * PIECE : (c + 1) * PIECE]


def inverse_kernel(q, inverse):
    values = q[...].astype(jnp.float32)
    query_inv = lax.rsqrt(jnp.sum(values * values, axis=1, keepdims=True) + EPSILON)
    inverse[...] = jnp.broadcast_to(query_inv, (128, 128))


def unit_kernel(q, inverse, unit):
    unit[...] = q[...].astype(jnp.float32) * inverse[:, :1]


def contrast_kernel(unit, positive, docs_mine, docs_other, coefficient, terms, own_docs):
    z_lo, y, _, x, core = place()
    d_mine, d_other = docs_mine[...], docs_other[...]
    doc_inv = lax.rsqrt(
        jnp.sum(d_mine * d_mine, axis=1, keepdims=True)
        + jnp.sum(d_other * d_other, axis=1, keepdims=True)
        + EPSILON
    )
    q_left, q_right = unit[:, :PIECE], unit[:, PIECE:]
    q_mine = jnp.where(core == 1, q_right, q_left)
    q_other = jnp.where(core == 1, q_left, q_right)
    logits = mm(d_mine * doc_inv, q_mine, NT, FULL_ACCURACY)
    logits = (logits + mm(d_other * doc_inv, q_other, NT, FULL_ACCURACY)) / INVERSE_TEMPER
    exps = jnp.exp(logits)
    at = lax.broadcasted_iota(jnp.int32, (NDOC, 128), 0)
    doc = ((at % 8) * 4 + at // 32) * DOCS + (at // 8) % 4
    target = (doc == positive[...]).astype(jnp.float32)
    coefficient[...] = exps / jnp.sum(exps, axis=0, keepdims=True) - target
    near = jnp.concatenate(
        [coefficient[pl.ds(pl.multiple_of(b * 32 + x * 8, 8), 8), :] for b in range(4)], axis=0
    )
    near_terms = mm(near, q_mine, NN, FULL_ACCURACY) / INVERSE_TEMPER
    for r in range(32):
        terms[r] = near_terms[r : r + 1]
    own_docs[...] = jnp.zeros((8, EMB), jnp.float32)
    for d in range(DOCS):
        r = y * 32 + d * 8 + z_lo
        a, b = docs_mine[pl.ds(r, 1), :], docs_other[pl.ds(r, 1), :]
        own_docs[d : d + 1, :PIECE] = jnp.where(core == 1, b, a)
        own_docs[d : d + 1, PIECE:] = jnp.where(core == 1, a, b)


def query_kernel(unit, inverse, docs_mine, docs_other, coefficient, query_grad):
    _, _, _, _, core = place()
    d_mine, d_other = docs_mine[...], docs_other[...]
    doc_inv = lax.rsqrt(
        jnp.sum(d_mine * d_mine, axis=1, keepdims=True)
        + jnp.sum(d_other * d_other, axis=1, keepdims=True)
        + EPSILON
    )
    scaled = coefficient[...] * doc_inv
    u_mine = mm(scaled, d_mine, TN, FULL_ACCURACY) / INVERSE_TEMPER
    u_other = mm(scaled, d_other, TN, FULL_ACCURACY) / INVERSE_TEMPER
    u_left = jnp.where(core == 1, u_other, u_mine)
    u_right = jnp.where(core == 1, u_mine, u_other)
    query_inv = inverse[:, :1]
    q_left, q_right = unit[:, :PIECE], unit[:, PIECE:]
    inner = jnp.sum(q_left * u_left, axis=1, keepdims=True) + jnp.sum(
        q_right * u_right, axis=1, keepdims=True
    )
    query_grad[:, :PIECE] = query_inv * (u_left - q_left * inner)
    query_grad[:, PIECE:] = query_inv * (u_right - q_right * inner)


def back_part(part, q, kv, bias, lse, out_low, delta, dq, d_kv, grads, weights):
    _, low, high = part

    def step(chunk, carry):
        blocked = bias[chunk]
        for group in range(KV_HEADS):
            k_rows = chunk_of(kv, chunk, group)
            v_rows = chunk_of(kv, chunk, KV_HEADS + group)
            for h in range(group * PER_GROUP, (group + 1) * PER_GROUP):
                at = head(h)
                scores = mm(k_rows, q[:, at], NT) * FACTOR + blocked
                probs = jnp.exp(scores - lse[0:1, at])
                flow = mm(v_rows, out_low[:, at], NT)
                grads[:, at] = (probs * (flow - delta[0:1, at])).astype(jnp.bfloat16)
                weights[:, at] = probs.astype(jnp.bfloat16)
            columns = slice(group * GROUP_W, (group + 1) * GROUP_W)
            score_grad = grads[:, columns]
            dq[:, columns] += mm(k_rows, score_grad, TN)
            k_part = mm(score_grad, head_rows(q, group), NN) * FACTOR
            v_part = mm(weights[:, columns], head_rows(out_low, group), NN)
            put_chunk(d_kv, chunk, group, k_part.astype(jnp.bfloat16))
            put_chunk(d_kv, chunk, KV_HEADS + group, v_part.astype(jnp.bfloat16))
        return carry

    lax.fori_loop(low, high, step, 0)


def back_low_kernel(
    lengths,
    q,
    mine,
    other,
    att,
    lse,
    own_docs,
    upstream,
    out_low,
    delta,
    dq_low,
    d_mine,
    d_other,
    bias,
    grads,
    weights,
):
    row = Row(lengths)
    d_mine[...] = jnp.zeros(d_mine.shape, d_mine.dtype)
    d_other[...] = jnp.zeros(d_other.shape, d_other.dtype)
    fill_bias(row, row.low, bias)
    w = jnp.concatenate(
        [
            jnp.concatenate([upstream[2 * d + c] for d in range(DOCS)] * 2, axis=0)
            for c in range(2)
        ],
        axis=1,
    )
    docs = own_docs[...]
    doc_inv = lax.rsqrt(jnp.sum(docs * docs, axis=1, keepdims=True) + EPSILON)
    unit = docs * doc_inv
    inner = jnp.sum(unit * w, axis=1, keepdims=True)
    doc_grad = doc_inv * (w - unit * inner) / row.length_column()
    big, small = halves(doc_grad)
    member = row.member.astype(jnp.bfloat16)
    out_low[...] = mm(member, big, TN).astype(jnp.bfloat16)
    both = jnp.concatenate([big, small], axis=0)
    twice = jnp.concatenate([member, member], axis=0)
    for h in range(HEADS):
        at = head(h)
        one = jnp.sum(mm(both[:, at], twice, TN) * att[:, at], axis=0, keepdims=True)
        delta[:, at] = jnp.broadcast_to(one, (8, TOK))
    dq_low[...] = jnp.zeros(dq_low.shape, jnp.float32)
    kv, d_kv = (mine, other), (d_mine, d_other)
    back_part(row.low, q, kv, bias, lse, out_low, delta, dq_low, d_kv, grads, weights)


def back_own_kernel(
    lengths,
    q,
    mine,
    other,
    lse,
    out_low,
    delta,
    dq_low,
    grad_q,
    d_mine,
    d_other,
    bias,
    dq,
    grads,
    weights,
):
    row = Row(lengths)
    d_mine[...] = jnp.zeros(d_mine.shape, d_mine.dtype)
    d_other[...] = jnp.zeros(d_other.shape, d_other.dtype)
    fill_bias(row, row.own, bias)
    dq[...] = dq_low[...]
    kv, d_kv = (mine, other), (d_mine, d_other)
    back_part(row.own, q, kv, bias, lse, out_low, delta, dq, d_kv, grads, weights)
    for h in range(HEADS):
        grad_q[:, head(h)] = (dq[:, head(h)].T * FACTOR).astype(jnp.bfloat16)


F32, BF16 = jnp.float32, jnp.bfloat16


def shape(dims, dtype):
    return jax.ShapeDtypeStruct(dims, dtype)


def run(kernel, name, outs, scratch, lengths, *arrays, flops=0):
    vmem = pl.BlockSpec(memory_space=pltpu.VMEM)
    smem = pl.BlockSpec(memory_space=pltpu.SMEM)
    first = () if lengths is None else (lengths,)
    return pl.pallas_call(
        kernel,
        out_shape=outs,
        in_specs=[smem] * len(first) + [vmem] * len(arrays),
        out_specs=tuple(vmem for _ in outs),
        scratch_shapes=scratch,
        compiler_params=pltpu.CompilerParams(vmem_limit_bytes=VMEM_BYTES),
        cost_estimate=pl.CostEstimate(flops=flops, bytes_accessed=0, transcendentals=0),
        name=name,
    )(*first, *arrays)


TERMS = shape((CHUNKS, TOK, 2 * KVW), BF16)
WIDE = pltpu.VMEM((HEAD_DIM, EMB), F32)
BIAS = pltpu.VMEM((CHUNKS, CHUNK, TOK), F32)
STATS = pltpu.VMEM((2, HEADS, TOK), F32)
ROUNDED = pltpu.VMEM((CHUNK, EMB), BF16)


def join(*arrays):
    return run(join_kernel, "join", (shape((TOK, 2 * KVW), BF16),), [], None, *arrays)[0]


def spread(kv):
    return run(spread_kernel, "spread", (shape((4, TOK, 2 * KVW), BF16),), [], None, kv)[0]


def near_bias(lengths):
    outs = (shape((CHUNKS, CHUNK, TOK), F32),)
    return run(bias_kernel, "near_bias", outs, [], lengths, flops=FILLS_A_WAIT)[0]


def attend_own(lengths, *arrays):
    outs = (shape((HEAD_DIM, EMB), F32), shape((8, EMB), F32))
    scratch = [STATS, ROUNDED, WIDE]
    return run(
        attend_own_kernel, "attend_own", outs, scratch, lengths, *arrays, flops=FILLS_A_WAIT
    )


def attend_low(lengths, *arrays):
    outs = (shape((HEAD_DIM, EMB), F32), shape((8, EMB), F32), shape((8, 1, PIECE), F32))
    scratch = [BIAS, STATS, ROUNDED, WIDE, pltpu.VMEM((8, EMB), F32)]
    return run(attend_low_kernel, "attend_low", outs, scratch, lengths, *arrays)


def query_inverses(q):
    outs = (shape((128, 128), F32),)
    return run(inverse_kernel, "query_inverses", outs, [], None, q, flops=FILLS_A_WAIT)[0]


def query_units(*arrays):
    outs = (shape((128, EMB), F32),)
    return run(unit_kernel, "query_units", outs, [], None, *arrays, flops=FILLS_A_WAIT)[0]


def contrast(*arrays):
    outs = (shape((NDOC, 128), F32), shape((32, 1, PIECE), F32), shape((8, EMB), F32))
    return run(contrast_kernel, "contrast", outs, [], None, *arrays)


def query_back(*arrays):
    outs = (shape((128, EMB), F32),)
    return run(query_kernel, "query_back", outs, [], None, *arrays, flops=FILLS_A_WAIT)[0]


def back_low(lengths, *arrays):
    outs = (
        shape((TOK, EMB), BF16),
        shape((8, EMB), F32),
        shape((HEAD_DIM, EMB), F32),
        TERMS,
        TERMS,
    )
    return run(back_low_kernel, "back_low", outs, [BIAS, ROUNDED, ROUNDED], lengths, *arrays)


def back_own(lengths, *arrays):
    outs = (shape((TOK, EMB), BF16), TERMS, TERMS)
    return run(back_own_kernel, "back_own", outs, [BIAS, WIDE, ROUNDED, ROUNDED], lengths, *arrays)


def to_all(block, axes, count):
    return lax.all_to_all(jnp.broadcast_to(block[None], (count,) + block.shape), axes, 0, 0)


def swap_cores(block):
    return lax.ppermute(block, "core", [(0, 1), (1, 0)])


def added(blocks):
    total = blocks[0].astype(F32)
    for i in range(1, blocks.shape[0]):
        total = total + blocks[i].astype(F32)
    return total


def pair_terms(d_mine, d_other):
    got = swap_cores(d_other)
    return (d_mine.astype(F32) + got.astype(F32)).astype(BF16)


def per_device(queries_q, keys, values, lengths, query_emb, positive):
    q = queries_q[0]
    kv = join(keys[0], values[0])
    kv_low = lax.ppermute(kv, "zhi", [(0, 1)])
    own_mine = lax.all_to_all(spread(kv), "x", 0, 0)
    inverse = query_inverses(query_emb)
    own_mine, inverse, after = lax.optimization_barrier((own_mine, inverse, lengths))
    own_other = swap_cores(own_mine)
    own_bias = near_bias(after)
    own_other, inverse, own_bias = lax.optimization_barrier((own_other, inverse, own_bias))
    unit = query_units(query_emb, inverse)
    kv_low, own_other, unit = lax.optimization_barrier((kv_low, own_other, unit))
    own_att, own_lse = attend_own(lengths, q, own_mine, own_other, own_bias)
    low_mine = lax.all_to_all(spread(kv_low), "x", 0, 0)
    low_mine, own_att = lax.optimization_barrier((low_mine, own_att))
    low_other = swap_cores(low_mine)
    att, lse, pieces = attend_low(lengths, q, low_mine, low_other, own_att, own_lse)

    part = added(lax.all_to_all(pieces, NEAR, 0, 0))
    column = to_all(part, ("zlo", "zhi"), 16)
    column = (column[0::2] + column[1::2]).reshape(8, PIECE)
    docs_mine = to_all(column, ("y", "x"), 16).reshape(NDOC, PIECE)
    docs_other = swap_cores(docs_mine)

    coefficient, terms, own_docs = contrast(
        unit, positive.reshape(1, 128), docs_mine, docs_other
    )
    terms = added(lax.all_to_all(terms, ("y", "zlo"), 0, 0))
    upstream = to_all(terms, NEAR, 8)

    out_low, delta, dq_low, d_mine, d_other = back_low(
        lengths, q, low_mine, low_other, att, lse, own_docs, upstream
    )
    paired = pair_terms(d_mine, d_other)
    paired, dq_low = lax.optimization_barrier((paired, dq_low))
    grad_q, own_d_mine, own_d_other = back_own(
        lengths, q, own_mine, own_other, lse, out_low, delta, dq_low
    )
    low_terms = lax.all_to_all(paired, "x", 0, 0)
    low_sum = added(low_terms).astype(BF16)
    own_paired = pair_terms(own_d_mine, own_d_other)
    from_high = lax.ppermute(low_sum, "zhi", [(1, 0)])
    low_sum, own_paired = lax.optimization_barrier((low_sum, own_paired))
    own_terms = lax.all_to_all(own_paired, "x", 0, 0)
    own_sum = added(own_terms)
    coefficient, low_sum = lax.optimization_barrier((coefficient, low_sum))
    query_grad = query_back(unit, inverse, docs_mine, docs_other, coefficient)
    query_grad, from_high = lax.optimization_barrier((query_grad, from_high))
    grad_k = (own_sum[:, :KVW] + from_high[:, :KVW].astype(F32)).astype(BF16)
    grad_v = (own_sum[:, KVW:] + from_high[:, KVW:].astype(F32)).astype(BF16)
    return (query_grad, grad_q[None], grad_k[None], grad_v[None])


def solution(mesh):
    fine = Mesh(mesh.devices.reshape(8, 4, 2, 4, 2), ("zlo", "y", "zhi", "x", "core"))
    dp, ctx = ("zlo", "y"), ("zhi", "x", "core")
    tokens = P(dp, ctx, None)
    return jax.shard_map(
        per_device,
        mesh=fine,
        in_specs=(tokens, tokens, tokens, P(dp, None), P(dp, None), P(dp)),
        out_specs=(P(dp, None), tokens, tokens, tokens),
        check_vma=False,
    )
```

```python
import jax
import jax.numpy as jnp
from jax import lax
from jax.experimental import pallas as pl
from jax.experimental.pallas import tpu as pltpu
from jax.sharding import Mesh
from jax.sharding import PartitionSpec as P

HEAD_DIM = 128
HEADS = 14
KV_HEADS = 2
PER_GROUP = HEADS // KV_HEADS
DOCS = 4
TOK = 128
SEQ = 2048
EMB = HEADS * HEAD_DIM
KVW = KV_HEADS * HEAD_DIM
GROUP_W = PER_GROUP * TOK
CHUNK = 2 * TOK
HALF = SEQ // 2
CHUNKS = HALF // CHUNK
PIECE = EMB // 2
NDOC = 128

FACTOR = HEAD_DIM ** (-0.5)
INVERSE_TEMPER = 0.05
EPSILON = 1e-06
FULL_ACCURACY = lax.Precision.HIGHEST
MASKED = -1e30
TINY = 1e-30
FILLS_A_WAIT = 10**12
NT = (((1,), (1,)), ((), ()))
TN = (((0,), (0,)), ((), ()))
NN = (((1,), (0,)), ((), ()))
NEAR = ("x", "core")
VMEM_BYTES = 24 * 1024 * 1024


def mm(a, b, dims, precision=None):
    return lax.dot_general(a, b, dims, precision=precision, preferred_element_type=jnp.float32)


def place():
    return tuple(lax.axis_index(axis) for axis in ("zlo", "y", "zhi", "x", "core"))


class Row:
    def __init__(self, lengths):
        _, _, self.high, x, self.core = place()
        self.first = ((self.high * 4 + x) * 2 + self.core) * TOK
        self.lengths = [lengths[0, d] for d in range(DOCS)]
        qpos = self.first + lax.broadcasted_iota(jnp.int32, (1, TOK), 1)
        start = jnp.zeros((1, TOK), jnp.int32)
        doc = jnp.zeros((1, TOK), jnp.int32)
        first_start = jnp.int32(0)
        end = jnp.int32(0)
        for d in range(DOCS - 1):
            end = end + self.lengths[d]
            start = jnp.where(qpos >= end, end, start)
            doc = doc + (qpos >= end).astype(jnp.int32)
            first_start = jnp.where(self.first >= end, end, first_start)
        self.qpos, self.start = qpos, start
        self.member = (lax.broadcasted_iota(jnp.int32, (8, TOK), 0) == doc).astype(jnp.float32)
        own_base = self.high * HALF
        self.own = (
            own_base,
            lax.div(jnp.maximum(first_start - own_base, 0), CHUNK),
            lax.div(self.first + (TOK - 1) - own_base, CHUNK) + 1,
        )
        self.low = (jnp.int32(0), lax.div(first_start, CHUNK), CHUNKS * self.high)

    def length_column(self):
        rows = lax.broadcasted_iota(jnp.int32, (8, 1), 0)
        column = jnp.ones((8, 1), jnp.float32)
        for d in range(DOCS):
            column = jnp.where(rows == d, self.lengths[d].astype(jnp.float32), column)
        return column

    def bias(self, base, chunk):
        at = lax.broadcasted_iota(jnp.int32, (CHUNK, TOK), 0)
        half = lax.div(at, TOK)
        turned = jnp.where(self.core == 1, 1 - half, half)
        pos = base + chunk * CHUNK + turned * TOK + (at - half * TOK)
        allowed = (pos >= self.start) & (pos <= self.qpos)
        return jnp.where(allowed, 0.0, MASKED).astype(jnp.float32)


def chunk_of(kv, chunk, column):
    at = slice(column * HEAD_DIM, (column + 1) * HEAD_DIM)
    return jnp.concatenate([half[chunk, :, at] for half in kv], axis=0)


def put_chunk(refs, chunk, column, rows):
    at = slice(column * HEAD_DIM, (column + 1) * HEAD_DIM)
    refs[0][chunk, :, at] = rows[:TOK]
    refs[1][chunk, :, at] = rows[TOK:]


def fill_bias(row, part, bias):
    base, low, high = part

    def step(chunk, carry):
        bias[chunk] = row.bias(base, chunk)
        return carry

    lax.fori_loop(low, high, step, 0)


def halves(values):
    top = values.astype(jnp.bfloat16)
    return top, (values - top.astype(jnp.float32)).astype(jnp.bfloat16)


def head_rows(ref, group):
    return jnp.concatenate(
        [
            ref[:, (group * PER_GROUP + h) * HEAD_DIM : (group * PER_GROUP + h + 1) * HEAD_DIM]
            for h in range(PER_GROUP)
        ],
        axis=0,
    )


def head(h):
    return slice(h * HEAD_DIM, (h + 1) * HEAD_DIM)


def part_attention(part, q, kv, bias, stats, weights, out):
    _, low, high = part
    stats[0] = jnp.full((HEADS, TOK), MASKED, jnp.float32)
    stats[1] = jnp.zeros((HEADS, TOK), jnp.float32)
    out[...] = jnp.zeros(out.shape, jnp.float32)

    def step(chunk, carry):
        blocked = bias[chunk]
        for group in range(KV_HEADS):
            k_rows = chunk_of(kv, chunk, group)
            scales = []
            for h in range(group * PER_GROUP, (group + 1) * PER_GROUP):
                scores = mm(k_rows, q[:, head(h)], NT) + blocked
                old = stats[0, h : h + 1]
                top = jnp.maximum(old, jnp.max(scores, axis=0, keepdims=True))
                exps = jnp.exp((scores - top) * FACTOR)
                weights[:, head(h)] = exps.astype(jnp.bfloat16)
                scale = jnp.exp((old - top) * FACTOR)
                stats[0, h : h + 1] = top
                stats[1, h : h + 1] = stats[1, h : h + 1] * scale + jnp.sum(
                    exps, axis=0, keepdims=True
                )
                scales.append(scale)
            columns = slice(group * GROUP_W, (group + 1) * GROUP_W)
            sums = mm(chunk_of(kv, chunk, KV_HEADS + group), weights[:, columns], TN)
            for i in range(PER_GROUP):
                at = head(group * PER_GROUP + i)
                out[:, at] = out[:, at] * scales[i] + sums[:, head(i)]
        return carry

    lax.fori_loop(low, high, step, 0)


def part_result(h, stats):
    total = jnp.maximum(stats[1, h : h + 1], TINY)
    return stats[0, h : h + 1] * FACTOR + jnp.log(total), 1.0 / total


def bias_kernel(lengths, bias):
    row = Row(lengths)
    fill_bias(row, row.own, bias)


def attend_own_kernel(lengths, q, mine, other, bias, att, lse, stats, weights, out):
    row = Row(lengths)
    part_attention(row.own, q, (mine, other), bias, stats, weights, out)
    for h in range(HEADS):
        log_total, inverse = part_result(h, stats)
        att[:, head(h)] = out[:, head(h)] * inverse
        lse[:, head(h)] = jnp.broadcast_to(log_total, (8, TOK))


def attend_low_kernel(
    lengths, q, mine, other, own_att, own_lse, att, lse, pieces, bias, stats, weights, out, doc_sum
):
    row = Row(lengths)
    fill_bias(row, row.low, bias)
    member = jnp.concatenate([row.member, jnp.zeros((TOK - 8, TOK), jnp.float32)], axis=0)
    member = member.astype(jnp.bfloat16)
    part_attention(row.low, q, (mine, other), bias, stats, weights, out)
    for h in range(HEADS):
        at = head(h)
        low_total, inverse = part_result(h, stats)
        own_total = own_lse[0:1, at]
        top = jnp.maximum(low_total, own_total)
        log_total = top + jnp.log(jnp.exp(low_total - top) + jnp.exp(own_total - top))
        own_scale = jnp.exp(own_total - log_total)
        low_scale = jnp.exp(low_total - log_total) * inverse
        lse[:, at] = jnp.broadcast_to(log_total, (8, TOK))
        merged = own_att[:, at] * own_scale + out[:, at] * low_scale
        att[:, at] = merged
        big, small = halves(merged)
        doc_sum[:, at] = (mm(big, member, NT) + mm(small, member, NT)).T[:8]
    mean = doc_sum[...] / row.length_column()
    for d in range(DOCS):
        for c in range(2):
            pieces[2 * d + c] = mean[d : d + 1, c * PIECE : (c + 1) * PIECE]


def inverse_kernel(q, inverse):
    values = q[...].astype(jnp.float32)
    query_inv = lax.rsqrt(jnp.sum(values * values, axis=1, keepdims=True) + EPSILON)
    inverse[...] = jnp.broadcast_to(query_inv, (128, 128))


def unit_kernel(q, inverse, unit):
    unit[...] = q[...].astype(jnp.float32) * inverse[:, :1]


def contrast_kernel(unit, positive, docs_mine, docs_other, coefficient, terms, own_docs):
    z_lo, y, _, x, core = place()
    d_mine, d_other = docs_mine[...], docs_other[...]
    doc_inv = lax.rsqrt(
        jnp.sum(d_mine * d_mine, axis=1, keepdims=True)
        + jnp.sum(d_other * d_other, axis=1, keepdims=True)
        + EPSILON
    )
    q_left, q_right = unit[:, :PIECE], unit[:, PIECE:]
    q_mine = jnp.where(core == 1, q_right, q_left)
    q_other = jnp.where(core == 1, q_left, q_right)
    logits = mm(d_mine * doc_inv, q_mine, NT, FULL_ACCURACY)
    logits = (logits + mm(d_other * doc_inv, q_other, NT, FULL_ACCURACY)) / INVERSE_TEMPER
    exps = jnp.exp(logits)
    at = lax.broadcasted_iota(jnp.int32, (NDOC, 128), 0)
    doc = ((at % 8) * 4 + at // 32) * DOCS + (at // 8) % 4
    target = (doc == positive[...]).astype(jnp.float32)
    coefficient[...] = exps / jnp.sum(exps, axis=0, keepdims=True) - target
    near = jnp.concatenate(
        [coefficient[pl.ds(pl.multiple_of(b * 32 + x * 8, 8), 8), :] for b in range(4)], axis=0
    )
    near_terms = mm(near, q_mine, NN, FULL_ACCURACY) / INVERSE_TEMPER
    for r in range(32):
        terms[r] = near_terms[r : r + 1]
    own_docs[...] = jnp.zeros((8, EMB), jnp.float32)
    for d in range(DOCS):
        r = y * 32 + d * 8 + z_lo
        a, b = docs_mine[pl.ds(r, 1), :], docs_other[pl.ds(r, 1), :]
        own_docs[d : d + 1, :PIECE] = jnp.where(core == 1, b, a)
        own_docs[d : d + 1, PIECE:] = jnp.where(core == 1, a, b)


def query_kernel(unit, inverse, docs_mine, docs_other, coefficient, query_grad):
    _, _, _, _, core = place()
    d_mine, d_other = docs_mine[...], docs_other[...]
    doc_inv = lax.rsqrt(
        jnp.sum(d_mine * d_mine, axis=1, keepdims=True)
        + jnp.sum(d_other * d_other, axis=1, keepdims=True)
        + EPSILON
    )
    scaled = coefficient[...] * doc_inv
    u_mine = mm(scaled, d_mine, TN, FULL_ACCURACY) / INVERSE_TEMPER
    u_other = mm(scaled, d_other, TN, FULL_ACCURACY) / INVERSE_TEMPER
    u_left = jnp.where(core == 1, u_other, u_mine)
    u_right = jnp.where(core == 1, u_mine, u_other)
    query_inv = inverse[:, :1]
    q_left, q_right = unit[:, :PIECE], unit[:, PIECE:]
    inner = jnp.sum(q_left * u_left, axis=1, keepdims=True) + jnp.sum(
        q_right * u_right, axis=1, keepdims=True
    )
    query_grad[:, :PIECE] = query_inv * (u_left - q_left * inner)
    query_grad[:, PIECE:] = query_inv * (u_right - q_right * inner)


def back_part(part, q, kv, bias, lse, out_low, delta, dq, d_kv, grads, weights):
    _, low, high = part

    def step(chunk, carry):
        blocked = bias[chunk]
        for group in range(KV_HEADS):
            k_rows = chunk_of(kv, chunk, group)
            v_rows = chunk_of(kv, chunk, KV_HEADS + group)
            for h in range(group * PER_GROUP, (group + 1) * PER_GROUP):
                at = head(h)
                scores = mm(k_rows, q[:, at], NT) * FACTOR + blocked
                probs = jnp.exp(scores - lse[0:1, at])
                flow = mm(v_rows, out_low[:, at], NT)
                grads[:, at] = (probs * (flow - delta[0:1, at])).astype(jnp.bfloat16)
                weights[:, at] = probs.astype(jnp.bfloat16)
            columns = slice(group * GROUP_W, (group + 1) * GROUP_W)
            score_grad = grads[:, columns]
            dq[:, columns] += mm(k_rows, score_grad, TN)
            k_part = mm(score_grad, head_rows(q, group), NN) * FACTOR
            v_part = mm(weights[:, columns], head_rows(out_low, group), NN)
            put_chunk(d_kv, chunk, group, k_part.astype(jnp.bfloat16))
            put_chunk(d_kv, chunk, KV_HEADS + group, v_part.astype(jnp.bfloat16))
        return carry

    lax.fori_loop(low, high, step, 0)


def back_low_kernel(
    lengths,
    q,
    mine,
    other,
    att,
    lse,
    own_docs,
    upstream,
    out_low,
    delta,
    dq_low,
    d_mine,
    d_other,
    bias,
    grads,
    weights,
):
    row = Row(lengths)
    d_mine[...] = jnp.zeros(d_mine.shape, d_mine.dtype)
    d_other[...] = jnp.zeros(d_other.shape, d_other.dtype)
    fill_bias(row, row.low, bias)
    w = jnp.concatenate(
        [
            jnp.concatenate([upstream[2 * d + c] for d in range(DOCS)] * 2, axis=0)
            for c in range(2)
        ],
        axis=1,
    )
    docs = own_docs[...]
    doc_inv = lax.rsqrt(jnp.sum(docs * docs, axis=1, keepdims=True) + EPSILON)
    unit = docs * doc_inv
    inner = jnp.sum(unit * w, axis=1, keepdims=True)
    doc_grad = doc_inv * (w - unit * inner) / row.length_column()
    big, small = halves(doc_grad)
    member = row.member.astype(jnp.bfloat16)
    out_low[...] = mm(member, big, TN).astype(jnp.bfloat16)
    both = jnp.concatenate([big, small], axis=0)
    twice = jnp.concatenate([member, member], axis=0)
    for h in range(HEADS):
        at = head(h)
        one = jnp.sum(mm(both[:, at], twice, TN) * att[:, at], axis=0, keepdims=True)
        delta[:, at] = jnp.broadcast_to(one, (8, TOK))
    dq_low[...] = jnp.zeros(dq_low.shape, jnp.float32)
    kv, d_kv = (mine, other), (d_mine, d_other)
    back_part(row.low, q, kv, bias, lse, out_low, delta, dq_low, d_kv, grads, weights)


def back_own_kernel(
    lengths,
    q,
    mine,
    other,
    lse,
    out_low,
    delta,
    dq_low,
    grad_q,
    d_mine,
    d_other,
    bias,
    dq,
    grads,
    weights,
):
    row = Row(lengths)
    d_mine[...] = jnp.zeros(d_mine.shape, d_mine.dtype)
    d_other[...] = jnp.zeros(d_other.shape, d_other.dtype)
    fill_bias(row, row.own, bias)
    dq[...] = dq_low[...]
    kv, d_kv = (mine, other), (d_mine, d_other)
    back_part(row.own, q, kv, bias, lse, out_low, delta, dq, d_kv, grads, weights)
    for h in range(HEADS):
        grad_q[:, head(h)] = (dq[:, head(h)].T * FACTOR).astype(jnp.bfloat16)


def total_kernel(terms, total):
    total[...] = added(terms)


def finish_kernel(near, far, grad_k, grad_v):
    total = (near[...] + far[...].astype(jnp.float32)).astype(jnp.bfloat16)
    grad_k[...] = total[:, :KVW]
    grad_v[...] = total[:, KVW:]


F32, BF16 = jnp.float32, jnp.bfloat16


def shape(dims, dtype):
    return jax.ShapeDtypeStruct(dims, dtype)


def run(kernel, name, outs, scratch, lengths, *arrays, flops=0):
    vmem = pl.BlockSpec(memory_space=pltpu.VMEM)
    smem = pl.BlockSpec(memory_space=pltpu.SMEM)
    first = () if lengths is None else (lengths,)
    return pl.pallas_call(
        kernel,
        out_shape=outs,
        in_specs=[smem] * len(first) + [vmem] * len(arrays),
        out_specs=tuple(vmem for _ in outs),
        scratch_shapes=scratch,
        compiler_params=pltpu.CompilerParams(vmem_limit_bytes=VMEM_BYTES),
        cost_estimate=pl.CostEstimate(flops=flops, bytes_accessed=0, transcendentals=0),
        name=name,
    )(*first, *arrays)


TERMS = shape((CHUNKS, TOK, 2 * KVW), BF16)
WIDE = pltpu.VMEM((HEAD_DIM, EMB), F32)
BIAS = pltpu.VMEM((CHUNKS, CHUNK, TOK), F32)
STATS = pltpu.VMEM((2, HEADS, TOK), F32)
ROUNDED = pltpu.VMEM((CHUNK, EMB), BF16)


def near_bias(lengths):
    outs = (shape((CHUNKS, CHUNK, TOK), F32),)
    return run(bias_kernel, "near_bias", outs, [], lengths, flops=FILLS_A_WAIT)[0]


def attend_own(lengths, *arrays):
    outs = (shape((HEAD_DIM, EMB), F32), shape((8, EMB), F32))
    scratch = [STATS, ROUNDED, WIDE]
    return run(
        attend_own_kernel, "attend_own", outs, scratch, lengths, *arrays, flops=FILLS_A_WAIT
    )


def attend_low(lengths, *arrays):
    outs = (shape((HEAD_DIM, EMB), F32), shape((8, EMB), F32), shape((8, 1, PIECE), F32))
    scratch = [BIAS, STATS, ROUNDED, WIDE, pltpu.VMEM((8, EMB), F32)]
    return run(attend_low_kernel, "attend_low", outs, scratch, lengths, *arrays)


def query_inverses(q):
    outs = (shape((128, 128), F32),)
    return run(inverse_kernel, "query_inverses", outs, [], None, q, flops=FILLS_A_WAIT)[0]


def query_units(*arrays):
    outs = (shape((128, EMB), F32),)
    return run(unit_kernel, "query_units", outs, [], None, *arrays, flops=FILLS_A_WAIT)[0]


def contrast(*arrays):
    outs = (shape((NDOC, 128), F32), shape((32, 1, PIECE), F32), shape((8, EMB), F32))
    return run(contrast_kernel, "contrast", outs, [], None, *arrays)


def query_back(*arrays):
    outs = (shape((128, EMB), F32),)
    return run(query_kernel, "query_back", outs, [], None, *arrays, flops=FILLS_A_WAIT)[0]


def total_of(terms):
    outs = (shape((TOK, 2 * KVW), F32),)
    return run(total_kernel, "total_of", outs, [], None, terms)[0]


def finish(*arrays):
    outs = (shape((TOK, KVW), BF16), shape((TOK, KVW), BF16))
    return run(finish_kernel, "finish", outs, [], None, *arrays)


def back_low(lengths, *arrays):
    outs = (
        shape((TOK, EMB), BF16),
        shape((8, EMB), F32),
        shape((HEAD_DIM, EMB), F32),
        TERMS,
        TERMS,
    )
    return run(back_low_kernel, "back_low", outs, [BIAS, ROUNDED, ROUNDED], lengths, *arrays)


def back_own(lengths, *arrays):
    outs = (shape((TOK, EMB), BF16), TERMS, TERMS)
    return run(back_own_kernel, "back_own", outs, [BIAS, WIDE, ROUNDED, ROUNDED], lengths, *arrays)


def to_all(block, axes, count):
    return lax.all_to_all(jnp.broadcast_to(block[None], (count,) + block.shape), axes, 0, 0)


def swap_cores(block):
    return lax.ppermute(block, "core", [(0, 1), (1, 0)])


def added(blocks):
    total = blocks[0].astype(F32)
    for i in range(1, blocks.shape[0]):
        total = total + blocks[i].astype(F32)
    return total


def pair_terms(d_mine, d_other):
    got = swap_cores(d_other)
    return (d_mine.astype(F32) + got.astype(F32)).astype(BF16)


def per_device(queries_q, keys, values, lengths, query_emb, positive):
    q = queries_q[0]
    kv = jnp.concatenate([keys[0], values[0]], axis=1)
    kv_low = lax.ppermute(kv, "zhi", [(0, 1)])
    own_mine = to_all(kv, "x", 4)
    inverse = query_inverses(query_emb)
    own_mine, inverse, after = lax.optimization_barrier((own_mine, inverse, lengths))
    own_other = swap_cores(own_mine)
    own_bias = near_bias(after)
    own_other, inverse, own_bias = lax.optimization_barrier((own_other, inverse, own_bias))
    unit = query_units(query_emb, inverse)
    kv_low, own_other, unit = lax.optimization_barrier((kv_low, own_other, unit))
    own_att, own_lse = attend_own(lengths, q, own_mine, own_other, own_bias)
    low_mine = to_all(kv_low, "x", 4)
    low_mine, own_att = lax.optimization_barrier((low_mine, own_att))
    low_other = swap_cores(low_mine)
    att, lse, pieces = attend_low(lengths, q, low_mine, low_other, own_att, own_lse)

    part = added(lax.all_to_all(pieces, NEAR, 0, 0))
    column = to_all(part, ("zlo", "zhi"), 16)
    column = (column[0::2] + column[1::2]).reshape(8, PIECE)
    docs_mine = to_all(column, ("y", "x"), 16).reshape(NDOC, PIECE)
    docs_other = swap_cores(docs_mine)

    coefficient, terms, own_docs = contrast(
        unit, positive.reshape(1, 128), docs_mine, docs_other
    )
    terms = added(lax.all_to_all(terms, ("y", "zlo"), 0, 0))
    upstream = to_all(terms, NEAR, 8)

    out_low, delta, dq_low, d_mine, d_other = back_low(
        lengths, q, low_mine, low_other, att, lse, own_docs, upstream
    )
    paired = pair_terms(d_mine, d_other)
    paired, dq_low = lax.optimization_barrier((paired, dq_low))
    grad_q, own_d_mine, own_d_other = back_own(
        lengths, q, own_mine, own_other, lse, out_low, delta, dq_low
    )
    low_terms = lax.all_to_all(paired, "x", 0, 0)
    low_sum = added(low_terms).astype(BF16)
    own_paired = pair_terms(own_d_mine, own_d_other)
    from_high = lax.ppermute(low_sum, "zhi", [(1, 0)])
    low_sum, own_paired = lax.optimization_barrier((low_sum, own_paired))
    own_terms = lax.all_to_all(own_paired, "x", 0, 0)
    coefficient, low_sum = lax.optimization_barrier((coefficient, low_sum))
    query_grad = query_back(unit, inverse, docs_mine, docs_other, coefficient)
    query_grad, own_terms = lax.optimization_barrier((query_grad, own_terms))
    grad_k, grad_v = finish(total_of(own_terms), from_high)
    return (query_grad, grad_q[None], grad_k[None], grad_v[None])


def solution(mesh):
    fine = Mesh(mesh.devices.reshape(8, 4, 2, 4, 2), ("zlo", "y", "zhi", "x", "core"))
    dp, ctx = ("zlo", "y"), ("zhi", "x", "core")
    tokens = P(dp, ctx, None)
    return jax.shard_map(
        per_device,
        mesh=fine,
        in_specs=(tokens, tokens, tokens, P(dp, None), P(dp, None), P(dp)),
        out_specs=(P(dp, None), tokens, tokens, tokens),
        check_vma=False,
    )
```

```python
import jax
import jax.numpy as jnp
from jax import lax
from jax.experimental import pallas as pl
from jax.experimental.pallas import tpu as pltpu
from jax.sharding import Mesh
from jax.sharding import PartitionSpec as P

HEAD_DIM = 128
HEADS = 14
KV_HEADS = 2
PER_GROUP = HEADS // KV_HEADS
DOCS = 4
TOK = 128
SEQ = 2048
EMB = HEADS * HEAD_DIM
KVW = KV_HEADS * HEAD_DIM
GROUP_W = PER_GROUP * TOK
CHUNK = 2 * TOK
HALF = SEQ // 2
CHUNKS = HALF // CHUNK
PIECE = EMB // 2
NDOC = 128

FACTOR = HEAD_DIM ** (-0.5)
INVERSE_TEMPER = 0.05
EPSILON = 1e-06
LOG2_E = 1.4426950408889634
FULL_ACCURACY = lax.Precision.HIGHEST
MASKED = -1e30
TINY = 1e-30
FILLS_A_WAIT = 10**12
NT = (((1,), (1,)), ((), ()))
TN = (((0,), (0,)), ((), ()))
NN = (((1,), (0,)), ((), ()))
NEAR = ("x", "core")
VMEM_BYTES = 24 * 1024 * 1024


def mm(a, b, dims, precision=None):
    return lax.dot_general(a, b, dims, precision=precision, preferred_element_type=jnp.float32)


def place():
    return tuple(lax.axis_index(axis) for axis in ("zlo", "y", "zhi", "x", "core"))


class Row:
    def __init__(self, lengths):
        _, _, self.high, x, self.core = place()
        self.first = ((self.high * 4 + x) * 2 + self.core) * TOK
        self.lengths = [lengths[0, d] for d in range(DOCS)]
        qpos = self.first + lax.broadcasted_iota(jnp.int32, (1, TOK), 1)
        start = jnp.zeros((1, TOK), jnp.int32)
        doc = jnp.zeros((1, TOK), jnp.int32)
        first_start = jnp.int32(0)
        end = jnp.int32(0)
        for d in range(DOCS - 1):
            end = end + self.lengths[d]
            start = jnp.where(qpos >= end, end, start)
            doc = doc + (qpos >= end).astype(jnp.int32)
            first_start = jnp.where(self.first >= end, end, first_start)
        self.qpos, self.start = qpos, start
        self.member = (lax.broadcasted_iota(jnp.int32, (8, TOK), 0) == doc).astype(jnp.float32)
        own_base = self.high * HALF
        self.own = (
            own_base,
            lax.div(jnp.maximum(first_start - own_base, 0), CHUNK),
            lax.div(self.first + (TOK - 1) - own_base, CHUNK) + 1,
        )
        self.low = (jnp.int32(0), lax.div(first_start, CHUNK), CHUNKS * self.high)

    def length_column(self):
        rows = lax.broadcasted_iota(jnp.int32, (8, 1), 0)
        column = jnp.ones((8, 1), jnp.float32)
        for d in range(DOCS):
            column = jnp.where(rows == d, self.lengths[d].astype(jnp.float32), column)
        return column

    def bias(self, base, chunk):
        at = lax.broadcasted_iota(jnp.int32, (CHUNK, TOK), 0)
        half = lax.div(at, TOK)
        turned = jnp.where(self.core == 1, 1 - half, half)
        pos = base + chunk * CHUNK + turned * TOK + (at - half * TOK)
        allowed = (pos >= self.start) & (pos <= self.qpos)
        return jnp.where(allowed, 0.0, MASKED).astype(jnp.float32)


def chunk_of(kv, chunk, column):
    at = slice(column * HEAD_DIM, (column + 1) * HEAD_DIM)
    return jnp.concatenate([half[chunk, :, at] for half in kv], axis=0)


def put_chunk(refs, chunk, column, rows):
    at = slice(column * HEAD_DIM, (column + 1) * HEAD_DIM)
    refs[0][chunk, :, at] = rows[:TOK]
    refs[1][chunk, :, at] = rows[TOK:]


def fill_bias(row, part, bias):
    base, low, high = part

    def step(chunk, carry):
        bias[chunk] = row.bias(base, chunk)
        return carry

    lax.fori_loop(low, high, step, 0)


def halves(values):
    top = values.astype(jnp.bfloat16)
    return top, (values - top.astype(jnp.float32)).astype(jnp.bfloat16)


def head_rows(ref, group):
    return jnp.concatenate(
        [
            ref[:, (group * PER_GROUP + h) * HEAD_DIM : (group * PER_GROUP + h + 1) * HEAD_DIM]
            for h in range(PER_GROUP)
        ],
        axis=0,
    )


def head(h):
    return slice(h * HEAD_DIM, (h + 1) * HEAD_DIM)


def spread_kernel(kv, out, done):
    copies = [pltpu.make_async_copy(kv, out.at[i], done.at[i]) for i in range(4)]
    for copy in copies:
        copy.start()
    for copy in copies:
        copy.wait()


def part_attention(part, q, kv, bias, stats, weights, out):
    _, low, high = part
    stats[0] = jnp.full((HEADS, TOK), MASKED, jnp.float32)
    stats[1] = jnp.zeros((HEADS, TOK), jnp.float32)
    out[...] = jnp.zeros(out.shape, jnp.float32)

    def step(chunk, carry):
        blocked = bias[chunk]
        for group in range(KV_HEADS):
            k_rows = chunk_of(kv, chunk, group)
            scales = []
            for h in range(group * PER_GROUP, (group + 1) * PER_GROUP):
                i = h - group * PER_GROUP
                if i % 2 == 0:
                    many = 2 if i + 1 < PER_GROUP else 1
                    pair = jnp.concatenate([q[:, head(h + j)] for j in range(many)], axis=0)
                    every = mm(k_rows, pair, NT)
                scores = every[:, head(i % 2)] + blocked
                old = stats[0, h : h + 1]
                top = jnp.maximum(old, jnp.max(scores, axis=0, keepdims=True))
                exps = jnp.exp2((scores - top) * (FACTOR * LOG2_E))
                weights[:, head(h)] = exps.astype(jnp.bfloat16)
                scale = jnp.exp((old - top) * FACTOR)
                stats[0, h : h + 1] = top
                stats[1, h : h + 1] = stats[1, h : h + 1] * scale + jnp.sum(
                    exps, axis=0, keepdims=True
                )
                scales.append(scale)
            columns = slice(group * GROUP_W, (group + 1) * GROUP_W)
            sums = mm(chunk_of(kv, chunk, KV_HEADS + group), weights[:, columns], TN)
            for i in range(PER_GROUP):
                at = head(group * PER_GROUP + i)
                out[:, at] = out[:, at] * scales[i] + sums[:, head(i)]
        return carry

    lax.fori_loop(low, high, step, 0)


def part_result(h, stats):
    total = jnp.maximum(stats[1, h : h + 1], TINY)
    return stats[0, h : h + 1] * FACTOR + jnp.log(total), 1.0 / total


def bias_kernel(lengths, own_bias, low_bias):
    row = Row(lengths)
    fill_bias(row, row.own, own_bias)
    fill_bias(row, row.low, low_bias)


def attend_own_kernel(lengths, q, mine, other, bias, att, lse, stats, weights, out):
    row = Row(lengths)
    part_attention(row.own, q, (mine, other), bias, stats, weights, out)
    for h in range(HEADS):
        log_total, inverse = part_result(h, stats)
        att[:, head(h)] = out[:, head(h)] * inverse
        lse[:, head(h)] = jnp.broadcast_to(log_total, (8, TOK))


def attend_low_kernel(
    lengths, q, mine, other, own_att, own_lse, bias, att, lse, pieces, stats, weights, out, doc_sum
):
    row = Row(lengths)
    member = jnp.concatenate([row.member, jnp.zeros((TOK - 8, TOK), jnp.float32)], axis=0)
    member = member.astype(jnp.bfloat16)
    part_attention(row.low, q, (mine, other), bias, stats, weights, out)
    for h in range(HEADS):
        at = head(h)
        low_total, inverse = part_result(h, stats)
        own_total = own_lse[0:1, at]
        top = jnp.maximum(low_total, own_total)
        log_total = top + jnp.log(jnp.exp(low_total - top) + jnp.exp(own_total - top))
        own_scale = jnp.exp(own_total - log_total)
        low_scale = jnp.exp(low_total - log_total) * inverse
        lse[:, at] = jnp.broadcast_to(log_total, (8, TOK))
        merged = own_att[:, at] * own_scale + out[:, at] * low_scale
        att[:, at] = merged
        big, small = halves(merged)
        doc_sum[:, at] = (mm(big, member, NT) + mm(small, member, NT)).T[:8]
    mean = doc_sum[...] / row.length_column()
    for d in range(DOCS):
        for c in range(2):
            pieces[2 * d + c] = mean[d : d + 1, c * PIECE : (c + 1) * PIECE]


def inverse_kernel(q, inverse):
    values = q[...].astype(jnp.float32)
    query_inv = lax.rsqrt(jnp.sum(values * values, axis=1, keepdims=True) + EPSILON)
    inverse[...] = jnp.broadcast_to(query_inv, (128, 128))


def unit_kernel(q, inverse, unit):
    unit[...] = q[...].astype(jnp.float32) * inverse[:, :1]


def contrast_kernel(unit, positive, docs_mine, docs_other, coefficient, terms, own_docs):
    z_lo, y, _, x, core = place()
    d_mine, d_other = docs_mine[...], docs_other[...]
    doc_inv = lax.rsqrt(
        jnp.sum(d_mine * d_mine, axis=1, keepdims=True)
        + jnp.sum(d_other * d_other, axis=1, keepdims=True)
        + EPSILON
    )
    q_left, q_right = unit[:, :PIECE], unit[:, PIECE:]
    q_mine = jnp.where(core == 1, q_right, q_left)
    q_other = jnp.where(core == 1, q_left, q_right)
    logits = mm(d_mine * doc_inv, q_mine, NT, FULL_ACCURACY)
    logits = (logits + mm(d_other * doc_inv, q_other, NT, FULL_ACCURACY)) / INVERSE_TEMPER
    exps = jnp.exp(logits)
    at = lax.broadcasted_iota(jnp.int32, (NDOC, 128), 0)
    doc = ((at % 8) * 4 + at // 32) * DOCS + (at // 8) % 4
    target = (doc == positive[...]).astype(jnp.float32)
    coefficient[...] = exps / jnp.sum(exps, axis=0, keepdims=True) - target
    near = jnp.concatenate(
        [coefficient[pl.ds(pl.multiple_of(b * 32 + x * 8, 8), 8), :] for b in range(4)], axis=0
    )
    near_terms = mm(near, q_mine, NN, FULL_ACCURACY) / INVERSE_TEMPER
    for r in range(32):
        terms[r] = near_terms[r : r + 1]
    own_docs[...] = jnp.zeros((8, EMB), jnp.float32)
    for d in range(DOCS):
        r = y * 32 + d * 8 + z_lo
        a, b = docs_mine[pl.ds(r, 1), :], docs_other[pl.ds(r, 1), :]
        own_docs[d : d + 1, :PIECE] = jnp.where(core == 1, b, a)
        own_docs[d : d + 1, PIECE:] = jnp.where(core == 1, a, b)


def query_kernel(unit, inverse, docs_mine, docs_other, coefficient, query_grad):
    _, _, _, _, core = place()
    d_mine, d_other = docs_mine[...], docs_other[...]
    doc_inv = lax.rsqrt(
        jnp.sum(d_mine * d_mine, axis=1, keepdims=True)
        + jnp.sum(d_other * d_other, axis=1, keepdims=True)
        + EPSILON
    )
    scaled = coefficient[...] * doc_inv
    u_mine = mm(scaled, d_mine, TN, FULL_ACCURACY) / INVERSE_TEMPER
    u_other = mm(scaled, d_other, TN, FULL_ACCURACY) / INVERSE_TEMPER
    u_left = jnp.where(core == 1, u_other, u_mine)
    u_right = jnp.where(core == 1, u_mine, u_other)
    query_inv = inverse[:, :1]
    q_left, q_right = unit[:, :PIECE], unit[:, PIECE:]
    inner = jnp.sum(q_left * u_left, axis=1, keepdims=True) + jnp.sum(
        q_right * u_right, axis=1, keepdims=True
    )
    query_grad[:, :PIECE] = query_inv * (u_left - q_left * inner)
    query_grad[:, PIECE:] = query_inv * (u_right - q_right * inner)


def back_part(part, q, kv, bias, lse, out_low, delta, dq, d_kv, grads, weights):
    _, low, high = part

    def step(chunk, carry):
        blocked = bias[chunk]
        for group in range(KV_HEADS):
            k_rows = chunk_of(kv, chunk, group)
            v_rows = chunk_of(kv, chunk, KV_HEADS + group)
            for h in range(group * PER_GROUP, (group + 1) * PER_GROUP):
                at = head(h)
                i = h - group * PER_GROUP
                if i % 2 == 0:
                    many = 2 if i + 1 < PER_GROUP else 1
                    pair = jnp.concatenate([q[:, head(h + j)] for j in range(many)], axis=0)
                    every = mm(k_rows, pair, NT)
                    pair = jnp.concatenate([out_low[:, head(h + j)] for j in range(many)], axis=0)
                    flows = mm(v_rows, pair, NT)
                scores = every[:, head(i % 2)] * (FACTOR * LOG2_E) + blocked
                probs = jnp.exp2(scores - lse[0:1, at] * LOG2_E)
                flow = flows[:, head(i % 2)]
                grads[:, at] = (probs * (flow - delta[0:1, at])).astype(jnp.bfloat16)
                weights[:, at] = probs.astype(jnp.bfloat16)
            columns = slice(group * GROUP_W, (group + 1) * GROUP_W)
            score_grad = grads[:, columns]
            dq[:, columns] += mm(k_rows, score_grad, TN)
            k_part = mm(score_grad, head_rows(q, group), NN) * FACTOR
            v_part = mm(weights[:, columns], head_rows(out_low, group), NN)
            put_chunk(d_kv, chunk, group, k_part.astype(jnp.bfloat16))
            put_chunk(d_kv, chunk, KV_HEADS + group, v_part.astype(jnp.bfloat16))
        return carry

    lax.fori_loop(low, high, step, 0)


def back_low_kernel(
    lengths,
    q,
    mine,
    other,
    att,
    lse,
    own_docs,
    upstream,
    bias,
    out_low,
    delta,
    dq_low,
    d_mine,
    d_other,
    grads,
    weights,
):
    row = Row(lengths)
    d_mine[...] = jnp.zeros(d_mine.shape, d_mine.dtype)
    d_other[...] = jnp.zeros(d_other.shape, d_other.dtype)
    w = jnp.concatenate(
        [
            jnp.concatenate([upstream[2 * d + c] for d in range(DOCS)] * 2, axis=0)
            for c in range(2)
        ],
        axis=1,
    )
    docs = own_docs[...]
    doc_inv = lax.rsqrt(jnp.sum(docs * docs, axis=1, keepdims=True) + EPSILON)
    unit = docs * doc_inv
    inner = jnp.sum(unit * w, axis=1, keepdims=True)
    doc_grad = doc_inv * (w - unit * inner) / row.length_column()
    big, small = halves(doc_grad)
    member = row.member.astype(jnp.bfloat16)
    out_low[...] = mm(member, big, TN).astype(jnp.bfloat16)
    both = jnp.concatenate([big, small], axis=0)
    twice = jnp.concatenate([member, member], axis=0)
    for h in range(HEADS):
        at = head(h)
        one = jnp.sum(mm(both[:, at], twice, TN) * att[:, at], axis=0, keepdims=True)
        delta[:, at] = jnp.broadcast_to(one, (8, TOK))
    dq_low[...] = jnp.zeros(dq_low.shape, jnp.float32)
    kv, d_kv = (mine, other), (d_mine, d_other)
    back_part(row.low, q, kv, bias, lse, out_low, delta, dq_low, d_kv, grads, weights)


def back_own_kernel(
    lengths,
    q,
    mine,
    other,
    lse,
    out_low,
    delta,
    dq_low,
    grad_q,
    d_mine,
    d_other,
    bias,
    dq,
    grads,
    weights,
):
    row = Row(lengths)
    d_mine[...] = jnp.zeros(d_mine.shape, d_mine.dtype)
    d_other[...] = jnp.zeros(d_other.shape, d_other.dtype)
    fill_bias(row, row.own, bias)
    dq[...] = dq_low[...]
    kv, d_kv = (mine, other), (d_mine, d_other)
    back_part(row.own, q, kv, bias, lse, out_low, delta, dq, d_kv, grads, weights)
    for h in range(HEADS):
        grad_q[:, head(h)] = (dq[:, head(h)].T * FACTOR).astype(jnp.bfloat16)


def total_kernel(terms, total):
    total[...] = added(terms)


def finish_kernel(near, far, grad_k, grad_v):
    total = (near[...] + far[...].astype(jnp.float32)).astype(jnp.bfloat16)
    grad_k[...] = total[:, :KVW]
    grad_v[...] = total[:, KVW:]


F32, BF16 = jnp.float32, jnp.bfloat16


def shape(dims, dtype):
    return jax.ShapeDtypeStruct(dims, dtype)


def run(kernel, name, outs, scratch, lengths, *arrays, flops=0):
    vmem = pl.BlockSpec(memory_space=pltpu.VMEM)
    smem = pl.BlockSpec(memory_space=pltpu.SMEM)
    first = () if lengths is None else (lengths,)
    return pl.pallas_call(
        kernel,
        out_shape=outs,
        in_specs=[smem] * len(first) + [vmem] * len(arrays),
        out_specs=tuple(vmem for _ in outs),
        scratch_shapes=scratch,
        compiler_params=pltpu.CompilerParams(vmem_limit_bytes=VMEM_BYTES),
        cost_estimate=pl.CostEstimate(flops=flops, bytes_accessed=0, transcendentals=0),
        name=name,
    )(*first, *arrays)


TERMS = shape((CHUNKS, TOK, 2 * KVW), BF16)
WIDE = pltpu.VMEM((HEAD_DIM, EMB), F32)
BIAS = pltpu.VMEM((CHUNKS, CHUNK, TOK), F32)
STATS = pltpu.VMEM((2, HEADS, TOK), F32)
ROUNDED = pltpu.VMEM((CHUNK, EMB), BF16)


def spread(kv):
    anywhere = pl.BlockSpec(memory_space=pl.ANY)
    return pl.pallas_call(
        spread_kernel,
        out_shape=shape((4, *kv.shape), kv.dtype),
        in_specs=[anywhere],
        out_specs=anywhere,
        scratch_shapes=[pltpu.SemaphoreType.DMA((4,))],
        compiler_params=pltpu.CompilerParams(vmem_limit_bytes=VMEM_BYTES),
        cost_estimate=pl.CostEstimate(flops=0, bytes_accessed=0, transcendentals=0),
        name="spread",
    )(kv)


def biases(lengths):
    one = shape((CHUNKS, CHUNK, TOK), F32)
    return run(bias_kernel, "biases", (one, one), [], lengths, flops=FILLS_A_WAIT)


def attend_own(lengths, *arrays):
    outs = (shape((HEAD_DIM, EMB), F32), shape((8, EMB), F32))
    scratch = [STATS, ROUNDED, WIDE]
    return run(
        attend_own_kernel, "attend_own", outs, scratch, lengths, *arrays, flops=FILLS_A_WAIT
    )


def attend_low(lengths, *arrays):
    outs = (shape((HEAD_DIM, EMB), F32), shape((8, EMB), F32), shape((8, 1, PIECE), F32))
    scratch = [STATS, ROUNDED, WIDE, pltpu.VMEM((8, EMB), F32)]
    return run(attend_low_kernel, "attend_low", outs, scratch, lengths, *arrays)


def query_inverses(q):
    outs = (shape((128, 128), F32),)
    return run(inverse_kernel, "query_inverses", outs, [], None, q, flops=FILLS_A_WAIT)[0]


def query_units(*arrays):
    outs = (shape((128, EMB), F32),)
    return run(unit_kernel, "query_units", outs, [], None, *arrays, flops=FILLS_A_WAIT)[0]


def contrast(*arrays):
    outs = (shape((NDOC, 128), F32), shape((32, 1, PIECE), F32), shape((8, EMB), F32))
    return run(contrast_kernel, "contrast", outs, [], None, *arrays)


def query_back(*arrays):
    outs = (shape((128, EMB), F32),)
    return run(query_kernel, "query_back", outs, [], None, *arrays, flops=FILLS_A_WAIT)[0]


def total_of(terms):
    outs = (shape((TOK, 2 * KVW), F32),)
    return run(total_kernel, "total_of", outs, [], None, terms)[0]


def finish(*arrays):
    outs = (shape((TOK, KVW), BF16), shape((TOK, KVW), BF16))
    return run(finish_kernel, "finish", outs, [], None, *arrays)


def back_low(lengths, *arrays):
    outs = (
        shape((TOK, EMB), BF16),
        shape((8, EMB), F32),
        shape((HEAD_DIM, EMB), F32),
        TERMS,
        TERMS,
    )
    return run(back_low_kernel, "back_low", outs, [ROUNDED, ROUNDED], lengths, *arrays)


def back_own(lengths, *arrays):
    outs = (shape((TOK, EMB), BF16), TERMS, TERMS)
    return run(back_own_kernel, "back_own", outs, [BIAS, WIDE, ROUNDED, ROUNDED], lengths, *arrays)


def to_all(block, axes, count):
    return lax.all_to_all(jnp.broadcast_to(block[None], (count,) + block.shape), axes, 0, 0)


def swap_cores(block):
    return lax.ppermute(block, "core", [(0, 1), (1, 0)])


def added(blocks):
    total = blocks[0].astype(F32)
    for i in range(1, blocks.shape[0]):
        total = total + blocks[i].astype(F32)
    return total


def pair_terms(d_mine, d_other):
    got = swap_cores(d_other)
    return (d_mine.astype(F32) + got.astype(F32)).astype(BF16)


def per_device(queries_q, keys, values, lengths, query_emb, positive):
    q = queries_q[0]
    kv = jnp.concatenate([keys[0], values[0]], axis=1)
    kv_low = lax.ppermute(kv, "zhi", [(0, 1)])
    own_mine = lax.all_to_all(spread(kv), "x", 0, 0)
    inverse = query_inverses(query_emb)
    own_mine, inverse, after = lax.optimization_barrier((own_mine, inverse, lengths))
    own_other = swap_cores(own_mine)
    own_bias, low_bias = biases(after)
    own_other, inverse, own_bias = lax.optimization_barrier((own_other, inverse, own_bias))
    unit = query_units(query_emb, inverse)
    kv_low, own_other, unit = lax.optimization_barrier((kv_low, own_other, unit))
    own_att, own_lse = attend_own(lengths, q, own_mine, own_other, own_bias)
    low_mine = lax.all_to_all(spread(kv_low), "x", 0, 0)
    low_mine, own_att = lax.optimization_barrier((low_mine, own_att))
    low_other = swap_cores(low_mine)
    att, lse, pieces = attend_low(
        lengths, q, low_mine, low_other, own_att, own_lse, low_bias
    )

    part = added(lax.all_to_all(pieces, NEAR, 0, 0))
    column = to_all(part, ("zlo", "zhi"), 16)
    column = (column[0::2] + column[1::2]).reshape(8, PIECE)
    docs_mine = to_all(column, ("y", "x"), 16).reshape(NDOC, PIECE)
    docs_other = swap_cores(docs_mine)

    coefficient, terms, own_docs = contrast(
        unit, positive.reshape(1, 128), docs_mine, docs_other
    )
    terms = added(lax.all_to_all(terms, ("y", "zlo"), 0, 0))
    upstream = to_all(terms, NEAR, 8)

    out_low, delta, dq_low, d_mine, d_other = back_low(
        lengths, q, low_mine, low_other, att, lse, own_docs, upstream, low_bias
    )
    paired = pair_terms(d_mine, d_other)
    paired, dq_low = lax.optimization_barrier((paired, dq_low))
    grad_q, own_d_mine, own_d_other = back_own(
        lengths, q, own_mine, own_other, lse, out_low, delta, dq_low
    )
    low_terms = lax.all_to_all(paired, "x", 0, 0)
    low_sum = added(low_terms).astype(BF16)
    own_paired = pair_terms(own_d_mine, own_d_other)
    from_high = lax.ppermute(low_sum, "zhi", [(1, 0)])
    low_sum, own_paired = lax.optimization_barrier((low_sum, own_paired))
    own_terms = lax.all_to_all(own_paired, "x", 0, 0)
    coefficient, low_sum = lax.optimization_barrier((coefficient, low_sum))
    query_grad = query_back(unit, inverse, docs_mine, docs_other, coefficient)
    query_grad, own_terms = lax.optimization_barrier((query_grad, own_terms))
    grad_k, grad_v = finish(total_of(own_terms), from_high)
    return (query_grad, grad_q[None], grad_k[None], grad_v[None])


def solution(mesh):
    fine = Mesh(mesh.devices.reshape(8, 4, 2, 4, 2), ("zlo", "y", "zhi", "x", "core"))
    dp, ctx = ("zlo", "y"), ("zhi", "x", "core")
    tokens = P(dp, ctx, None)
    return jax.shard_map(
        per_device,
        mesh=fine,
        in_specs=(tokens, tokens, tokens, P(dp, None), P(dp, None), P(dp)),
        out_specs=(P(dp, None), tokens, tokens, tokens),
        check_vma=False,
    )
```

```python
import jax
import jax.numpy as jnp
from jax import lax
from jax.experimental import pallas as pl
from jax.experimental.pallas import tpu as pltpu
from jax.sharding import Mesh
from jax.sharding import PartitionSpec as P

HEAD_DIM = 128
HEADS = 14
KV_HEADS = 2
PER_GROUP = HEADS // KV_HEADS
DOCS = 4
TOK = 128
SEQ = 2048
EMB = HEADS * HEAD_DIM
KVW = KV_HEADS * HEAD_DIM
GROUP_W = PER_GROUP * TOK
CHUNK = 2 * TOK
HALF = SEQ // 2
CHUNKS = HALF // CHUNK
PIECE = EMB // 2
NDOC = 128

FACTOR = HEAD_DIM ** (-0.5)
INVERSE_TEMPER = 0.05
EPSILON = 1e-06
LOG2_E = 1.4426950408889634
FULL_ACCURACY = lax.Precision.HIGHEST
MASKED = -1e30
TINY = 1e-30
FILLS_A_WAIT = 10**12
NT = (((1,), (1,)), ((), ()))
TN = (((0,), (0,)), ((), ()))
NN = (((1,), (0,)), ((), ()))
NEAR = ("x", "core")
VMEM_BYTES = 24 * 1024 * 1024


def mm(a, b, dims, precision=None):
    return lax.dot_general(a, b, dims, precision=precision, preferred_element_type=jnp.float32)


def place():
    return tuple(lax.axis_index(axis) for axis in ("zlo", "y", "zhi", "x", "core"))


class Row:
    def __init__(self, lengths):
        _, _, self.high, x, self.core = place()
        self.first = ((self.high * 4 + x) * 2 + self.core) * TOK
        self.lengths = [lengths[0, d] for d in range(DOCS)]
        qpos = self.first + lax.broadcasted_iota(jnp.int32, (1, TOK), 1)
        start = jnp.zeros((1, TOK), jnp.int32)
        doc = jnp.zeros((1, TOK), jnp.int32)
        first_start = jnp.int32(0)
        end = jnp.int32(0)
        for d in range(DOCS - 1):
            end = end + self.lengths[d]
            start = jnp.where(qpos >= end, end, start)
            doc = doc + (qpos >= end).astype(jnp.int32)
            first_start = jnp.where(self.first >= end, end, first_start)
        self.qpos, self.start = qpos, start
        self.member = (lax.broadcasted_iota(jnp.int32, (8, TOK), 0) == doc).astype(jnp.float32)
        own_base = self.high * HALF
        self.own = (
            own_base,
            lax.div(jnp.maximum(first_start - own_base, 0), CHUNK),
            lax.div(self.first + (TOK - 1) - own_base, CHUNK) + 1,
        )
        self.low = (jnp.int32(0), lax.div(first_start, CHUNK), CHUNKS * self.high)

    def length_column(self):
        rows = lax.broadcasted_iota(jnp.int32, (8, 1), 0)
        column = jnp.ones((8, 1), jnp.float32)
        for d in range(DOCS):
            column = jnp.where(rows == d, self.lengths[d].astype(jnp.float32), column)
        return column

    def bias(self, base, chunk):
        at = lax.broadcasted_iota(jnp.int32, (CHUNK, TOK), 0)
        half = lax.div(at, TOK)
        turned = jnp.where(self.core == 1, 1 - half, half)
        pos = base + chunk * CHUNK + turned * TOK + (at - half * TOK)
        allowed = (pos >= self.start) & (pos <= self.qpos)
        return jnp.where(allowed, 0.0, MASKED).astype(jnp.float32)


def chunk_of(kv, chunk, column):
    at = slice(column * HEAD_DIM, (column + 1) * HEAD_DIM)
    return jnp.concatenate([half[chunk, :, at] for half in kv], axis=0)


def put_chunk(refs, chunk, column, rows):
    at = slice(column * HEAD_DIM, (column + 1) * HEAD_DIM)
    refs[0][chunk, :, at] = rows[:TOK]
    refs[1][chunk, :, at] = rows[TOK:]


def fill_bias(row, part, bias):
    base, low, high = part

    def step(chunk, carry):
        bias[chunk] = row.bias(base, chunk)
        return carry

    lax.fori_loop(low, high, step, 0)


def halves(values):
    top = values.astype(jnp.bfloat16)
    return top, (values - top.astype(jnp.float32)).astype(jnp.bfloat16)


def head_rows(ref, group):
    return jnp.concatenate(
        [
            ref[:, (group * PER_GROUP + h) * HEAD_DIM : (group * PER_GROUP + h + 1) * HEAD_DIM]
            for h in range(PER_GROUP)
        ],
        axis=0,
    )


def head(h):
    return slice(h * HEAD_DIM, (h + 1) * HEAD_DIM)


def spread_kernel(kv, out, done):
    copies = [pltpu.make_async_copy(kv, out.at[i], done.at[i]) for i in range(4)]
    for copy in copies:
        copy.start()
    for copy in copies:
        copy.wait()


def part_attention(part, q, kv, bias, stats, weights, out):
    _, low, high = part
    stats[0] = jnp.full((HEADS, TOK), MASKED, jnp.float32)
    stats[1] = jnp.zeros((HEADS, TOK), jnp.float32)
    out[...] = jnp.zeros(out.shape, jnp.float32)

    def step(chunk, carry):
        blocked = bias[chunk]
        for group in range(KV_HEADS):
            k_rows = chunk_of(kv, chunk, group)
            scales = []
            for h in range(group * PER_GROUP, (group + 1) * PER_GROUP):
                i = h - group * PER_GROUP
                if i % 2 == 0:
                    many = 2 if i + 1 < PER_GROUP else 1
                    pair = jnp.concatenate([q[:, head(h + j)] for j in range(many)], axis=0)
                    every = mm(k_rows, pair, NT)
                scores = every[:, head(i % 2)] + blocked
                old = stats[0, h : h + 1]
                top = jnp.maximum(old, jnp.max(scores, axis=0, keepdims=True))
                exps = jnp.exp2((scores - top) * (FACTOR * LOG2_E))
                weights[:, head(h)] = exps.astype(jnp.bfloat16)
                scale = jnp.exp((old - top) * FACTOR)
                stats[0, h : h + 1] = top
                stats[1, h : h + 1] = stats[1, h : h + 1] * scale + jnp.sum(
                    exps, axis=0, keepdims=True
                )
                scales.append(scale)
            columns = slice(group * GROUP_W, (group + 1) * GROUP_W)
            sums = mm(chunk_of(kv, chunk, KV_HEADS + group), weights[:, columns], TN)
            for i in range(PER_GROUP):
                at = head(group * PER_GROUP + i)
                out[:, at] = out[:, at] * scales[i] + sums[:, head(i)]
        return carry

    lax.fori_loop(low, high, step, 0)


def part_result(h, stats):
    total = jnp.maximum(stats[1, h : h + 1], TINY)
    return stats[0, h : h + 1] * FACTOR + jnp.log(total), 1.0 / total


def bias_kernel(lengths, own_bias, low_bias):
    row = Row(lengths)
    fill_bias(row, row.own, own_bias)
    fill_bias(row, row.low, low_bias)


def attend_own_kernel(lengths, q, mine, other, bias, att, lse, stats, weights, out):
    row = Row(lengths)
    part_attention(row.own, q, (mine, other), bias, stats, weights, out)
    for h in range(HEADS):
        log_total, inverse = part_result(h, stats)
        att[:, head(h)] = out[:, head(h)] * inverse
        lse[:, head(h)] = jnp.broadcast_to(log_total, (8, TOK))


def attend_low_kernel(
    lengths, q, mine, other, own_att, own_lse, bias, att, lse, pieces, stats, weights, out, doc_sum
):
    row = Row(lengths)
    member = jnp.concatenate([row.member, jnp.zeros((TOK - 8, TOK), jnp.float32)], axis=0)
    member = member.astype(jnp.bfloat16)
    part_attention(row.low, q, (mine, other), bias, stats, weights, out)
    for h in range(HEADS):
        at = head(h)
        low_total, inverse = part_result(h, stats)
        own_total = own_lse[0:1, at]
        top = jnp.maximum(low_total, own_total)
        log_total = top + jnp.log(jnp.exp(low_total - top) + jnp.exp(own_total - top))
        own_scale = jnp.exp(own_total - log_total)
        low_scale = jnp.exp(low_total - log_total) * inverse
        lse[:, at] = jnp.broadcast_to(log_total, (8, TOK))
        merged = own_att[:, at] * own_scale + out[:, at] * low_scale
        att[:, at] = merged
        big, small = halves(merged)
        doc_sum[:, at] = (mm(big, member, NT) + mm(small, member, NT)).T[:8]
    mean = doc_sum[...] / row.length_column()
    for d in range(DOCS):
        for c in range(2):
            pieces[2 * d + c] = mean[d : d + 1, c * PIECE : (c + 1) * PIECE]


def inverse_kernel(q, inverse):
    values = q[...].astype(jnp.float32)
    query_inv = lax.rsqrt(jnp.sum(values * values, axis=1, keepdims=True) + EPSILON)
    inverse[...] = jnp.broadcast_to(query_inv, (128, 128))


def unit_kernel(q, inverse, unit):
    unit[...] = q[...].astype(jnp.float32) * inverse[:, :1]


def contrast_kernel(unit, positive, docs_mine, docs_other, coefficient, terms, own_docs):
    z_lo, y, _, x, core = place()
    d_mine, d_other = docs_mine[...], docs_other[...]
    doc_inv = lax.rsqrt(
        jnp.sum(d_mine * d_mine, axis=1, keepdims=True)
        + jnp.sum(d_other * d_other, axis=1, keepdims=True)
        + EPSILON
    )
    q_left, q_right = unit[:, :PIECE], unit[:, PIECE:]
    q_mine = jnp.where(core == 1, q_right, q_left)
    q_other = jnp.where(core == 1, q_left, q_right)
    logits = mm(d_mine * doc_inv, q_mine, NT, FULL_ACCURACY)
    logits = (logits + mm(d_other * doc_inv, q_other, NT, FULL_ACCURACY)) / INVERSE_TEMPER
    exps = jnp.exp(logits)
    at = lax.broadcasted_iota(jnp.int32, (NDOC, 128), 0)
    doc = ((at % 8) * 4 + at // 32) * DOCS + (at // 8) % 4
    target = (doc == positive[...]).astype(jnp.float32)
    coefficient[...] = exps / jnp.sum(exps, axis=0, keepdims=True) - target
    near = jnp.concatenate(
        [coefficient[pl.ds(pl.multiple_of(b * 32 + x * 8, 8), 8), :] for b in range(4)], axis=0
    )
    near_terms = mm(near, q_mine, NN, FULL_ACCURACY) / INVERSE_TEMPER
    for r in range(32):
        terms[r] = near_terms[r : r + 1]
    own_docs[...] = jnp.zeros((8, EMB), jnp.float32)
    for d in range(DOCS):
        r = y * 32 + d * 8 + z_lo
        a, b = docs_mine[pl.ds(r, 1), :], docs_other[pl.ds(r, 1), :]
        own_docs[d : d + 1, :PIECE] = jnp.where(core == 1, b, a)
        own_docs[d : d + 1, PIECE:] = jnp.where(core == 1, a, b)


def query_kernel(unit, inverse, docs_mine, docs_other, coefficient, query_grad):
    _, _, _, _, core = place()
    d_mine, d_other = docs_mine[...], docs_other[...]
    doc_inv = lax.rsqrt(
        jnp.sum(d_mine * d_mine, axis=1, keepdims=True)
        + jnp.sum(d_other * d_other, axis=1, keepdims=True)
        + EPSILON
    )
    scaled = coefficient[...] * doc_inv
    u_mine = mm(scaled, d_mine, TN, FULL_ACCURACY) / INVERSE_TEMPER
    u_other = mm(scaled, d_other, TN, FULL_ACCURACY) / INVERSE_TEMPER
    u_left = jnp.where(core == 1, u_other, u_mine)
    u_right = jnp.where(core == 1, u_mine, u_other)
    query_inv = inverse[:, :1]
    q_left, q_right = unit[:, :PIECE], unit[:, PIECE:]
    inner = jnp.sum(q_left * u_left, axis=1, keepdims=True) + jnp.sum(
        q_right * u_right, axis=1, keepdims=True
    )
    query_grad[:, :PIECE] = query_inv * (u_left - q_left * inner)
    query_grad[:, PIECE:] = query_inv * (u_right - q_right * inner)


def back_part(part, q, kv, bias, lse, out_low, delta, dq, d_kv, grads, weights):
    _, low, high = part

    def step(chunk, carry):
        blocked = bias[chunk]
        for group in range(KV_HEADS):
            k_rows = chunk_of(kv, chunk, group)
            v_rows = chunk_of(kv, chunk, KV_HEADS + group)
            for h in range(group * PER_GROUP, (group + 1) * PER_GROUP):
                at = head(h)
                i = h - group * PER_GROUP
                if i % 2 == 0:
                    many = 2 if i + 1 < PER_GROUP else 1
                    pair = jnp.concatenate([q[:, head(h + j)] for j in range(many)], axis=0)
                    every = mm(k_rows, pair, NT)
                    pair = jnp.concatenate([out_low[:, head(h + j)] for j in range(many)], axis=0)
                    flows = mm(v_rows, pair, NT)
                scores = every[:, head(i % 2)] * (FACTOR * LOG2_E) + blocked
                probs = jnp.exp2(scores - lse[0:1, at] * LOG2_E)
                flow = flows[:, head(i % 2)]
                grads[:, at] = (probs * (flow - delta[0:1, at])).astype(jnp.bfloat16)
                weights[:, at] = probs.astype(jnp.bfloat16)
            columns = slice(group * GROUP_W, (group + 1) * GROUP_W)
            score_grad = grads[:, columns]
            dq[:, columns] += mm(k_rows, score_grad, TN)
            k_part = mm(score_grad, head_rows(q, group), NN) * FACTOR
            v_part = mm(weights[:, columns], head_rows(out_low, group), NN)
            put_chunk(d_kv, chunk, group, k_part.astype(jnp.bfloat16))
            put_chunk(d_kv, chunk, KV_HEADS + group, v_part.astype(jnp.bfloat16))
        return carry

    lax.fori_loop(low, high, step, 0)


def back_low_kernel(
    lengths,
    q,
    mine,
    other,
    att,
    lse,
    own_docs,
    upstream,
    bias,
    out_low,
    delta,
    dq_low,
    d_mine,
    d_other,
    grads,
    weights,
):
    row = Row(lengths)
    d_mine[...] = jnp.zeros(d_mine.shape, d_mine.dtype)
    d_other[...] = jnp.zeros(d_other.shape, d_other.dtype)
    w = jnp.concatenate(
        [
            jnp.concatenate([upstream[2 * d + c] for d in range(DOCS)] * 2, axis=0)
            for c in range(2)
        ],
        axis=1,
    )
    docs = own_docs[...]
    doc_inv = lax.rsqrt(jnp.sum(docs * docs, axis=1, keepdims=True) + EPSILON)
    unit = docs * doc_inv
    inner = jnp.sum(unit * w, axis=1, keepdims=True)
    doc_grad = doc_inv * (w - unit * inner) / row.length_column()
    big, small = halves(doc_grad)
    member = row.member.astype(jnp.bfloat16)
    out_low[...] = mm(member, big, TN).astype(jnp.bfloat16)
    both = jnp.concatenate([big, small], axis=0)
    twice = jnp.concatenate([member, member], axis=0)
    for h in range(HEADS):
        at = head(h)
        one = jnp.sum(mm(both[:, at], twice, TN) * att[:, at], axis=0, keepdims=True)
        delta[:, at] = jnp.broadcast_to(one, (8, TOK))
    dq_low[...] = jnp.zeros(dq_low.shape, jnp.float32)
    kv, d_kv = (mine, other), (d_mine, d_other)
    back_part(row.low, q, kv, bias, lse, out_low, delta, dq_low, d_kv, grads, weights)


def back_own_kernel(
    lengths,
    q,
    mine,
    other,
    lse,
    out_low,
    delta,
    dq_low,
    grad_q,
    d_mine,
    d_other,
    bias,
    dq,
    grads,
    weights,
):
    row = Row(lengths)
    d_mine[...] = jnp.zeros(d_mine.shape, d_mine.dtype)
    d_other[...] = jnp.zeros(d_other.shape, d_other.dtype)
    fill_bias(row, row.own, bias)
    dq[...] = dq_low[...]
    kv, d_kv = (mine, other), (d_mine, d_other)
    back_part(row.own, q, kv, bias, lse, out_low, delta, dq, d_kv, grads, weights)
    for h in range(HEADS):
        grad_q[:, head(h)] = (dq[:, head(h)].T * FACTOR).astype(jnp.bfloat16)


def total_kernel(terms, total):
    total[...] = added(terms)


def finish_kernel(near, far, grad_k, grad_v):
    total = (near[...] + far[...].astype(jnp.float32)).astype(jnp.bfloat16)
    grad_k[...] = total[:, :KVW]
    grad_v[...] = total[:, KVW:]


F32, BF16 = jnp.float32, jnp.bfloat16


def shape(dims, dtype):
    return jax.ShapeDtypeStruct(dims, dtype)


def run(kernel, name, outs, scratch, lengths, *arrays, flops=0):
    vmem = pl.BlockSpec(memory_space=pltpu.VMEM)
    smem = pl.BlockSpec(memory_space=pltpu.SMEM)
    first = () if lengths is None else (lengths,)
    return pl.pallas_call(
        kernel,
        out_shape=outs,
        in_specs=[smem] * len(first) + [vmem] * len(arrays),
        out_specs=tuple(vmem for _ in outs),
        scratch_shapes=scratch,
        compiler_params=pltpu.CompilerParams(vmem_limit_bytes=VMEM_BYTES),
        cost_estimate=pl.CostEstimate(flops=flops, bytes_accessed=0, transcendentals=0),
        name=name,
    )(*first, *arrays)


TERMS = shape((CHUNKS, TOK, 2 * KVW), BF16)
WIDE = pltpu.VMEM((HEAD_DIM, EMB), F32)
BIAS = pltpu.VMEM((CHUNKS, CHUNK, TOK), F32)
STATS = pltpu.VMEM((2, HEADS, TOK), F32)
ROUNDED = pltpu.VMEM((CHUNK, EMB), BF16)


def spread(kv):
    return pl.pallas_call(
        spread_kernel,
        out_shape=shape((4, *kv.shape), kv.dtype),
        in_specs=[pl.BlockSpec(memory_space=pltpu.VMEM)],
        out_specs=pl.BlockSpec(memory_space=pl.ANY),
        scratch_shapes=[pltpu.SemaphoreType.DMA((4,))],
        compiler_params=pltpu.CompilerParams(vmem_limit_bytes=VMEM_BYTES),
        cost_estimate=pl.CostEstimate(flops=0, bytes_accessed=0, transcendentals=0),
        name="spread",
    )(kv)


def biases(lengths):
    one = shape((CHUNKS, CHUNK, TOK), F32)
    return run(bias_kernel, "biases", (one, one), [], lengths, flops=FILLS_A_WAIT)


def attend_own(lengths, *arrays):
    outs = (shape((HEAD_DIM, EMB), F32), shape((8, EMB), F32))
    scratch = [STATS, ROUNDED, WIDE]
    return run(
        attend_own_kernel, "attend_own", outs, scratch, lengths, *arrays, flops=FILLS_A_WAIT
    )


def attend_low(lengths, *arrays):
    outs = (shape((HEAD_DIM, EMB), F32), shape((8, EMB), F32), shape((8, 1, PIECE), F32))
    scratch = [STATS, ROUNDED, WIDE, pltpu.VMEM((8, EMB), F32)]
    return run(attend_low_kernel, "attend_low", outs, scratch, lengths, *arrays)


def query_inverses(q):
    outs = (shape((128, 128), F32),)
    return run(inverse_kernel, "query_inverses", outs, [], None, q, flops=FILLS_A_WAIT)[0]


def query_units(*arrays):
    outs = (shape((128, EMB), F32),)
    return run(unit_kernel, "query_units", outs, [], None, *arrays, flops=FILLS_A_WAIT)[0]


def contrast(*arrays):
    outs = (shape((NDOC, 128), F32), shape((32, 1, PIECE), F32), shape((8, EMB), F32))
    return run(contrast_kernel, "contrast", outs, [], None, *arrays)


def query_back(*arrays):
    outs = (shape((128, EMB), F32),)
    return run(query_kernel, "query_back", outs, [], None, *arrays, flops=FILLS_A_WAIT)[0]


def total_of(terms):
    outs = (shape((TOK, 2 * KVW), F32),)
    return run(total_kernel, "total_of", outs, [], None, terms)[0]


def finish(*arrays):
    outs = (shape((TOK, KVW), BF16), shape((TOK, KVW), BF16))
    return run(finish_kernel, "finish", outs, [], None, *arrays)


def back_low(lengths, *arrays):
    outs = (
        shape((TOK, EMB), BF16),
        shape((8, EMB), F32),
        shape((HEAD_DIM, EMB), F32),
        TERMS,
        TERMS,
    )
    return run(back_low_kernel, "back_low", outs, [ROUNDED, ROUNDED], lengths, *arrays)


def back_own(lengths, *arrays):
    outs = (shape((TOK, EMB), BF16), TERMS, TERMS)
    return run(back_own_kernel, "back_own", outs, [BIAS, WIDE, ROUNDED, ROUNDED], lengths, *arrays)


def to_all(block, axes, count):
    return lax.all_to_all(jnp.broadcast_to(block[None], (count,) + block.shape), axes, 0, 0)


def swap_cores(block):
    return lax.ppermute(block, "core", [(0, 1), (1, 0)])


def added(blocks):
    total = blocks[0].astype(F32)
    for i in range(1, blocks.shape[0]):
        total = total + blocks[i].astype(F32)
    return total


def pair_terms(d_mine, d_other):
    got = swap_cores(d_other)
    return (d_mine.astype(F32) + got.astype(F32)).astype(BF16)


def per_device(queries_q, keys, values, lengths, query_emb, positive):
    q = queries_q[0]
    kv = jnp.concatenate([keys[0], values[0]], axis=1)
    kv_low = lax.ppermute(kv, "zhi", [(0, 1)])
    own_mine = lax.all_to_all(spread(kv), "x", 0, 0)
    inverse = query_inverses(query_emb)
    own_mine, inverse, after = lax.optimization_barrier((own_mine, inverse, lengths))
    own_other = swap_cores(own_mine)
    own_bias, low_bias = biases(after)
    own_other, inverse, own_bias = lax.optimization_barrier((own_other, inverse, own_bias))
    unit = query_units(query_emb, inverse)
    kv_low, own_other, unit = lax.optimization_barrier((kv_low, own_other, unit))
    own_att, own_lse = attend_own(lengths, q, own_mine, own_other, own_bias)
    low_mine = lax.all_to_all(spread(kv_low), "x", 0, 0)
    low_mine, own_att = lax.optimization_barrier((low_mine, own_att))
    low_other = swap_cores(low_mine)
    att, lse, pieces = attend_low(
        lengths, q, low_mine, low_other, own_att, own_lse, low_bias
    )

    part = added(lax.all_to_all(pieces, NEAR, 0, 0))
    column = to_all(part, ("zlo", "zhi"), 16)
    column = (column[0::2] + column[1::2]).reshape(8, PIECE)
    docs_mine = to_all(column, ("y", "x"), 16).reshape(NDOC, PIECE)
    docs_other = swap_cores(docs_mine)

    coefficient, terms, own_docs = contrast(
        unit, positive.reshape(1, 128), docs_mine, docs_other
    )
    terms = added(lax.all_to_all(terms, ("y", "zlo"), 0, 0))
    upstream = to_all(terms, NEAR, 8)

    out_low, delta, dq_low, d_mine, d_other = back_low(
        lengths, q, low_mine, low_other, att, lse, own_docs, upstream, low_bias
    )
    paired = pair_terms(d_mine, d_other)
    paired, dq_low = lax.optimization_barrier((paired, dq_low))
    grad_q, own_d_mine, own_d_other = back_own(
        lengths, q, own_mine, own_other, lse, out_low, delta, dq_low
    )
    low_terms = lax.all_to_all(paired, "x", 0, 0)
    low_sum = added(low_terms).astype(BF16)
    own_paired = pair_terms(own_d_mine, own_d_other)
    from_high = lax.ppermute(low_sum, "zhi", [(1, 0)])
    low_sum, own_paired = lax.optimization_barrier((low_sum, own_paired))
    own_terms = lax.all_to_all(own_paired, "x", 0, 0)
    coefficient, low_sum = lax.optimization_barrier((coefficient, low_sum))
    query_grad = query_back(unit, inverse, docs_mine, docs_other, coefficient)
    query_grad, own_terms = lax.optimization_barrier((query_grad, own_terms))
    grad_k, grad_v = finish(total_of(own_terms), from_high)
    return (query_grad, grad_q[None], grad_k[None], grad_v[None])


def solution(mesh):
    fine = Mesh(mesh.devices.reshape(8, 4, 2, 4, 2), ("zlo", "y", "zhi", "x", "core"))
    dp, ctx = ("zlo", "y"), ("zhi", "x", "core")
    tokens = P(dp, ctx, None)
    return jax.shard_map(
        per_device,
        mesh=fine,
        in_specs=(tokens, tokens, tokens, P(dp, None), P(dp, None), P(dp)),
        out_specs=(P(dp, None), tokens, tokens, tokens),
        check_vma=False,
    )
```

```python
import jax
import jax.numpy as jnp
from jax import lax
from jax.experimental import pallas as pl
from jax.experimental.pallas import tpu as pltpu
from jax.sharding import Mesh
from jax.sharding import PartitionSpec as P

HEAD_DIM = 128
HEADS = 14
KV_HEADS = 2
PER_GROUP = HEADS // KV_HEADS
DOCS = 4
TOK = 128
SEQ = 2048
EMB = HEADS * HEAD_DIM
KVW = KV_HEADS * HEAD_DIM
GROUP_W = PER_GROUP * TOK
CHUNK = 2 * TOK
HALF = SEQ // 2
CHUNKS = HALF // CHUNK
PIECE = EMB // 2
NDOC = 128

FACTOR = HEAD_DIM ** (-0.5)
INVERSE_TEMPER = 0.05
EPSILON = 1e-06
LOG2_E = 1.4426950408889634
FULL_ACCURACY = lax.Precision.HIGHEST
MASKED = -1e30
TINY = 1e-30
FILLS_A_WAIT = 10**12
NT = (((1,), (1,)), ((), ()))
TN = (((0,), (0,)), ((), ()))
NN = (((1,), (0,)), ((), ()))
NEAR = ("x", "core")
VMEM_BYTES = 24 * 1024 * 1024


def mm(a, b, dims, precision=None):
    return lax.dot_general(a, b, dims, precision=precision, preferred_element_type=jnp.float32)


def place():
    return tuple(lax.axis_index(axis) for axis in ("zlo", "y", "zhi", "x", "core"))


class Row:
    def __init__(self, lengths):
        _, _, self.high, x, self.core = place()
        self.first = ((self.high * 4 + x) * 2 + self.core) * TOK
        self.lengths = [lengths[0, d] for d in range(DOCS)]
        qpos = self.first + lax.broadcasted_iota(jnp.int32, (1, TOK), 1)
        start = jnp.zeros((1, TOK), jnp.int32)
        doc = jnp.zeros((1, TOK), jnp.int32)
        first_start = jnp.int32(0)
        end = jnp.int32(0)
        for d in range(DOCS - 1):
            end = end + self.lengths[d]
            start = jnp.where(qpos >= end, end, start)
            doc = doc + (qpos >= end).astype(jnp.int32)
            first_start = jnp.where(self.first >= end, end, first_start)
        self.qpos, self.start = qpos, start
        self.member = (lax.broadcasted_iota(jnp.int32, (8, TOK), 0) == doc).astype(jnp.float32)
        own_base = self.high * HALF
        self.own = (
            own_base,
            lax.div(jnp.maximum(first_start - own_base, 0), CHUNK),
            lax.div(self.first + (TOK - 1) - own_base, CHUNK) + 1,
        )
        self.low = (jnp.int32(0), lax.div(first_start, CHUNK), CHUNKS * self.high)

    def length_column(self):
        rows = lax.broadcasted_iota(jnp.int32, (8, 1), 0)
        column = jnp.ones((8, 1), jnp.float32)
        for d in range(DOCS):
            column = jnp.where(rows == d, self.lengths[d].astype(jnp.float32), column)
        return column

    def bias(self, base, chunk):
        at = lax.broadcasted_iota(jnp.int32, (CHUNK, TOK), 0)
        half = lax.div(at, TOK)
        turned = jnp.where(self.core == 1, 1 - half, half)
        pos = base + chunk * CHUNK + turned * TOK + (at - half * TOK)
        allowed = (pos >= self.start) & (pos <= self.qpos)
        return jnp.where(allowed, 0.0, MASKED).astype(jnp.float32)


def chunk_of(kv, chunk, column):
    at = slice(column * HEAD_DIM, (column + 1) * HEAD_DIM)
    return jnp.concatenate([half[chunk, :, at] for half in kv], axis=0)


def put_chunk(refs, chunk, column, rows):
    at = slice(column * HEAD_DIM, (column + 1) * HEAD_DIM)
    refs[0][chunk, :, at] = rows[:TOK]
    refs[1][chunk, :, at] = rows[TOK:]


def fill_bias(row, part, bias):
    base, low, high = part

    def step(chunk, carry):
        bias[chunk] = row.bias(base, chunk)
        return carry

    lax.fori_loop(low, high, step, 0)


def halves(values):
    top = values.astype(jnp.bfloat16)
    return top, (values - top.astype(jnp.float32)).astype(jnp.bfloat16)


def head_rows(ref, group):
    return jnp.concatenate(
        [
            ref[:, (group * PER_GROUP + h) * HEAD_DIM : (group * PER_GROUP + h + 1) * HEAD_DIM]
            for h in range(PER_GROUP)
        ],
        axis=0,
    )


def head(h):
    return slice(h * HEAD_DIM, (h + 1) * HEAD_DIM)


def spread_kernel(kv, out, done):
    copies = [pltpu.make_async_copy(kv, out.at[i], done.at[i]) for i in range(4)]
    for copy in copies:
        copy.start()
    for copy in copies:
        copy.wait()


def part_attention(part, q, kv, bias, stats, weights, out):
    _, low, high = part
    stats[0] = jnp.full((HEADS, TOK), MASKED, jnp.float32)
    stats[1] = jnp.zeros((HEADS, TOK), jnp.float32)
    out[...] = jnp.zeros(out.shape, jnp.float32)

    def step(chunk, carry):
        blocked = bias[chunk]
        for group in range(KV_HEADS):
            k_rows = chunk_of(kv, chunk, group)
            scales = []
            for h in range(group * PER_GROUP, (group + 1) * PER_GROUP):
                i = h - group * PER_GROUP
                if i % 2 == 0:
                    many = 2 if i + 1 < PER_GROUP else 1
                    pair = jnp.concatenate([q[:, head(h + j)] for j in range(many)], axis=0)
                    every = mm(k_rows, pair, NT)
                scores = every[:, head(i % 2)] + blocked
                old = stats[0, h : h + 1]
                top = jnp.maximum(old, jnp.max(scores, axis=0, keepdims=True))
                exps = jnp.exp2((scores - top) * (FACTOR * LOG2_E))
                weights[:, head(h)] = exps.astype(jnp.bfloat16)
                scale = jnp.exp((old - top) * FACTOR)
                stats[0, h : h + 1] = top
                stats[1, h : h + 1] = stats[1, h : h + 1] * scale + jnp.sum(
                    exps, axis=0, keepdims=True
                )
                scales.append(scale)
            columns = slice(group * GROUP_W, (group + 1) * GROUP_W)
            sums = mm(chunk_of(kv, chunk, KV_HEADS + group), weights[:, columns], TN)
            for i in range(PER_GROUP):
                at = head(group * PER_GROUP + i)
                out[:, at] = out[:, at] * scales[i] + sums[:, head(i)]
        return carry

    lax.fori_loop(low, high, step, 0)


def part_result(h, stats):
    total = jnp.maximum(stats[1, h : h + 1], TINY)
    return stats[0, h : h + 1] * FACTOR + jnp.log(total), 1.0 / total


def bias_kernel(lengths, own_bias, low_bias):
    row = Row(lengths)
    fill_bias(row, row.own, own_bias)
    fill_bias(row, row.low, low_bias)


def attend_own_kernel(lengths, q, mine, other, bias, att, lse, stats, weights, out):
    row = Row(lengths)
    part_attention(row.own, q, (mine, other), bias, stats, weights, out)
    for h in range(HEADS):
        log_total, inverse = part_result(h, stats)
        att[:, head(h)] = out[:, head(h)] * inverse
        lse[:, head(h)] = jnp.broadcast_to(log_total, (8, TOK))


def attend_low_kernel(
    lengths, q, mine, other, own_att, own_lse, bias, att, lse, pieces, stats, weights, out, doc_sum
):
    row = Row(lengths)
    member = jnp.concatenate([row.member, jnp.zeros((TOK - 8, TOK), jnp.float32)], axis=0)
    member = member.astype(jnp.bfloat16)
    part_attention(row.low, q, (mine, other), bias, stats, weights, out)
    for h in range(HEADS):
        at = head(h)
        low_total, inverse = part_result(h, stats)
        own_total = own_lse[0:1, at]
        top = jnp.maximum(low_total, own_total)
        log_total = top + jnp.log(jnp.exp(low_total - top) + jnp.exp(own_total - top))
        own_scale = jnp.exp(own_total - log_total)
        low_scale = jnp.exp(low_total - log_total) * inverse
        lse[:, at] = jnp.broadcast_to(log_total, (8, TOK))
        merged = own_att[:, at] * own_scale + out[:, at] * low_scale
        att[:, at] = merged
        big, small = halves(merged)
        doc_sum[:, at] = (mm(big, member, NT) + mm(small, member, NT)).T[:8]
    mean = doc_sum[...] / row.length_column()
    for d in range(DOCS):
        for c in range(2):
            pieces[2 * d + c] = mean[d : d + 1, c * PIECE : (c + 1) * PIECE]


def inverse_kernel(q, inverse):
    values = q[...].astype(jnp.float32)
    query_inv = lax.rsqrt(jnp.sum(values * values, axis=1, keepdims=True) + EPSILON)
    inverse[...] = jnp.broadcast_to(query_inv, (128, 128))


def unit_kernel(q, inverse, unit):
    unit[...] = q[...].astype(jnp.float32) * inverse[:, :1]


def mm_parts(a, b, dims):
    a_big, a_small = halves(a)
    b_big, b_small = halves(b)
    return mm(a_big, b_big, dims) + (mm(a_big, b_small, dims) + mm(a_small, b_big, dims))


def contrast_kernel(unit, positive, docs_mine, docs_other, coefficient, terms, own_docs):
    z_lo, y, _, x, core = place()
    d_mine, d_other = docs_mine[...], docs_other[...]
    doc_inv = lax.rsqrt(
        jnp.sum(d_mine * d_mine, axis=1, keepdims=True)
        + jnp.sum(d_other * d_other, axis=1, keepdims=True)
        + EPSILON
    )
    q_left, q_right = unit[:, :PIECE], unit[:, PIECE:]
    q_mine = jnp.where(core == 1, q_right, q_left)
    q_other = jnp.where(core == 1, q_left, q_right)
    logits = mm_parts(d_mine * doc_inv, q_mine, NT)
    logits = (logits + mm_parts(d_other * doc_inv, q_other, NT)) / INVERSE_TEMPER
    exps = jnp.exp(logits)
    at = lax.broadcasted_iota(jnp.int32, (NDOC, 128), 0)
    doc = ((at % 8) * 4 + at // 32) * DOCS + (at // 8) % 4
    target = (doc == positive[...]).astype(jnp.float32)
    coefficient[...] = exps / jnp.sum(exps, axis=0, keepdims=True) - target
    near = jnp.concatenate(
        [coefficient[pl.ds(pl.multiple_of(b * 32 + x * 8, 8), 8), :] for b in range(4)], axis=0
    )
    near_terms = mm_parts(near, q_mine, NN) / INVERSE_TEMPER
    for r in range(32):
        terms[r] = near_terms[r : r + 1]
    own_docs[...] = jnp.zeros((8, EMB), jnp.float32)
    for d in range(DOCS):
        r = y * 32 + d * 8 + z_lo
        a, b = docs_mine[pl.ds(r, 1), :], docs_other[pl.ds(r, 1), :]
        own_docs[d : d + 1, :PIECE] = jnp.where(core == 1, b, a)
        own_docs[d : d + 1, PIECE:] = jnp.where(core == 1, a, b)


def query_kernel(unit, inverse, docs_mine, docs_other, coefficient, query_grad):
    _, _, _, _, core = place()
    d_mine, d_other = docs_mine[...], docs_other[...]
    doc_inv = lax.rsqrt(
        jnp.sum(d_mine * d_mine, axis=1, keepdims=True)
        + jnp.sum(d_other * d_other, axis=1, keepdims=True)
        + EPSILON
    )
    scaled = coefficient[...] * doc_inv
    u_mine = mm(scaled, d_mine, TN, FULL_ACCURACY) / INVERSE_TEMPER
    u_other = mm(scaled, d_other, TN, FULL_ACCURACY) / INVERSE_TEMPER
    u_left = jnp.where(core == 1, u_other, u_mine)
    u_right = jnp.where(core == 1, u_mine, u_other)
    query_inv = inverse[:, :1]
    q_left, q_right = unit[:, :PIECE], unit[:, PIECE:]
    inner = jnp.sum(q_left * u_left, axis=1, keepdims=True) + jnp.sum(
        q_right * u_right, axis=1, keepdims=True
    )
    query_grad[:, :PIECE] = query_inv * (u_left - q_left * inner)
    query_grad[:, PIECE:] = query_inv * (u_right - q_right * inner)


def back_part(part, q, kv, bias, lse, out_low, delta, dq, d_kv, grads, weights):
    _, low, high = part

    def step(chunk, carry):
        blocked = bias[chunk]
        for group in range(KV_HEADS):
            k_rows = chunk_of(kv, chunk, group)
            v_rows = chunk_of(kv, chunk, KV_HEADS + group)
            for h in range(group * PER_GROUP, (group + 1) * PER_GROUP):
                at = head(h)
                i = h - group * PER_GROUP
                if i % 2 == 0:
                    many = 2 if i + 1 < PER_GROUP else 1
                    pair = jnp.concatenate([q[:, head(h + j)] for j in range(many)], axis=0)
                    every = mm(k_rows, pair, NT)
                    pair = jnp.concatenate([out_low[:, head(h + j)] for j in range(many)], axis=0)
                    flows = mm(v_rows, pair, NT)
                scores = every[:, head(i % 2)] * (FACTOR * LOG2_E) + blocked
                probs = jnp.exp2(scores - lse[0:1, at] * LOG2_E)
                flow = flows[:, head(i % 2)]
                grads[:, at] = (probs * (flow - delta[0:1, at])).astype(jnp.bfloat16)
                weights[:, at] = probs.astype(jnp.bfloat16)
            columns = slice(group * GROUP_W, (group + 1) * GROUP_W)
            score_grad = grads[:, columns]
            dq[:, columns] += mm(k_rows, score_grad, TN)
            k_part = mm(score_grad, head_rows(q, group), NN) * FACTOR
            v_part = mm(weights[:, columns], head_rows(out_low, group), NN)
            put_chunk(d_kv, chunk, group, k_part.astype(jnp.bfloat16))
            put_chunk(d_kv, chunk, KV_HEADS + group, v_part.astype(jnp.bfloat16))
        return carry

    lax.fori_loop(low, high, step, 0)


def back_low_kernel(
    lengths,
    q,
    mine,
    other,
    att,
    lse,
    own_docs,
    upstream,
    bias,
    out_low,
    delta,
    dq_low,
    d_mine,
    d_other,
    grads,
    weights,
):
    row = Row(lengths)
    d_mine[...] = jnp.zeros(d_mine.shape, d_mine.dtype)
    d_other[...] = jnp.zeros(d_other.shape, d_other.dtype)
    w = jnp.concatenate(
        [
            jnp.concatenate([upstream[2 * d + c] for d in range(DOCS)] * 2, axis=0)
            for c in range(2)
        ],
        axis=1,
    )
    docs = own_docs[...]
    doc_inv = lax.rsqrt(jnp.sum(docs * docs, axis=1, keepdims=True) + EPSILON)
    unit = docs * doc_inv
    inner = jnp.sum(unit * w, axis=1, keepdims=True)
    doc_grad = doc_inv * (w - unit * inner) / row.length_column()
    big, small = halves(doc_grad)
    member = row.member.astype(jnp.bfloat16)
    out_low[...] = mm(member, big, TN).astype(jnp.bfloat16)
    both = jnp.concatenate([big, small], axis=0)
    twice = jnp.concatenate([member, member], axis=0)
    for h in range(HEADS):
        at = head(h)
        one = jnp.sum(mm(both[:, at], twice, TN) * att[:, at], axis=0, keepdims=True)
        delta[:, at] = jnp.broadcast_to(one, (8, TOK))
    dq_low[...] = jnp.zeros(dq_low.shape, jnp.float32)
    kv, d_kv = (mine, other), (d_mine, d_other)
    back_part(row.low, q, kv, bias, lse, out_low, delta, dq_low, d_kv, grads, weights)


def back_own_kernel(
    lengths,
    q,
    mine,
    other,
    lse,
    out_low,
    delta,
    dq_low,
    grad_q,
    d_mine,
    d_other,
    bias,
    dq,
    grads,
    weights,
):
    row = Row(lengths)
    d_mine[...] = jnp.zeros(d_mine.shape, d_mine.dtype)
    d_other[...] = jnp.zeros(d_other.shape, d_other.dtype)
    fill_bias(row, row.own, bias)
    dq[...] = dq_low[...]
    kv, d_kv = (mine, other), (d_mine, d_other)
    back_part(row.own, q, kv, bias, lse, out_low, delta, dq, d_kv, grads, weights)
    for h in range(HEADS):
        grad_q[:, head(h)] = (dq[:, head(h)].T * FACTOR).astype(jnp.bfloat16)


def total_kernel(terms, total):
    total[...] = added(terms)


def finish_kernel(near, far, grad_k, grad_v):
    total = (near[...] + far[...].astype(jnp.float32)).astype(jnp.bfloat16)
    grad_k[...] = total[:, :KVW]
    grad_v[...] = total[:, KVW:]


F32, BF16 = jnp.float32, jnp.bfloat16


def shape(dims, dtype):
    return jax.ShapeDtypeStruct(dims, dtype)


def run(kernel, name, outs, scratch, lengths, *arrays, flops=0):
    vmem = pl.BlockSpec(memory_space=pltpu.VMEM)
    smem = pl.BlockSpec(memory_space=pltpu.SMEM)
    first = () if lengths is None else (lengths,)
    return pl.pallas_call(
        kernel,
        out_shape=outs,
        in_specs=[smem] * len(first) + [vmem] * len(arrays),
        out_specs=tuple(vmem for _ in outs),
        scratch_shapes=scratch,
        compiler_params=pltpu.CompilerParams(vmem_limit_bytes=VMEM_BYTES),
        cost_estimate=pl.CostEstimate(flops=flops, bytes_accessed=0, transcendentals=0),
        name=name,
    )(*first, *arrays)


TERMS = shape((CHUNKS, TOK, 2 * KVW), BF16)
WIDE = pltpu.VMEM((HEAD_DIM, EMB), F32)
BIAS = pltpu.VMEM((CHUNKS, CHUNK, TOK), F32)
STATS = pltpu.VMEM((2, HEADS, TOK), F32)
ROUNDED = pltpu.VMEM((CHUNK, EMB), BF16)


def spread(kv):
    return pl.pallas_call(
        spread_kernel,
        out_shape=shape((4, *kv.shape), kv.dtype),
        in_specs=[pl.BlockSpec(memory_space=pltpu.VMEM)],
        out_specs=pl.BlockSpec(memory_space=pl.ANY),
        scratch_shapes=[pltpu.SemaphoreType.DMA((4,))],
        compiler_params=pltpu.CompilerParams(vmem_limit_bytes=VMEM_BYTES),
        cost_estimate=pl.CostEstimate(flops=0, bytes_accessed=0, transcendentals=0),
        name="spread",
    )(kv)


def biases(lengths):
    one = shape((CHUNKS, CHUNK, TOK), F32)
    return run(bias_kernel, "biases", (one, one), [], lengths, flops=FILLS_A_WAIT)


def attend_own(lengths, *arrays):
    outs = (shape((HEAD_DIM, EMB), F32), shape((8, EMB), F32))
    scratch = [STATS, ROUNDED, WIDE]
    return run(
        attend_own_kernel, "attend_own", outs, scratch, lengths, *arrays, flops=FILLS_A_WAIT
    )


def attend_low(lengths, *arrays):
    outs = (shape((HEAD_DIM, EMB), F32), shape((8, EMB), F32), shape((8, 1, PIECE), F32))
    scratch = [STATS, ROUNDED, WIDE, pltpu.VMEM((8, EMB), F32)]
    return run(attend_low_kernel, "attend_low", outs, scratch, lengths, *arrays)


def query_inverses(q):
    outs = (shape((128, 128), F32),)
    return run(inverse_kernel, "query_inverses", outs, [], None, q, flops=FILLS_A_WAIT)[0]


def query_units(*arrays):
    outs = (shape((128, EMB), F32),)
    return run(unit_kernel, "query_units", outs, [], None, *arrays, flops=FILLS_A_WAIT)[0]


def contrast(*arrays):
    outs = (shape((NDOC, 128), F32), shape((32, 1, PIECE), F32), shape((8, EMB), F32))
    return run(contrast_kernel, "contrast", outs, [], None, *arrays)


def query_back(*arrays):
    outs = (shape((128, EMB), F32),)
    return run(query_kernel, "query_back", outs, [], None, *arrays, flops=FILLS_A_WAIT)[0]


def total_of(terms):
    outs = (shape((TOK, 2 * KVW), F32),)
    return run(total_kernel, "total_of", outs, [], None, terms)[0]


def finish(*arrays):
    outs = (shape((TOK, KVW), BF16), shape((TOK, KVW), BF16))
    return run(finish_kernel, "finish", outs, [], None, *arrays)


def back_low(lengths, *arrays):
    outs = (
        shape((TOK, EMB), BF16),
        shape((8, EMB), F32),
        shape((HEAD_DIM, EMB), F32),
        TERMS,
        TERMS,
    )
    return run(back_low_kernel, "back_low", outs, [ROUNDED, ROUNDED], lengths, *arrays)


def back_own(lengths, *arrays):
    outs = (shape((TOK, EMB), BF16), TERMS, TERMS)
    return run(back_own_kernel, "back_own", outs, [BIAS, WIDE, ROUNDED, ROUNDED], lengths, *arrays)


def to_all(block, axes, count):
    return lax.all_to_all(jnp.broadcast_to(block[None], (count,) + block.shape), axes, 0, 0)


def swap_cores(block):
    return lax.ppermute(block, "core", [(0, 1), (1, 0)])


def added(blocks):
    total = blocks[0].astype(F32)
    for i in range(1, blocks.shape[0]):
        total = total + blocks[i].astype(F32)
    return total


def pair_terms(d_mine, d_other):
    got = swap_cores(d_other)
    return (d_mine.astype(F32) + got.astype(F32)).astype(BF16)


def per_device(queries_q, keys, values, lengths, query_emb, positive):
    q = queries_q[0]
    kv = jnp.concatenate([keys[0], values[0]], axis=1)
    kv_low = lax.ppermute(kv, "zhi", [(0, 1)])
    own_mine = lax.all_to_all(spread(kv), "x", 0, 0)
    inverse = query_inverses(query_emb)
    own_mine, inverse, after = lax.optimization_barrier((own_mine, inverse, lengths))
    own_other = swap_cores(own_mine)
    own_bias, low_bias = biases(after)
    own_other, inverse, own_bias = lax.optimization_barrier((own_other, inverse, own_bias))
    unit = query_units(query_emb, inverse)
    kv_low, own_other, unit = lax.optimization_barrier((kv_low, own_other, unit))
    own_att, own_lse = attend_own(lengths, q, own_mine, own_other, own_bias)
    low_mine = lax.all_to_all(spread(kv_low), "x", 0, 0)
    low_mine, own_att = lax.optimization_barrier((low_mine, own_att))
    low_other = swap_cores(low_mine)
    att, lse, pieces = attend_low(
        lengths, q, low_mine, low_other, own_att, own_lse, low_bias
    )

    part = added(lax.all_to_all(pieces, NEAR, 0, 0))
    column = to_all(part, ("zlo", "zhi"), 16)
    column = (column[0::2] + column[1::2]).reshape(8, PIECE)
    docs_mine = to_all(column, ("y", "x"), 16).reshape(NDOC, PIECE)
    docs_other = swap_cores(docs_mine)

    coefficient, terms, own_docs = contrast(
        unit, positive.reshape(1, 128), docs_mine, docs_other
    )
    terms = added(lax.all_to_all(terms, ("y", "zlo"), 0, 0))
    upstream = to_all(terms, NEAR, 8)

    out_low, delta, dq_low, d_mine, d_other = back_low(
        lengths, q, low_mine, low_other, att, lse, own_docs, upstream, low_bias
    )
    paired = pair_terms(d_mine, d_other)
    paired, dq_low = lax.optimization_barrier((paired, dq_low))
    grad_q, own_d_mine, own_d_other = back_own(
        lengths, q, own_mine, own_other, lse, out_low, delta, dq_low
    )
    low_terms = lax.all_to_all(paired, "x", 0, 0)
    low_sum = added(low_terms).astype(BF16)
    own_paired = pair_terms(own_d_mine, own_d_other)
    from_high = lax.ppermute(low_sum, "zhi", [(1, 0)])
    low_sum, own_paired = lax.optimization_barrier((low_sum, own_paired))
    own_terms = lax.all_to_all(own_paired, "x", 0, 0)
    coefficient, low_sum = lax.optimization_barrier((coefficient, low_sum))
    query_grad = query_back(unit, inverse, docs_mine, docs_other, coefficient)
    query_grad, own_terms = lax.optimization_barrier((query_grad, own_terms))
    grad_k, grad_v = finish(total_of(own_terms), from_high)
    return (query_grad, grad_q[None], grad_k[None], grad_v[None])


def solution(mesh):
    fine = Mesh(mesh.devices.reshape(8, 4, 2, 4, 2), ("zlo", "y", "zhi", "x", "core"))
    dp, ctx = ("zlo", "y"), ("zhi", "x", "core")
    tokens = P(dp, ctx, None)
    return jax.shard_map(
        per_device,
        mesh=fine,
        in_specs=(tokens, tokens, tokens, P(dp, None), P(dp, None), P(dp)),
        out_specs=(P(dp, None), tokens, tokens, tokens),
        check_vma=False,
    )
```
